32 devices in a mesh: lb: 4 (over x, core), rb: 4 (over z), rep: 2 (over y).
Axes of the slice: x: 2, y: 2, z: 4, core: 2. Of those that a mesh axis runs over, the one named last changes fastest.
Arguments:
- left_factor: bfloat16 [1024, 1024], P('lb', 'rep'), may hold values from -5 to 5
- boundary_site: bfloat16 [1024, 16, 1024], P('rep', None, 'rb'), may hold values from -6 to 6
- double_layer: float32 [16, 16], replicated, may hold values from -1.5 to 1.5
Outputs:
- site_q: float32 [16, 1024, 1024], P('rep', 'lb', 'rb')
- factor: float32 [1024, 1024], P('lb')
The draws below stay inside these ranges and needn't reach their ends.
All inputs are finite; a program needn't handle non-finite values.
Results may differ from the reference program's by a relative error of at most 0.0032.
Values sent between devices are 32-bit elements; how exact they have to be, the bound alone decides.
No kernel may reach another device: no remote copies, remote signals or barrier semaphores. Data moves between devices by JAX's collectives and lax.ppermute only.
A program may use at most 128 MiB of HBM per device.

```python
import math
import jax
import jax.numpy as jnp
from jax import lax

CHI = 1024
PHYS = 16


def draw_left_factor(key, part):
    first = jax.random.fold_in(key, 11)
    noise = jax.random.normal(first, (CHI, CHI), jnp.float32) * (0.6 / math.sqrt(CHI))
    matrix = jnp.eye(CHI, dtype=jnp.float32) + noise
    return matrix.astype(jnp.bfloat16)


def shard_levels(own_key, dims, cuts, least, largest):
    def one(axis_at, shards_of):
        draws = jax.random.uniform(jax.random.fold_in(jax.random.fold_in(own_key, 6), axis_at), (shards_of,), jnp.float32, least / len(cuts), largest / len(cuts))
        return jnp.repeat(jnp.exp(draws), dims[axis_at] // shards_of).reshape((-1,) + (1,) * (len(dims) - axis_at - 1))

    loudness = one(*cuts[0])
    for cut in cuts[1:]:
        loudness = loudness * one(*cut)
    return loudness


def bell_draw(own_key, extent, deviation, most, pieces=(), kind=jnp.bfloat16):
    level = shard_levels(own_key, extent, pieces, -0.22, 0.18) if pieces else 1.0
    values = jax.random.normal(own_key, extent, jnp.float32) * deviation * level
    return jnp.minimum(jnp.maximum(values, -most), most).astype(kind)


def setup_inputs(seed: int = 0) -> dict:
    keys = jax.random.split(jax.random.key(seed), 4)
    left_factor = draw_left_factor(jax.random.fold_in(keys[3], 71), 0)
    boundary_site = bell_draw(keys[1], (CHI, PHYS, CHI), 1.0, 6.0, ((0, 2), (2, 4)))
    double_layer = bell_draw(keys[2], (PHYS, PHYS), PHYS ** -0.5, 1.5, (), jnp.float32)
    return {"left_factor": left_factor, "boundary_site": boundary_site, "double_layer": double_layer}


def reference(left_factor, boundary_site, double_layer):
    hp = lax.Precision.HIGHEST
    absorbed = jnp.einsum('kur,ue->ker', boundary_site.astype(jnp.float32), double_layer, precision=hp).astype(jnp.bfloat16)
    grown = jnp.einsum('ik,ker->eir', left_factor.astype(jnp.float32), absorbed.astype(jnp.float32), precision=hp)
    gram = jnp.einsum('eir,ejr->ij', grown, grown, precision=hp)
    lower = jnp.linalg.cholesky(gram)
    matrix = jnp.transpose(grown, (1, 0, 2)).reshape(CHI, PHYS * CHI)
    solved = jax.scipy.linalg.solve_triangular(lower, matrix, lower=True)
    scale = math.sqrt(PHYS * CHI)
    site_q = jnp.transpose(solved.reshape(CHI, PHYS, CHI), (1, 0, 2)) * scale
    return (site_q, lower / scale)
```

```python
import functools
import math

import jax
import jax.numpy as jnp
from jax import lax
from jax.sharding import PartitionSpec as P

BLOCK = 128


def swap(array, axis, size, distance):
    return lax.ppermute(array, axis, [(i, i ^ distance) for i in range(size)])


def upper_bit(axis, distance):
    return lax.rem(lax.div(lax.axis_index(axis), distance), 2)


def distances(size):
    out = []
    while 1 << len(out) < size:
        out.append(1 << len(out))
    return out


def join(array, axis, size, distance, dim):
    other = swap(array, axis, size, distance)
    mine_second = upper_bit(axis, distance) == 1
    first = jnp.where(mine_second, other, array)
    second = jnp.where(mine_second, array, other)
    return jnp.concatenate([first, second], dim)


def halves(array, bit):
    half = array.shape[0] // 2
    mine = lax.dynamic_slice_in_dim(array, bit * half, half, 0)
    other = lax.dynamic_slice_in_dim(array, (1 - bit) * half, half, 0)
    return mine, other


def reduce_scatter(parts, orders):
    halved = []
    for stage in zip(*orders):
        sent, kept, cut = [], [], []
        for part, (axis, size, distance) in zip(parts, stage):
            cut.append(part.shape[0] % 16 == 0)
            if cut[-1]:
                mine, other = halves(part, upper_bit(axis, distance))
            else:
                mine, other = part, part
            kept.append(mine)
            sent.append(swap(other, axis, size, distance))
        parts = [k + s for k, s in zip(kept, sent)]
        halved.append(cut)
    return parts, halved


def all_gather(parts, orders, halved):
    stages = list(zip(*orders))
    for stage, cut in zip(stages[::-1], halved[::-1]):
        parts = [
            join(part, axis, size, distance, 0) if was_cut else part
            for part, (axis, size, distance), was_cut in zip(parts, stage, cut)
        ]
    return parts


def gather_slots(array, axis, size):
    held = [(0, array)]
    for d in distances(size)[::-1]:
        held += [(slot ^ d, swap(piece, axis, size, d)) for slot, piece in held]
    return held


def split3(array):
    high = lax.reduce_precision(array, 8, 7)
    rest = array - high
    middle = lax.reduce_precision(rest, 8, 7)
    low = rest - middle
    return [piece.astype(jnp.bfloat16) for piece in (high, middle, low)]


def pack(matrix):
    n = matrix.shape[0] // BLOCK
    rows = []
    for i in range(n // 2):
        j = n - 1 - i
        rows.append(
            jnp.concatenate(
                [
                    matrix[i * BLOCK : (i + 1) * BLOCK, : (i + 1) * BLOCK],
                    matrix[j * BLOCK : (j + 1) * BLOCK, : (j + 1) * BLOCK],
                ],
                1,
            )
        )
    return jnp.concatenate(rows, 0)


def unpack(packed, size):
    n = size // BLOCK
    rows = [None] * n
    for i in range(n // 2):
        j = n - 1 - i
        row = packed[i * BLOCK : (i + 1) * BLOCK]
        for at, lo in ((i, 0), (j, (i + 1) * BLOCK)):
            blocks = [row[:, lo : lo + at * BLOCK], row[:, lo + at * BLOCK : lo + (at + 1) * BLOCK] * 0.5]
            blocks.append(jnp.zeros((BLOCK, size - (at + 1) * BLOCK), packed.dtype))
            rows[at] = jnp.concatenate(blocks, 1)
    return jnp.concatenate(rows, 0)


def shards(sizes, left_factor, boundary_site, double_layer):
    lb, rb, rep = sizes["lb"], sizes["rb"], sizes["rep"]
    highest = lax.Precision.HIGHEST
    l, p = lax.axis_index("lb"), lax.axis_index("rep")
    depth, phys, right = boundary_site.shape
    east = phys // rep
    chi = depth * rep
    row_count = left_factor.shape[0]

    nothing = double_layer[0, 0] * 0.0

    rows = left_factor.astype(jnp.float32)
    for d in distances(rep):
        rows = join(rows, "rep", rep, d, 1)
    left = jnp.zeros((chi, chi), jnp.bfloat16)
    for slot, piece in gather_slots(rows, "lb", lb):
        piece = (piece + nothing).astype(jnp.bfloat16)
        left = lax.dynamic_update_slice(left, piece, ((l ^ slot) * row_count, 0))

    absorbed = jnp.einsum(
        "kur,ue->ekr", boundary_site.astype(jnp.float32), double_layer, precision=highest
    ).astype(jnp.bfloat16)
    own = lax.dynamic_slice_in_dim(absorbed, p * east, east, 0)

    east_part, right_parts = max(1, east // lb), max(1, lb // east)
    right_part = right // right_parts
    east_at, right_at = (l // right_parts) * east_part, (l % right_parts) * right_part

    def chunk(q):
        return lax.dynamic_slice(
            absorbed, (q * east + east_at, 0, right_at), (east_part, depth, right_part)
        )

    columns = jnp.zeros((east_part, chi, right_part), jnp.bfloat16)
    columns = lax.dynamic_update_slice(columns, chunk(p), (0, p * depth, 0))
    others = []
    for s in range(1, rep):
        q = p ^ s
        got = swap(chunk(q).astype(jnp.float32), "rep", rep, s)
        others.append(got)
        got = (got + nothing).astype(jnp.bfloat16)
        columns = lax.dynamic_update_slice(columns, got, (0, q * depth, 0))
    moment = jnp.einsum("ekr,ejr->kj", columns, columns, preferred_element_type=jnp.float32)

    packed = pack(moment)
    steps = {a: [(a, n, d) for d in distances(n)] for a, n in (("lb", lb), ("rb", rb), ("rep", rep))}
    core, across = steps["lb"][:1], steps["lb"][1:]
    base = across + steps["rep"] + steps["rb"]
    near = across[:1] + steps["rep"][:1] + steps["rb"][:1]
    far = [step for step in base if step not in near]
    orders = [near[i:] + near[:i] + far for i in range(3)]
    (packed,), cut_core = reduce_scatter([packed], [core])
    third = packed.shape[1] // 3
    parts = [packed[:, i * third : (i + 1) * third] for i in range(3)]
    parts, cut = reduce_scatter(parts, orders)
    parts = all_gather(parts, orders, cut)
    (packed,) = all_gather([jnp.concatenate(parts, 1)], [core], cut_core)

    lower_half = unpack(packed, chi)
    dot = functools.partial(jnp.dot, preferred_element_type=jnp.float32)
    product = sum(dot(left, piece) for piece in split3(lower_half)[::-1])
    half_gram = sum(dot(piece, left.T) for piece in split3(product)[::-1])
    gram = half_gram + half_gram.T
    lower = jnp.linalg.cholesky(gram)
    weights = jax.scipy.linalg.solve_triangular(lower, left.astype(jnp.float32), lower=True)
    weights = lax.dynamic_slice_in_dim(weights, l * row_count, row_count, 0)

    scale = math.sqrt(phys * rb * right)
    site = jnp.zeros((east, chi, right), jnp.bfloat16)
    site = lax.dynamic_update_slice(site, own, (0, p * depth, 0))
    for s, got in zip(range(1, rep), others):
        for slot, piece in gather_slots(got, "lb", lb):
            owner = l ^ slot
            at = ((owner // right_parts) * east_part, (p ^ s) * depth, (owner % right_parts) * right_part)
            piece = (piece + nothing).astype(jnp.bfloat16)
            site = lax.dynamic_update_slice(site, piece, at)
    site_q = jnp.einsum(
        "ik,ekr->eir", (weights * scale).astype(jnp.bfloat16), site, preferred_element_type=jnp.float32
    )
    factor = lax.dynamic_slice_in_dim(lower, l * row_count, row_count, 0) / scale
    return (site_q, factor)


def solution(mesh):
    return jax.shard_map(
        functools.partial(shards, dict(mesh.shape)),
        mesh=mesh,
        in_specs=(P("lb", "rep"), P("rep", None, "rb"), P()),
        out_specs=(P("rep", "lb", "rb"), P("lb", None)),
        check_vma=False,
    )
```

```python
import functools
import math

import jax
import jax.numpy as jnp
from jax import lax
from jax.experimental import pallas as pl
from jax.experimental.pallas import tpu as pltpu
from jax.sharding import PartitionSpec as P

BLOCK = 128


def swap(array, axis, size, distance):
    return lax.ppermute(array, axis, [(i, i ^ distance) for i in range(size)])


def upper_bit(axis, distance):
    return lax.rem(lax.div(lax.axis_index(axis), distance), 2)


def distances(size):
    out = []
    while 1 << len(out) < size:
        out.append(1 << len(out))
    return out


def join(array, axis, size, distance, dim):
    other = swap(array, axis, size, distance)
    mine_second = upper_bit(axis, distance) == 1
    first = jnp.where(mine_second, other, array)
    second = jnp.where(mine_second, array, other)
    return jnp.concatenate([first, second], dim)


def halves(array, bit):
    half = array.shape[0] // 2
    mine = lax.dynamic_slice_in_dim(array, bit * half, half, 0)
    other = lax.dynamic_slice_in_dim(array, (1 - bit) * half, half, 0)
    return mine, other


def reduce_scatter(parts, orders):
    halved = []
    for stage in zip(*orders):
        sent, kept, cut = [], [], []
        for part, (axis, size, distance) in zip(parts, stage):
            cut.append(part.shape[0] % 16 == 0)
            if cut[-1]:
                mine, other = halves(part, upper_bit(axis, distance))
            else:
                mine, other = part, part
            kept.append(mine)
            sent.append(swap(other, axis, size, distance))
        parts = [k + s for k, s in zip(kept, sent)]
        halved.append(cut)
    return parts, halved


def all_gather(parts, orders, halved):
    stages = list(zip(*orders))
    for stage, cut in zip(stages[::-1], halved[::-1]):
        parts = [
            join(part, axis, size, distance, 0) if was_cut else part
            for part, (axis, size, distance), was_cut in zip(parts, stage, cut)
        ]
    return parts


def gather_slots(array, axis, size):
    held = [(0, array)]
    for d in distances(size)[::-1]:
        held += [(slot ^ d, swap(piece, axis, size, d)) for slot, piece in held]
    return held


def split3(array):
    high = lax.reduce_precision(array, 8, 7)
    rest = array - high
    middle = lax.reduce_precision(rest, 8, 7)
    low = rest - middle
    return [piece.astype(jnp.bfloat16) for piece in (high, middle, low)]


def pack(matrix):
    n = matrix.shape[0] // BLOCK
    rows = []
    for i in range(n // 2):
        j = n - 1 - i
        rows.append(
            jnp.concatenate(
                [
                    matrix[i * BLOCK : (i + 1) * BLOCK, : (i + 1) * BLOCK],
                    matrix[j * BLOCK : (j + 1) * BLOCK, : (j + 1) * BLOCK],
                ],
                1,
            )
        )
    return jnp.concatenate(rows, 0)


def unpack(packed, size):
    n = size // BLOCK
    rows = [None] * n
    for i in range(n // 2):
        j = n - 1 - i
        row = packed[i * BLOCK : (i + 1) * BLOCK]
        for at, lo in ((i, 0), (j, (i + 1) * BLOCK)):
            blocks = [row[:, lo : lo + at * BLOCK], row[:, lo + at * BLOCK : lo + (at + 1) * BLOCK] * 0.5]
            blocks.append(jnp.zeros((BLOCK, size - (at + 1) * BLOCK), packed.dtype))
            rows[at] = jnp.concatenate(blocks, 1)
    return jnp.concatenate(rows, 0)


def sub(x, s):
    return jnp.broadcast_to(x[s : s + 1, :], x.shape)


def lane(x, k):
    return jnp.broadcast_to(x[:, k : k + 1], x.shape)


def inverse_factor(block):
    n, wide = BLOCK // 8, 8
    rows = [block[8 * b : 8 * b + 8] for b in range(n)]
    sub_id = lax.broadcasted_iota(jnp.int32, (8, BLOCK), 0)
    lane_id = lax.broadcasted_iota(jnp.int32, (8, BLOCK), 1)
    pivots = []
    head = [lane(rows[0], c) for c in range(wide)]
    for b in range(n):
        k = wide * b
        cols = [[head[c]] + [lane(rows[i], k + c) for i in range(b + 1, n)] for c in range(wide)]
        if b + 1 < n:
            head = [lane(rows[b + 1], k + wide + c) for c in range(wide)]
        inside = (lane_id >= k) & (lane_id < k + wide)
        for i in range(b, n):
            rows[i] = jnp.where(inside, 0.0, rows[i])
        pivot = jnp.ones((8, BLOCK), jnp.float32)
        for c in range(wide):
            d = sub(cols[c][0], c)
            inverse = 1.0 / d
            pivot = jnp.where(sub_id == c, d, pivot)
            for c2 in range(c + 1, wide):
                m = sub(cols[c][0], c2) * inverse
                for i in range(n - b):
                    cols[c2][i] = cols[c2][i] - cols[c][i] * m
            factors = [cols[c][i] * inverse for i in range(n - b)]
            if b + 1 < n:
                for c2 in range(wide):
                    head[c2] = head[c2] - factors[1] * sub(cols[c][1], c2)
            factors[0] = jnp.where(sub_id > c, factors[0], 0.0)
            row = jnp.where(lane_id == k + c, 1.0, sub(rows[b], c))
            for i in range(n - b):
                rows[b + i] = rows[b + i] - factors[i] * row
        pivots.append(pivot)
    out = []
    for b in range(n):
        diagonal = sub_id + 8 * b
        row = jnp.where(lane_id < diagonal, rows[b], jnp.where(lane_id == diagonal, 1.0, 0.0))
        out.append(row * lax.rsqrt(pivots[b]))
    return jnp.concatenate(out, 0)


def split(x, pieces):
    out = []
    for i in range(pieces):
        out.append(x.astype(jnp.bfloat16))
        if i + 1 < pieces:
            x = x - out[-1].astype(jnp.float32)
    return out


def product(a, b):
    terms = [
        jnp.dot(a[i], b[j], preferred_element_type=jnp.float32)
        for i in range(len(a))
        for j in range(len(b))
        if i + j < max(len(a), len(b))
    ]
    return sum(terms[1:], terms[0])


PIECES = 2


def factor_kernel(scale, at_ref, gram_ref, left_ref, factor_ref, weights_ref, now, solved, lows, low):
    chi = gram_ref.shape[0]
    n = chi // BLOCK
    solved[...] = jnp.zeros_like(solved)
    lows[...] = jnp.zeros_like(lows)
    now[:, :chi] = gram_ref[:BLOCK]
    now[:, chi:] = left_ref[:BLOCK].astype(jnp.float32)

    def body(j, _):
        here = pl.ds(pl.multiple_of(j * BLOCK, BLOCK), BLOCK)
        after = pl.ds(pl.multiple_of(jnp.minimum(j + 1, n - 1) * BLOCK, BLOCK), BLOCK)
        inverse = split(inverse_factor(now[:, here]), PIECES)
        multiples = [lows[i, after, :] for i in range(PIECES)]
        next_gram = gram_ref[after, :] - product(multiples, [solved[i, :, :chi] for i in range(PIECES)])
        next_left = left_ref[after, :].astype(jnp.float32) - product(
            multiples, [solved[i, :, chi:] for i in range(PIECES)]
        )
        row = now[...]
        row_gram = product(inverse, split(row[:, :chi], PIECES))
        row_left = product(inverse, split(row[:, chi:], PIECES))
        row_gram_pieces, row_left_pieces = split(row_gram, PIECES), split(row_left, PIECES)
        for i in range(PIECES):
            solved[i, here, :chi] = row_gram_pieces[i]
            solved[i, here, chi:] = row_left_pieces[i]
        low[:, here] = row_gram.T
        for i, piece in enumerate(split(low[:, here], PIECES)):
            lows[i, :, here] = piece
        multiples = [lows[i, after, here] for i in range(PIECES)]
        now[:, :chi] = next_gram - product(multiples, row_gram_pieces)
        now[:, chi:] = next_left - product(multiples, row_left_pieces)
        return 0

    lax.fori_loop(0, n, body, 0)
    rows = factor_ref.shape[0]
    mine = pl.ds(pl.multiple_of(at_ref[0], 16), rows)
    row_id = lax.broadcasted_iota(jnp.int32, (rows, chi), 0) + at_ref[0]
    column_id = lax.broadcasted_iota(jnp.int32, (rows, chi), 1)
    factor_ref[...] = jnp.where(column_id <= row_id, low[mine, :] * (1.0 / scale), 0.0)
    weights_ref[...] = solved[0, mine, chi:]


def factorize(gram, left, at, rows, scale):
    chi = gram.shape[0]
    whole = pl.BlockSpec(memory_space=pltpu.VMEM)
    return pl.pallas_call(
        functools.partial(factor_kernel, scale),
        out_shape=[
            jax.ShapeDtypeStruct((rows, chi), jnp.float32),
            jax.ShapeDtypeStruct((rows, chi), jnp.bfloat16),
        ],
        in_specs=[pl.BlockSpec(memory_space=pltpu.SMEM), whole, whole],
        out_specs=[whole, whole],
        scratch_shapes=[
            pltpu.VMEM((BLOCK, 2 * chi), jnp.float32),
            pltpu.VMEM((PIECES, chi, 2 * chi), jnp.bfloat16),
            pltpu.VMEM((PIECES, chi, chi), jnp.bfloat16),
            pltpu.VMEM((chi, chi), jnp.float32),
        ],
        compiler_params=pltpu.CompilerParams(vmem_limit_bytes=48 * 2**20),
        cost_estimate=pl.CostEstimate(flops=6 * 2 * chi**3, bytes_accessed=8 * chi**2, transcendentals=0),
    )(at, gram, left)


def shards(sizes, left_factor, boundary_site, double_layer):
    lb, rb, rep = sizes["lb"], sizes["rb"], sizes["rep"]
    highest = lax.Precision.HIGHEST
    l, p = lax.axis_index("lb"), lax.axis_index("rep")
    depth, phys, right = boundary_site.shape
    east = phys // rep
    chi = depth * rep
    row_count = left_factor.shape[0]

    nothing = double_layer[0, 0] * 0.0

    rows = left_factor.astype(jnp.float32)
    for d in distances(rep):
        rows = join(rows, "rep", rep, d, 1)
    left = jnp.zeros((chi, chi), jnp.bfloat16)
    for slot, piece in gather_slots(rows, "lb", lb):
        piece = (piece + nothing).astype(jnp.bfloat16)
        left = lax.dynamic_update_slice(left, piece, ((l ^ slot) * row_count, 0))

    absorbed = jnp.einsum(
        "kur,ue->ekr", boundary_site.astype(jnp.float32), double_layer, precision=highest
    ).astype(jnp.bfloat16)
    own = lax.dynamic_slice_in_dim(absorbed, p * east, east, 0)

    east_part, right_parts = max(1, east // lb), max(1, lb // east)
    right_part = right // right_parts
    east_at, right_at = (l // right_parts) * east_part, (l % right_parts) * right_part

    def chunk(q):
        return lax.dynamic_slice(
            absorbed, (q * east + east_at, 0, right_at), (east_part, depth, right_part)
        )

    columns = jnp.zeros((east_part, chi, right_part), jnp.bfloat16)
    columns = lax.dynamic_update_slice(columns, chunk(p), (0, p * depth, 0))
    others = []
    for s in range(1, rep):
        q = p ^ s
        got = swap(chunk(q).astype(jnp.float32), "rep", rep, s)
        others.append(got)
        got = (got + nothing).astype(jnp.bfloat16)
        columns = lax.dynamic_update_slice(columns, got, (0, q * depth, 0))
    moment = jnp.einsum("ekr,ejr->kj", columns, columns, preferred_element_type=jnp.float32)

    packed = pack(moment)
    steps = {a: [(a, n, d) for d in distances(n)] for a, n in (("lb", lb), ("rb", rb), ("rep", rep))}
    core, across = steps["lb"][:1], steps["lb"][1:]
    base = across + steps["rep"] + steps["rb"]
    near = across[:1] + steps["rep"][:1] + steps["rb"][:1]
    far = [step for step in base if step not in near]
    orders = [near[i:] + near[:i] + far for i in range(3)]
    (packed,), cut_core = reduce_scatter([packed], [core])
    third = packed.shape[1] // 3
    parts = [packed[:, i * third : (i + 1) * third] for i in range(3)]
    parts, cut = reduce_scatter(parts, orders)
    parts = all_gather(parts, orders, cut)
    (packed,) = all_gather([jnp.concatenate(parts, 1)], [core], cut_core)

    lower_half = unpack(packed, chi)
    dot = functools.partial(jnp.dot, preferred_element_type=jnp.float32)
    product = sum(dot(left, piece) for piece in split3(lower_half)[::-1])
    half_gram = sum(dot(piece, left.T) for piece in split3(product)[::-1])
    gram = half_gram + half_gram.T
    scale = math.sqrt(phys * rb * right)
    at = (l * row_count).astype(jnp.int32)[None]
    factor, weights = factorize(gram, left, at, row_count, scale)

    site = jnp.zeros((east, chi, right), jnp.bfloat16)
    site = lax.dynamic_update_slice(site, own, (0, p * depth, 0))
    for s, got in zip(range(1, rep), others):
        for slot, piece in gather_slots(got, "lb", lb):
            owner = l ^ slot
            at = ((owner // right_parts) * east_part, (p ^ s) * depth, (owner % right_parts) * right_part)
            piece = (piece + nothing).astype(jnp.bfloat16)
            site = lax.dynamic_update_slice(site, piece, at)
    site_q = jnp.einsum("ik,ekr->eir", weights, site, preferred_element_type=jnp.float32) * scale
    return (site_q, factor)


def solution(mesh):
    return jax.shard_map(
        functools.partial(shards, dict(mesh.shape)),
        mesh=mesh,
        in_specs=(P("lb", "rep"), P("rep", None, "rb"), P()),
        out_specs=(P("rep", "lb", "rb"), P("lb", None)),
        check_vma=False,
    )
```

```python
import functools
import math

import jax
import jax.numpy as jnp
from jax import lax
from jax.experimental import pallas as pl
from jax.experimental.pallas import tpu as pltpu
from jax.sharding import PartitionSpec as P

BLOCK = 128


def swap(array, step):
    axis, size, distance = step
    return lax.ppermute(array, axis, [(i, i ^ distance) for i in range(size)])


def steps_of(axis, size):
    return [(axis, size, 1 << i) for i in range(size.bit_length() - 1)]


def gather_slots(held, steps):
    for step in steps:
        held = held + [(slot ^ step[2], swap(piece, step)) for slot, piece in held]
    return held


def cut_steps(steps, rows):
    count = 0
    while count < len(steps) and rows % 16 == 0:
        rows, count = rows // 2, count + 1
    return count


def position(steps):
    place = jnp.int32(0)
    for axis, _, distance in steps:
        place = place * 2 + lax.rem(lax.div(lax.axis_index(axis), distance), 2)
    return place


def reduce_parts(parts, orders, cuts):
    for at in range(max(map(len, orders))):
        moving = [(i, orders[i][at]) for i in range(len(parts)) if at < len(orders[i])]
        kept, got = {}, {}
        for i, step in moving:
            half = parts[i].shape[0] // 2
            kept[i], sent = (parts[i][:half], parts[i][half:]) if at < cuts[i] else (parts[i], parts[i])
            got[i] = swap(sent, step)
        parts = [kept[i] + got[i] if i in got else part for i, part in enumerate(parts)]
    return parts


def gather_parts(parts, orders, cuts):
    for at in range(max(cuts) - 1, -1, -1):
        got = {i: swap(parts[i], orders[i][at]) for i in range(len(parts)) if at < cuts[i]}
        parts = [jnp.concatenate([part, got[i]], 0) if i in got else part for i, part in enumerate(parts)]
    return parts


HIGHEST = lax.Precision.HIGHEST
GROUP = 16
PIECES = 2


def dot(a, b, transposed=False):
    dims = (((1,), (1 if transposed else 0,)), ((), ()))
    return lax.dot_general(a, b, dims, preferred_element_type=jnp.float32)


def absorb_kernel(east_parts, legs_ref, site_ref, double_ref, *out_refs):
    phys = double_ref.shape[0]
    legs = sum(east_parts)
    row = lax.broadcasted_iota(jnp.int32, (legs * GROUP, GROUP * phys), 0)
    column = lax.broadcasted_iota(jnp.int32, (legs * GROUP, GROUP * phys), 1)
    chosen = jnp.concatenate(
        [
            jnp.where(lax.broadcasted_iota(jnp.int32, (GROUP, phys), 1) == legs_ref[i], 1.0, 0.0)
            for i in range(legs)
        ],
        0,
    )
    values = lax.dot_general(
        chosen, double_ref[...], (((1,), (1,)), ((), ())), precision=HIGHEST, preferred_element_type=jnp.float32
    )
    spread = jnp.where(
        lax.broadcasted_iota(jnp.int32, (phys, GROUP * phys), 0)
        == lax.rem(lax.broadcasted_iota(jnp.int32, (phys, GROUP * phys), 1), phys),
        1.0,
        0.0,
    )
    values = jnp.dot(values, spread, precision=HIGHEST, preferred_element_type=jnp.float32)
    high, low = split(jnp.where(lax.rem(row, GROUP) == lax.div(column, phys), values, 0.0), 2)
    groups = site_ref.shape[0] // (GROUP * phys)
    for g in range(groups):
        rows = site_ref[g * GROUP * phys : (g + 1) * GROUP * phys, :]
        absorbed = (dot(high, rows) + dot(low, rows)).astype(jnp.bfloat16)
        leg = 0
        for out_ref, count in zip(out_refs, east_parts):
            for e in range(count):
                piece = absorbed[(leg + e) * GROUP : (leg + e + 1) * GROUP]
                out_ref[e, g * GROUP : (g + 1) * GROUP, :] = piece.astype(out_ref.dtype)
            leg += count


def absorb(boundary_site, double_layer, legs, east_parts):
    depth, phys, right = boundary_site.shape
    tiles = max(1, depth // 128)
    tile = depth // tiles
    out_shape, out_specs = [], []
    for i, count in enumerate(east_parts):
        out_shape.append(jax.ShapeDtypeStruct((count, depth, right), jnp.bfloat16 if i == 0 else jnp.float32))
        out_specs.append(pl.BlockSpec((count, tile, right), lambda t: (0, t, 0)))
    return pl.pallas_call(
        functools.partial(absorb_kernel, east_parts),
        grid=(tiles,),
        out_shape=out_shape,
        in_specs=[
            pl.BlockSpec(memory_space=pltpu.SMEM),
            pl.BlockSpec((tile * phys, right), lambda t: (t, 0)),
            pl.BlockSpec(memory_space=pltpu.VMEM),
        ],
        out_specs=out_specs,
        compiler_params=pltpu.CompilerParams(vmem_limit_bytes=32 * 2**20),
        cost_estimate=pl.CostEstimate(
            flops=2 * 2 * depth * right * GROUP * phys * sum(east_parts), bytes_accessed=8 * depth * right * phys, transcendentals=0
        ),
    )(legs, boundary_site.reshape(depth * phys, right), double_layer)


def moment_kernel(chi, chunk, third, place_ref, *refs):
    *block_refs, kept_ref, sent_ref, columns, packed = refs
    rep = len(block_refs)
    count, depth, width = block_refs[0].shape
    n = chi // BLOCK
    for i, block_ref in enumerate(block_refs):
        at = pl.ds(pl.multiple_of((place_ref[0] ^ i) * depth, depth), depth)
        for e in range(count):
            columns[at, e * width : (e + 1) * width] = block_ref[e].astype(jnp.bfloat16)
    for i in range(n):
        group, lo = (i, 0) if i < n // 2 else (n - 1 - i, (n - i) * BLOCK)
        packed[group * BLOCK : (group + 1) * BLOCK, lo : lo + (i + 1) * BLOCK] = dot(
            columns[i * BLOCK : (i + 1) * BLOCK], columns[: (i + 1) * BLOCK], True
        )
    half = kept_ref.shape[0]
    for part in range(3):
        lanes = slice(part * third, (part + 1) * third)
        for t in range(packed.shape[0] // chunk):
            rows = pl.ds(pl.multiple_of((place_ref[1 + part] ^ t) * chunk, 8), chunk)
            at = t * chunk
            to_ref = kept_ref if at < half else sent_ref
            to_ref[at % half : at % half + chunk, lanes] = packed[rows, lanes]


def moment(blocks, places, chi, chunk):
    rows, width = chi // 2, chi + BLOCK
    count, _, right = blocks[0].shape
    whole = pl.BlockSpec(memory_space=pltpu.VMEM)
    return pl.pallas_call(
        functools.partial(moment_kernel, chi, chunk, width // 3),
        out_shape=[jax.ShapeDtypeStruct((rows // 2, width), jnp.float32)] * 2,
        in_specs=[pl.BlockSpec(memory_space=pltpu.SMEM)] + [whole] * len(blocks),
        out_specs=[whole, whole],
        scratch_shapes=[pltpu.VMEM((chi, count * right), jnp.bfloat16), pltpu.VMEM((rows, width), jnp.float32)],
        compiler_params=pltpu.CompilerParams(vmem_limit_bytes=32 * 2**20),
        cost_estimate=pl.CostEstimate(flops=chi * chi * count * right, bytes_accessed=6 * chi * chi, transcendentals=0),
    )(places, *blocks)


def sub(x, s):
    return jnp.broadcast_to(x[s : s + 1, :], x.shape)


def lane(x, k):
    return jnp.broadcast_to(x[:, k : k + 1], x.shape)


def inverse_factor(block):
    n, wide = BLOCK // 8, 8
    rows = [block[8 * b : 8 * b + 8] for b in range(n)]
    sub_id = lax.broadcasted_iota(jnp.int32, (8, BLOCK), 0)
    lane_id = lax.broadcasted_iota(jnp.int32, (8, BLOCK), 1)
    pivots = []
    head = [lane(rows[0], c) for c in range(wide)]
    for b in range(n):
        k = wide * b
        cols = [[head[c]] + [lane(rows[i], k + c) for i in range(b + 1, n)] for c in range(wide)]
        if b + 1 < n:
            head = [lane(rows[b + 1], k + wide + c) for c in range(wide)]
        inside = (lane_id >= k) & (lane_id < k + wide)
        for i in range(b, n):
            rows[i] = jnp.where(inside, 0.0, rows[i])
        pivot = jnp.ones((8, BLOCK), jnp.float32)
        for c in range(wide):
            d = sub(cols[c][0], c)
            inverse = 1.0 / d
            pivot = jnp.where(sub_id == c, d, pivot)
            for c2 in range(c + 1, wide):
                m = sub(cols[c][0], c2) * inverse
                for i in range(n - b):
                    cols[c2][i] = cols[c2][i] - cols[c][i] * m
            factors = [cols[c][i] * inverse for i in range(n - b)]
            if b + 1 < n:
                for c2 in range(wide):
                    head[c2] = head[c2] - factors[1] * sub(cols[c][1], c2)
            factors[0] = jnp.where(sub_id > c, factors[0], 0.0)
            row = jnp.where(lane_id == k + c, 1.0, sub(rows[b], c))
            for i in range(n - b):
                rows[b + i] = rows[b + i] - factors[i] * row
        pivots.append(pivot)
    out = []
    for b in range(n):
        diagonal = sub_id + 8 * b
        row = jnp.where(lane_id < diagonal, rows[b], jnp.where(lane_id == diagonal, 1.0, 0.0))
        out.append(row * lax.rsqrt(pivots[b]))
    return jnp.concatenate(out, 0)


def split(x, pieces):
    out = []
    for i in range(pieces):
        out.append(x.astype(jnp.bfloat16))
        if i + 1 < pieces:
            x = x - out[-1].astype(jnp.float32)
    return out


def product(a, b):
    terms = [
        jnp.dot(a[i], b[j], preferred_element_type=jnp.float32)
        for i in range(len(a))
        for j in range(len(b))
        if i + j < max(len(a), len(b))
    ]
    return sum(terms[1:], terms[0])


def factor_kernel(scale, chunk, place_ref, mine_ref, other_ref, *refs):
    *left_refs, factor_ref, weights_ref, left, packed, moments, now, solved, lows, low = refs
    chi = left.shape[0]
    n = chi // BLOCK
    rows, width = left_refs[0].shape
    across = chi // width
    for i, left_ref in enumerate(left_refs):
        row_at = pl.multiple_of((place_ref[0] ^ (i // across)) * rows, 16)
        column_at = pl.multiple_of((place_ref[1] ^ (i % across)) * width, 128)
        left[pl.ds(row_at, rows), pl.ds(column_at, width)] = left_ref[...].astype(jnp.bfloat16)
    half, third = mine_ref.shape[0], mine_ref.shape[1] // 3
    for part in range(3):
        lanes = slice(part * third, (part + 1) * third)
        for t in range(2 * half // chunk):
            at = pl.ds(pl.multiple_of((place_ref[2 + part] ^ t) * chunk, 8), chunk)
            from_ref = mine_ref if t * chunk < half else other_ref
            packed[at, lanes] = from_ref[t * chunk % half : t * chunk % half + chunk, lanes]
    for i in range(n):
        group, lo = (i, 0) if i < n // 2 else (n - 1 - i, (n - i) * BLOCK)
        for k in range(i + 1):
            block = packed[group * BLOCK : (group + 1) * BLOCK, lo + k * BLOCK : lo + (k + 1) * BLOCK]
            for piece, value in enumerate(split(block, PIECES)):
                moments[piece, i * BLOCK : (i + 1) * BLOCK, k * BLOCK : (k + 1) * BLOCK] = value
            if k < i:
                for piece, value in enumerate(split(block.T, PIECES)):
                    moments[piece, k * BLOCK : (k + 1) * BLOCK, i * BLOCK : (i + 1) * BLOCK] = value
    solved[...] = jnp.zeros_like(solved)
    lows[...] = jnp.zeros_like(lows)

    def gram_row(at):
        held = left[at, :]
        row = sum(dot(held, moments[i]) for i in range(PIECES))
        return sum(dot(piece, left[...], True) for piece in split(row, PIECES))

    now[:, :chi] = gram_row(pl.ds(0, BLOCK))
    now[:, chi:] = left[:BLOCK, :].astype(jnp.float32)

    def body(j, _):
        here = pl.ds(pl.multiple_of(j * BLOCK, BLOCK), BLOCK)
        after = pl.ds(pl.multiple_of(jnp.minimum(j + 1, n - 1) * BLOCK, BLOCK), BLOCK)
        inverse = split(inverse_factor(now[:, here]), PIECES)
        multiples = [lows[i, after, :] for i in range(PIECES)]
        next_gram = gram_row(after) - product(multiples, [solved[i, :, :chi] for i in range(PIECES)])
        next_left = left[after, :].astype(jnp.float32) - product(
            multiples, [solved[i, :, chi:] for i in range(PIECES)]
        )
        row = now[...]
        row_gram = product(inverse, split(row[:, :chi], PIECES))
        row_left = product(inverse, split(row[:, chi:], PIECES))
        row_gram_pieces, row_left_pieces = split(row_gram, PIECES), split(row_left, PIECES)
        for i in range(PIECES):
            solved[i, here, :chi] = row_gram_pieces[i]
            solved[i, here, chi:] = row_left_pieces[i]
        low[:, here] = row_gram.T
        for i, piece in enumerate(split(low[:, here], PIECES)):
            lows[i, :, here] = piece
        multiples = [lows[i, after, here] for i in range(PIECES)]
        now[:, :chi] = next_gram - product(multiples, row_gram_pieces)
        now[:, chi:] = next_left - product(multiples, row_left_pieces)
        return 0

    lax.fori_loop(0, n, body, 0)
    count = factor_ref.shape[0]
    first = place_ref[0] * count
    mine = pl.ds(pl.multiple_of(first, 16), count)
    row_id = lax.broadcasted_iota(jnp.int32, (count, chi), 0) + first
    column_id = lax.broadcasted_iota(jnp.int32, (count, chi), 1)
    factor_ref[...] = jnp.where(column_id <= row_id, low[mine, :] * (1.0 / scale), 0.0)
    weights_ref[...] = solved[0, mine, chi:]


def factorize(mine, other, left_blocks, places, chi, chunk, scale):
    rows = left_blocks[0].shape[0]
    whole = pl.BlockSpec(memory_space=pltpu.VMEM)
    return pl.pallas_call(
        functools.partial(factor_kernel, scale, chunk),
        out_shape=[
            jax.ShapeDtypeStruct((rows, chi), jnp.float32),
            jax.ShapeDtypeStruct((rows, chi), jnp.bfloat16),
        ],
        in_specs=[pl.BlockSpec(memory_space=pltpu.SMEM)] + [whole] * (2 + len(left_blocks)),
        out_specs=[whole, whole],
        scratch_shapes=[
            pltpu.VMEM((chi, chi), jnp.bfloat16),
            pltpu.VMEM((chi // 2, chi + BLOCK), jnp.float32),
            pltpu.VMEM((PIECES, chi, chi), jnp.bfloat16),
            pltpu.VMEM((BLOCK, 2 * chi), jnp.float32),
            pltpu.VMEM((PIECES, chi, 2 * chi), jnp.bfloat16),
            pltpu.VMEM((PIECES, chi, chi), jnp.bfloat16),
            pltpu.VMEM((chi, chi), jnp.float32),
        ],
        compiler_params=pltpu.CompilerParams(vmem_limit_bytes=52 * 2**20),
        cost_estimate=pl.CostEstimate(flops=20 * 2 * chi**3, bytes_accessed=16 * chi**2, transcendentals=0),
    )(places, mine, other, *left_blocks)


def site_kernel(scale, place_ref, weights_ref, own_ref, *refs):
    *got_refs, out_ref = refs
    depth = own_ref.shape[1]
    mine = weights_ref[:, pl.ds(pl.multiple_of(place_ref[1] * depth, depth), depth)]
    other = weights_ref[:, pl.ds(pl.multiple_of((place_ref[1] ^ 1) * depth, depth), depth)]
    for slot, got_ref in enumerate(got_refs):
        count = got_ref.shape[0]
        for i in range(count):
            e = (place_ref[0] ^ slot) * count + i
            out_ref[e] = scale * (dot(mine, own_ref[e]) + dot(other, got_ref[i].astype(jnp.bfloat16)))


def make_site(weights, own, got, places, scale):
    rows, chi = weights.shape
    east, _, right = own.shape
    whole = pl.BlockSpec(memory_space=pltpu.VMEM)
    return pl.pallas_call(
        functools.partial(site_kernel, scale),
        out_shape=jax.ShapeDtypeStruct((east, rows, right), jnp.float32),
        in_specs=[pl.BlockSpec(memory_space=pltpu.SMEM)] + [whole] * (2 + len(got)),
        out_specs=whole,
        compiler_params=pltpu.CompilerParams(vmem_limit_bytes=32 * 2**20),
        cost_estimate=pl.CostEstimate(flops=2 * rows * chi * east * right, bytes_accessed=8 * east * chi * right, transcendentals=0),
    )(places, weights, own, *got)


def shards(sizes, left_factor, boundary_site, double_layer):
    lb, rb, rep = sizes["lb"], sizes["rb"], sizes["rep"]
    l, p = lax.axis_index("lb"), lax.axis_index("rep")
    depth, phys, right = boundary_site.shape
    east = phys // rep
    chi = depth * rep
    scale = math.sqrt(phys * rb * right)
    steps = {axis: steps_of(axis, size) for axis, size in sizes.items()}
    core, across = steps["lb"][:1], steps["lb"][1:]

    left_blocks = gather_slots([(0, left_factor.astype(jnp.float32))], steps["rep"])
    left_blocks = [piece for _, piece in sorted(left_blocks, key=lambda pair: pair[0])]
    left_blocks = [gather_slots([(0, piece)], across[::-1] + core) for piece in left_blocks]
    left_blocks = [sorted(pieces, key=lambda pair: pair[0]) for pieces in left_blocks]
    left_blocks = [left_blocks[q][s][1] for s in range(lb) for q in range(rep)]

    east_part, right_parts = max(1, east // lb), max(1, lb // east)
    right_part = right // right_parts
    east_at, right_at = (l // right_parts) * east_part, (l % right_parts) * right_part
    legs = [p * east + i for i in range(east)]
    for s in range(1, rep):
        legs += [(p ^ s) * east + east_at + i for i in range(east_part)]
    legs = jnp.stack(legs).astype(jnp.int32)
    own, *sent = absorb(boundary_site, double_layer, legs, [east] + [east_part] * (rep - 1))
    if right_parts > 1:
        sent = [lax.dynamic_slice_in_dim(piece, right_at, right_part, 2) for piece in sent]
    got = [swap(piece, ("rep", rep, s)) for s, piece in zip(range(1, rep), sent)]
    share = lax.dynamic_slice(own, (east_at, 0, right_at), (east_part, depth, right_part))

    near = across[:1] + steps["rep"][:1] + steps["rb"][:1]
    far = [step for step in across + steps["rep"] + steps["rb"] if step not in near]
    orders = [near[i:] + near[:i] + far for i in range(3)]
    cut = cut_steps(orders[0], chi // 4)
    chunk = (chi // 4) >> cut
    bits = [position(core + order[:cut]) for order in orders]
    places = jnp.stack([p] + bits).astype(jnp.int32)
    kept, sent = moment([share] + got, places, chi, chunk)
    whole = kept + swap(sent, core[0])
    third = whole.shape[1] // 3
    parts = [whole[:, i * third : (i + 1) * third] for i in range(3)]
    parts = reduce_parts(parts, orders, [cut] * 3)
    parts = gather_parts(parts, orders, [cut] * 3)
    whole = jnp.concatenate(parts, 1)
    other = swap(whole, core[0])

    got = [gather_slots([(0, piece)], core) for piece in got]
    held, whole = lax.optimization_barrier(([[piece for _, piece in pieces] for pieces in got], whole))
    got = [gather_slots(list(zip(range(2), pieces)), across[::-1]) for pieces in held]

    places = jnp.stack([l, p] + bits).astype(jnp.int32)
    factor, weights = factorize(whole, other, left_blocks, places, chi, chunk, scale)
    if rep == 2 and right_parts == 1:
        pieces = [piece for _, piece in sorted(got[0], key=lambda pair: pair[0])]
        site_q = make_site(weights, own, pieces, places, scale)
    else:
        nothing = double_layer[0, 0] * 0.0
        site = jnp.zeros((east, chi, right), jnp.bfloat16)
        site = lax.dynamic_update_slice(site, own, (0, p * depth, 0))
        for s, pieces in zip(range(1, rep), got):
            for slot, piece in pieces:
                owner = l ^ slot
                at = ((owner // right_parts) * east_part, (p ^ s) * depth, (owner % right_parts) * right_part)
                site = lax.dynamic_update_slice(site, (piece + nothing).astype(jnp.bfloat16), at)
        site_q = jnp.einsum("ik,ekr->eir", weights, site, preferred_element_type=jnp.float32) * scale
    return (site_q, factor)


def solution(mesh):
    return jax.shard_map(
        functools.partial(shards, dict(mesh.shape)),
        mesh=mesh,
        in_specs=(P("lb", "rep"), P("rep", None, "rb"), P()),
        out_specs=(P("rep", "lb", "rb"), P("lb", None)),
        check_vma=False,
    )
```

```python
import functools
import math

import jax
import jax.numpy as jnp
from jax import lax
from jax.experimental import pallas as pl
from jax.experimental.pallas import tpu as pltpu
from jax.sharding import PartitionSpec as P

BLOCK = 128


def swap(array, step):
    axis, size, distance = step
    return lax.ppermute(array, axis, [(i, i ^ distance) for i in range(size)])


def steps_of(axis, size):
    return [(axis, size, 1 << i) for i in range(size.bit_length() - 1)]


def gather_slots(held, steps):
    for step in steps:
        held = held + [(slot ^ step[2], swap(piece, step)) for slot, piece in held]
    return held


def cut_steps(steps, rows):
    count = 0
    while count < len(steps) and rows % 16 == 0:
        rows, count = rows // 2, count + 1
    return count


def position(steps):
    place = jnp.int32(0)
    for axis, _, distance in steps:
        place = place * 2 + lax.rem(lax.div(lax.axis_index(axis), distance), 2)
    return place


def swap_parts(parts, steps):
    parts = lax.optimization_barrier(parts)
    return lax.optimization_barrier([swap(part, step) for part, step in zip(parts, steps)])


def reduce_parts(parts, orders, cuts):
    for at in range(cuts):
        half = parts[0].shape[0] // 2
        got = swap_parts([part[half:] for part in parts], [order[at] for order in orders])
        parts = [part[:half] + other for part, other in zip(parts, got)]
    return parts


def gather_parts(parts, orders, cuts):
    for at in range(cuts - 1, -1, -1):
        got = swap_parts(parts, [order[at] for order in orders])
        parts = [jnp.concatenate([part, other], 0) for part, other in zip(parts, got)]
    return parts


HIGHEST = lax.Precision.HIGHEST
GROUP = 16
PIECES = 2


def dot(a, b, transposed=False):
    dims = (((1,), (1 if transposed else 0,)), ((), ()))
    return lax.dot_general(a, b, dims, preferred_element_type=jnp.float32)


def absorb_kernel(east_parts, legs_ref, site_ref, double_ref, *out_refs):
    phys = double_ref.shape[0]
    legs = sum(east_parts)
    row = lax.broadcasted_iota(jnp.int32, (legs * GROUP, GROUP * phys), 0)
    column = lax.broadcasted_iota(jnp.int32, (legs * GROUP, GROUP * phys), 1)
    chosen = jnp.concatenate(
        [
            jnp.where(lax.broadcasted_iota(jnp.int32, (GROUP, phys), 1) == legs_ref[i], 1.0, 0.0)
            for i in range(legs)
        ],
        0,
    )
    values = lax.dot_general(
        chosen, double_ref[...], (((1,), (1,)), ((), ())), precision=HIGHEST, preferred_element_type=jnp.float32
    )
    spread = jnp.where(
        lax.broadcasted_iota(jnp.int32, (phys, GROUP * phys), 0)
        == lax.rem(lax.broadcasted_iota(jnp.int32, (phys, GROUP * phys), 1), phys),
        1.0,
        0.0,
    )
    values = jnp.dot(values, spread, precision=HIGHEST, preferred_element_type=jnp.float32)
    high, low = split(jnp.where(lax.rem(row, GROUP) == lax.div(column, phys), values, 0.0), 2)
    groups = site_ref.shape[0] // (GROUP * phys)
    for g in range(groups):
        rows = site_ref[g * GROUP * phys : (g + 1) * GROUP * phys, :]
        absorbed = (dot(high, rows) + dot(low, rows)).astype(jnp.bfloat16)
        leg = 0
        for out_ref, count in zip(out_refs, east_parts):
            for e in range(count):
                piece = absorbed[(leg + e) * GROUP : (leg + e + 1) * GROUP]
                out_ref[e, g * GROUP : (g + 1) * GROUP, :] = piece.astype(out_ref.dtype)
            leg += count


def absorb(boundary_site, double_layer, legs, east_parts, dtype):
    legs = jnp.stack(legs).astype(jnp.int32)
    depth, phys, right = boundary_site.shape
    tiles = max(1, depth // 128)
    tile = depth // tiles
    out_shape, out_specs = [], []
    for count in east_parts:
        out_shape.append(jax.ShapeDtypeStruct((count, depth, right), dtype))
        out_specs.append(pl.BlockSpec((count, tile, right), lambda t: (0, t, 0)))
    return pl.pallas_call(
        functools.partial(absorb_kernel, east_parts),
        grid=(tiles,),
        out_shape=out_shape,
        in_specs=[
            pl.BlockSpec(memory_space=pltpu.SMEM),
            pl.BlockSpec((tile * phys, right), lambda t: (t, 0)),
            pl.BlockSpec(memory_space=pltpu.VMEM),
        ],
        out_specs=out_specs,
        compiler_params=pltpu.CompilerParams(vmem_limit_bytes=32 * 2**20),
        cost_estimate=pl.CostEstimate(
            flops=2 * 2 * depth * right * GROUP * phys * sum(east_parts), bytes_accessed=8 * depth * right * phys, transcendentals=0
        ),
    )(legs, boundary_site.reshape(depth * phys, right), double_layer)


def moment_kernel(chi, chunk, third, place_ref, *refs):
    *block_refs, kept_ref, sent_ref, columns, packed = refs
    rep = len(block_refs)
    count, depth, width = block_refs[0].shape
    n = chi // BLOCK
    for i, block_ref in enumerate(block_refs):
        at = pl.ds(pl.multiple_of((place_ref[0] ^ i) * depth, depth), depth)
        for e in range(count):
            columns[at, e * width : (e + 1) * width] = block_ref[e].astype(jnp.bfloat16)
    for i in range(n):
        group, lo = (i, 0) if i < n // 2 else (n - 1 - i, (n - i) * BLOCK)
        packed[group * BLOCK : (group + 1) * BLOCK, lo : lo + (i + 1) * BLOCK] = dot(
            columns[i * BLOCK : (i + 1) * BLOCK], columns[: (i + 1) * BLOCK], True
        )
    half = kept_ref.shape[0]
    for part in range(3):
        lanes = slice(part * third, (part + 1) * third)
        for t in range(packed.shape[0] // chunk):
            rows = pl.ds(pl.multiple_of((place_ref[1 + part] ^ t) * chunk, 8), chunk)
            at = t * chunk
            to_ref = kept_ref if at < half else sent_ref
            to_ref[at % half : at % half + chunk, lanes] = packed[rows, lanes]


def moment(blocks, places, chi, chunk):
    rows, width = chi // 2, chi + BLOCK
    count, _, right = blocks[0].shape
    whole = pl.BlockSpec(memory_space=pltpu.VMEM)
    return pl.pallas_call(
        functools.partial(moment_kernel, chi, chunk, width // 3),
        out_shape=[jax.ShapeDtypeStruct((rows // 2, width), jnp.float32)] * 2,
        in_specs=[pl.BlockSpec(memory_space=pltpu.SMEM)] + [whole] * len(blocks),
        out_specs=[whole, whole],
        scratch_shapes=[pltpu.VMEM((chi, count * right), jnp.bfloat16), pltpu.VMEM((rows, width), jnp.float32)],
        compiler_params=pltpu.CompilerParams(vmem_limit_bytes=32 * 2**20),
        cost_estimate=pl.CostEstimate(flops=chi * chi * count * right, bytes_accessed=6 * chi * chi, transcendentals=0),
    )(places, *blocks)


def sub(x, s):
    return jnp.broadcast_to(x[s : s + 1, :], x.shape)


def lane(x, k):
    return jnp.broadcast_to(x[:, k : k + 1], x.shape)


def inverse_factor(block):
    n, wide = BLOCK // 8, 8
    rows = [block[8 * b : 8 * b + 8] for b in range(n)]
    sub_id = lax.broadcasted_iota(jnp.int32, (8, BLOCK), 0)
    lane_id = lax.broadcasted_iota(jnp.int32, (8, BLOCK), 1)
    pivots = []
    head = [lane(rows[0], c) for c in range(wide)]
    for b in range(n):
        k = wide * b
        cols = [[head[c]] + [lane(rows[i], k + c) for i in range(b + 1, n)] for c in range(wide)]
        if b + 1 < n:
            head = [lane(rows[b + 1], k + wide + c) for c in range(wide)]
        inside = (lane_id >= k) & (lane_id < k + wide)
        for i in range(b, n):
            rows[i] = jnp.where(inside, 0.0, rows[i])
        pivot = jnp.ones((8, BLOCK), jnp.float32)
        for c in range(wide):
            d = sub(cols[c][0], c)
            inverse = 1.0 / d
            pivot = jnp.where(sub_id == c, d, pivot)
            for c2 in range(c + 1, wide):
                m = sub(cols[c][0], c2) * inverse
                for i in range(n - b):
                    cols[c2][i] = cols[c2][i] - cols[c][i] * m
            factors = [cols[c][i] * inverse for i in range(n - b)]
            if b + 1 < n:
                for c2 in range(wide):
                    head[c2] = head[c2] - factors[1] * sub(cols[c][1], c2)
            factors[0] = jnp.where(sub_id > c, factors[0], 0.0)
            row = jnp.where(lane_id == k + c, 1.0, sub(rows[b], c))
            for i in range(n - b):
                rows[b + i] = rows[b + i] - factors[i] * row
        pivots.append(pivot)
    out = []
    for b in range(n):
        diagonal = sub_id + 8 * b
        row = jnp.where(lane_id < diagonal, rows[b], jnp.where(lane_id == diagonal, 1.0, 0.0))
        out.append(row * lax.rsqrt(pivots[b]))
    return jnp.concatenate(out, 0)


def split(x, pieces):
    out = []
    for i in range(pieces):
        out.append(x.astype(jnp.bfloat16))
        if i + 1 < pieces:
            x = x - out[-1].astype(jnp.float32)
    return out


def product(a, b):
    terms = [
        jnp.dot(a[i], b[j], preferred_element_type=jnp.float32)
        for i in range(len(a))
        for j in range(len(b))
        if i + j < max(len(a), len(b))
    ]
    return sum(terms[1:], terms[0])


def factor_kernel(scale, chunk, place_ref, mine_ref, other_ref, *refs):
    *left_refs, factor_ref, weights_ref, left, packed, moments, now, solved, lows, low = refs
    chi = left.shape[0]
    n = chi // BLOCK
    rows, width = left_refs[0].shape
    across = chi // width
    for i, left_ref in enumerate(left_refs):
        row_at = pl.multiple_of((place_ref[0] ^ (i // across)) * rows, 16)
        column_at = pl.multiple_of((place_ref[1] ^ (i % across)) * width, 128)
        left[pl.ds(row_at, rows), pl.ds(column_at, width)] = left_ref[...].astype(jnp.bfloat16)
    half, third = mine_ref.shape[0], mine_ref.shape[1] // 3
    for part in range(3):
        lanes = slice(part * third, (part + 1) * third)
        for t in range(2 * half // chunk):
            at = pl.ds(pl.multiple_of((place_ref[2 + part] ^ t) * chunk, 8), chunk)
            from_ref = mine_ref if t * chunk < half else other_ref
            packed[at, lanes] = from_ref[t * chunk % half : t * chunk % half + chunk, lanes]
    for i in range(n):
        group, lo = (i, 0) if i < n // 2 else (n - 1 - i, (n - i) * BLOCK)
        for k in range(i + 1):
            block = packed[group * BLOCK : (group + 1) * BLOCK, lo + k * BLOCK : lo + (k + 1) * BLOCK]
            for piece, value in enumerate(split(block, PIECES)):
                moments[piece, i * BLOCK : (i + 1) * BLOCK, k * BLOCK : (k + 1) * BLOCK] = value
            if k < i:
                for piece, value in enumerate(split(block.T, PIECES)):
                    moments[piece, k * BLOCK : (k + 1) * BLOCK, i * BLOCK : (i + 1) * BLOCK] = value
    solved[...] = jnp.zeros_like(solved)
    lows[...] = jnp.zeros_like(lows)

    def gram_row(at):
        held = left[at, :]
        row = sum(dot(held, moments[i]) for i in range(PIECES))
        return sum(dot(piece, left[...], True) for piece in split(row, PIECES))

    now[:, :chi] = gram_row(pl.ds(0, BLOCK))
    now[:, chi:] = left[:BLOCK, :].astype(jnp.float32)

    def body(j, _):
        here = pl.ds(pl.multiple_of(j * BLOCK, BLOCK), BLOCK)
        after = pl.ds(pl.multiple_of(jnp.minimum(j + 1, n - 1) * BLOCK, BLOCK), BLOCK)
        inverse = split(inverse_factor(now[:, here]), PIECES)
        multiples = [lows[i, after, :] for i in range(PIECES)]
        next_gram = gram_row(after) - product(multiples, [solved[i, :, :chi] for i in range(PIECES)])
        next_left = left[after, :].astype(jnp.float32) - product(
            multiples, [solved[i, :, chi:] for i in range(PIECES)]
        )
        row = now[...]
        row_gram = product(inverse, split(row[:, :chi], PIECES))
        row_left = product(inverse, split(row[:, chi:], PIECES))
        row_gram_pieces, row_left_pieces = split(row_gram, PIECES), split(row_left, PIECES)
        for i in range(PIECES):
            solved[i, here, :chi] = row_gram_pieces[i]
            solved[i, here, chi:] = row_left_pieces[i]
        low[:, here] = row_gram.T
        for i, piece in enumerate(split(low[:, here], PIECES)):
            lows[i, :, here] = piece
        multiples = [lows[i, after, here] for i in range(PIECES)]
        now[:, :chi] = next_gram - product(multiples, row_gram_pieces)
        now[:, chi:] = next_left - product(multiples, row_left_pieces)
        return 0

    lax.fori_loop(0, n, body, 0)
    count = factor_ref.shape[0]
    first = place_ref[0] * count
    mine = pl.ds(pl.multiple_of(first, 16), count)
    row_id = lax.broadcasted_iota(jnp.int32, (count, chi), 0) + first
    column_id = lax.broadcasted_iota(jnp.int32, (count, chi), 1)
    factor_ref[...] = jnp.where(column_id <= row_id, low[mine, :] * (1.0 / scale), 0.0)
    weights_ref[...] = solved[0, mine, chi:]


def factorize(mine, other, left_blocks, places, chi, chunk, scale):
    rows = left_blocks[0].shape[0]
    whole = pl.BlockSpec(memory_space=pltpu.VMEM)
    return pl.pallas_call(
        functools.partial(factor_kernel, scale, chunk),
        out_shape=[
            jax.ShapeDtypeStruct((rows, chi), jnp.float32),
            jax.ShapeDtypeStruct((rows, chi), jnp.bfloat16),
        ],
        in_specs=[pl.BlockSpec(memory_space=pltpu.SMEM)] + [whole] * (2 + len(left_blocks)),
        out_specs=[whole, whole],
        scratch_shapes=[
            pltpu.VMEM((chi, chi), jnp.bfloat16),
            pltpu.VMEM((chi // 2, chi + BLOCK), jnp.float32),
            pltpu.VMEM((PIECES, chi, chi), jnp.bfloat16),
            pltpu.VMEM((BLOCK, 2 * chi), jnp.float32),
            pltpu.VMEM((PIECES, chi, 2 * chi), jnp.bfloat16),
            pltpu.VMEM((PIECES, chi, chi), jnp.bfloat16),
            pltpu.VMEM((chi, chi), jnp.float32),
        ],
        compiler_params=pltpu.CompilerParams(vmem_limit_bytes=52 * 2**20),
        cost_estimate=pl.CostEstimate(flops=20 * 2 * chi**3, bytes_accessed=16 * chi**2, transcendentals=0),
    )(places, mine, other, *left_blocks)


def site_kernel(scale, place_ref, weights_ref, own_ref, *refs):
    *got_refs, out_ref = refs
    depth = own_ref.shape[1]
    mine = weights_ref[:, pl.ds(pl.multiple_of(place_ref[1] * depth, depth), depth)]
    other = weights_ref[:, pl.ds(pl.multiple_of((place_ref[1] ^ 1) * depth, depth), depth)]
    for slot, got_ref in enumerate(got_refs):
        count = got_ref.shape[0]
        for i in range(count):
            e = (place_ref[0] ^ slot) * count + i
            out_ref[e] = scale * (dot(mine, own_ref[e]) + dot(other, got_ref[i].astype(jnp.bfloat16)))


def make_site(weights, own, got, places, scale):
    rows, chi = weights.shape
    east, _, right = own.shape
    whole = pl.BlockSpec(memory_space=pltpu.VMEM)
    return pl.pallas_call(
        functools.partial(site_kernel, scale),
        out_shape=jax.ShapeDtypeStruct((east, rows, right), jnp.float32),
        in_specs=[pl.BlockSpec(memory_space=pltpu.SMEM)] + [whole] * (2 + len(got)),
        out_specs=whole,
        compiler_params=pltpu.CompilerParams(vmem_limit_bytes=32 * 2**20),
        cost_estimate=pl.CostEstimate(flops=2 * rows * chi * east * right, bytes_accessed=8 * east * chi * right, transcendentals=0),
    )(places, weights, own, *got)


def shards(sizes, left_factor, boundary_site, double_layer):
    lb, rb, rep = sizes["lb"], sizes["rb"], sizes["rep"]
    l, p = lax.axis_index("lb"), lax.axis_index("rep")
    depth, phys, right = boundary_site.shape
    east = phys // rep
    chi = depth * rep
    scale = math.sqrt(phys * rb * right)
    steps = {axis: steps_of(axis, size) for axis, size in sizes.items()}
    core, across = steps["lb"][:1], steps["lb"][1:]

    left_blocks = gather_slots([(0, left_factor.astype(jnp.float32))], steps["rep"])
    left_blocks = [piece for _, piece in sorted(left_blocks, key=lambda pair: pair[0])]
    left_blocks = [gather_slots([(0, piece)], across[::-1] + core) for piece in left_blocks]
    left_blocks = [sorted(pieces, key=lambda pair: pair[0]) for pieces in left_blocks]
    left_blocks = [left_blocks[q][s][1] for s in range(lb) for q in range(rep)]

    east_part, right_parts = max(1, east // lb), max(1, lb // east)
    right_part = right // right_parts
    east_at, right_at = (l // right_parts) * east_part, (l % right_parts) * right_part
    legs = [(p ^ s) * east + east_at + i for s in range(1, rep) for i in range(east_part)]
    sent = absorb(boundary_site, double_layer, legs, [east_part] * (rep - 1), jnp.float32)
    if right_parts > 1:
        sent = [lax.dynamic_slice_in_dim(piece, right_at, right_part, 2) for piece in sent]
    got = [swap(piece, ("rep", rep, s)) for s, piece in zip(range(1, rep), sent)]
    (own,) = absorb(boundary_site, double_layer, [p * east + i for i in range(east)], [east], jnp.bfloat16)
    share = lax.dynamic_slice(own, (east_at, 0, right_at), (east_part, depth, right_part))
    got, left_blocks = lax.optimization_barrier((got, left_blocks))

    near = across[:1] + steps["rep"][:1] + steps["rb"][:1]
    far = [step for step in across + steps["rep"] + steps["rb"] if step not in near]
    orders = [near[i:] + near[:i] for i in range(3)]
    cut = cut_steps(near, chi // 4)
    chunk = (chi // 4) >> cut
    bits = [position(core + order[:cut]) for order in orders]
    places = jnp.stack([p] + bits).astype(jnp.int32)
    kept, sent = moment([share] + got, places, chi, chunk)
    whole = kept + swap(sent, core[0])
    third = whole.shape[1] // 3
    parts = [whole[:, i * third : (i + 1) * third] for i in range(3)]
    parts = reduce_parts(parts, orders, cut)
    whole = jnp.concatenate(parts, 1)
    pairs = [[piece, swap(piece, core[0])] for piece in got]
    whole, pairs = lax.optimization_barrier((whole, pairs))
    for step in far:
        whole = whole + swap(whole, step)
    parts = [whole[:, i * third : (i + 1) * third] for i in range(3)]
    parts = gather_parts(parts, orders, cut)
    whole = jnp.concatenate(parts, 1)
    other = swap(whole, core[0])

    pairs, whole = lax.optimization_barrier((pairs, whole))
    got = [gather_slots(list(zip(range(2), pair)), across[::-1]) for pair in pairs]

    places = jnp.stack([l, p] + bits).astype(jnp.int32)
    factor, weights = factorize(whole, other, left_blocks, places, chi, chunk, scale)
    if rep == 2 and right_parts == 1:
        pieces = [piece for _, piece in sorted(got[0], key=lambda pair: pair[0])]
        site_q = make_site(weights, own, pieces, places, scale)
    else:
        nothing = double_layer[0, 0] * 0.0
        site = jnp.zeros((east, chi, right), jnp.bfloat16)
        site = lax.dynamic_update_slice(site, own, (0, p * depth, 0))
        for s, pieces in zip(range(1, rep), got):
            for slot, piece in pieces:
                owner = l ^ slot
                at = ((owner // right_parts) * east_part, (p ^ s) * depth, (owner % right_parts) * right_part)
                site = lax.dynamic_update_slice(site, (piece + nothing).astype(jnp.bfloat16), at)
        site_q = jnp.einsum("ik,ekr->eir", weights, site, preferred_element_type=jnp.float32) * scale
    return (site_q, factor)


def solution(mesh):
    return jax.shard_map(
        functools.partial(shards, dict(mesh.shape)),
        mesh=mesh,
        in_specs=(P("lb", "rep"), P("rep", None, "rb"), P()),
        out_specs=(P("rep", "lb", "rb"), P("lb", None)),
        check_vma=False,
    )
```

```python
import functools
import math

import jax
import jax.numpy as jnp
from jax import lax
from jax.experimental import pallas as pl
from jax.experimental.pallas import tpu as pltpu
from jax.sharding import PartitionSpec as P

BLOCK = 128


def swap(array, step):
    axis, size, distance = step
    return lax.ppermute(array, axis, [(i, i ^ distance) for i in range(size)])


def steps_of(axis, size):
    return [(axis, size, 1 << i) for i in range(size.bit_length() - 1)]


def gather_slots(held, steps):
    for step in steps:
        held = held + [(slot ^ step[2], swap(piece, step)) for slot, piece in held]
    return held


def cut_steps(steps, rows):
    count = 0
    while count < len(steps) and rows % 16 == 0:
        rows, count = rows // 2, count + 1
    return count


def position(steps):
    place = jnp.int32(0)
    for axis, _, distance in steps:
        place = place * 2 + lax.rem(lax.div(lax.axis_index(axis), distance), 2)
    return place


def swap_parts(parts, steps):
    parts = lax.optimization_barrier(parts)
    return lax.optimization_barrier([swap(part, step) for part, step in zip(parts, steps)])


def reduce_parts(parts, orders, cuts):
    for at in range(cuts):
        half = parts[0].shape[0] // 2
        got = swap_parts([part[half:] for part in parts], [order[at] for order in orders])
        parts = [part[:half] + other for part, other in zip(parts, got)]
    return parts


def gather_parts(parts, orders, cuts):
    for at in range(cuts - 1, -1, -1):
        got = swap_parts(parts, [order[at] for order in orders])
        parts = [jnp.concatenate([part, other], 0) for part, other in zip(parts, got)]
    return parts


HIGHEST = lax.Precision.HIGHEST
GROUP = 16
PIECES = 2


def dot(a, b, transposed=False):
    dims = (((1,), (1 if transposed else 0,)), ((), ()))
    return lax.dot_general(a, b, dims, preferred_element_type=jnp.float32)


def absorb_kernel(east_parts, legs_ref, site_ref, double_ref, *out_refs):
    phys = double_ref.shape[0]
    legs = sum(east_parts)
    row = lax.broadcasted_iota(jnp.int32, (legs * GROUP, GROUP * phys), 0)
    column = lax.broadcasted_iota(jnp.int32, (legs * GROUP, GROUP * phys), 1)
    chosen = jnp.concatenate(
        [
            jnp.where(lax.broadcasted_iota(jnp.int32, (GROUP, phys), 1) == legs_ref[i], 1.0, 0.0)
            for i in range(legs)
        ],
        0,
    )
    values = lax.dot_general(
        chosen, double_ref[...], (((1,), (1,)), ((), ())), precision=HIGHEST, preferred_element_type=jnp.float32
    )
    spread = jnp.where(
        lax.broadcasted_iota(jnp.int32, (phys, GROUP * phys), 0)
        == lax.rem(lax.broadcasted_iota(jnp.int32, (phys, GROUP * phys), 1), phys),
        1.0,
        0.0,
    )
    values = jnp.dot(values, spread, precision=HIGHEST, preferred_element_type=jnp.float32)
    both = jnp.concatenate(split(jnp.where(lax.rem(row, GROUP) == lax.div(column, phys), values, 0.0), 2), 0)
    groups = site_ref.shape[0] // (GROUP * phys)
    for g in range(groups):
        rows = site_ref[g * GROUP * phys : (g + 1) * GROUP * phys, :]
        absorbed = dot(both, rows)
        absorbed = (absorbed[: legs * GROUP] + absorbed[legs * GROUP :]).astype(jnp.bfloat16)
        leg = 0
        for out_ref, count in zip(out_refs, east_parts):
            for e in range(count):
                piece = absorbed[(leg + e) * GROUP : (leg + e + 1) * GROUP]
                out_ref[e, g * GROUP : (g + 1) * GROUP, :] = piece.astype(out_ref.dtype)
            leg += count


def absorb(boundary_site, double_layer, legs, east_parts, dtype):
    legs = jnp.stack(legs).astype(jnp.int32)
    depth, phys, right = boundary_site.shape
    tiles = max(1, depth // 128)
    tile = depth // tiles
    out_shape, out_specs = [], []
    for count in east_parts:
        out_shape.append(jax.ShapeDtypeStruct((count, depth, right), dtype))
        out_specs.append(pl.BlockSpec((count, tile, right), lambda t: (0, t, 0)))
    return pl.pallas_call(
        functools.partial(absorb_kernel, east_parts),
        grid=(tiles,),
        out_shape=out_shape,
        in_specs=[
            pl.BlockSpec(memory_space=pltpu.SMEM),
            pl.BlockSpec((tile * phys, right), lambda t: (t, 0)),
            pl.BlockSpec(memory_space=pltpu.VMEM),
        ],
        out_specs=out_specs,
        compiler_params=pltpu.CompilerParams(vmem_limit_bytes=32 * 2**20),
        cost_estimate=pl.CostEstimate(
            flops=2 * 2 * depth * right * GROUP * phys * sum(east_parts), bytes_accessed=8 * depth * right * phys, transcendentals=0
        ),
    )(legs, boundary_site.reshape(depth * phys, right), double_layer)


def moment_kernel(chi, chunk, third, place_ref, *refs):
    *block_refs, kept_ref, sent_ref, columns, packed = refs
    rep = len(block_refs)
    count, depth, width = block_refs[0].shape
    n = chi // BLOCK
    for i, block_ref in enumerate(block_refs):
        at = pl.ds(pl.multiple_of((place_ref[0] ^ i) * depth, depth), depth)
        for e in range(count):
            columns[at, e * width : (e + 1) * width] = block_ref[e].astype(jnp.bfloat16)
    for i in range(n):
        group, lo = (i, 0) if i < n // 2 else (n - 1 - i, (n - i) * BLOCK)
        packed[group * BLOCK : (group + 1) * BLOCK, lo : lo + (i + 1) * BLOCK] = dot(
            columns[i * BLOCK : (i + 1) * BLOCK], columns[: (i + 1) * BLOCK], True
        )
    half = kept_ref.shape[0]
    for part in range(3):
        lanes = slice(part * third, (part + 1) * third)
        for t in range(packed.shape[0] // chunk):
            rows = pl.ds(pl.multiple_of((place_ref[1 + part] ^ t) * chunk, 8), chunk)
            at = t * chunk
            to_ref = kept_ref if at < half else sent_ref
            to_ref[at % half : at % half + chunk, lanes] = packed[rows, lanes]


def moment(blocks, places, chi, chunk):
    rows, width = chi // 2, chi + BLOCK
    count, _, right = blocks[0].shape
    whole = pl.BlockSpec(memory_space=pltpu.VMEM)
    return pl.pallas_call(
        functools.partial(moment_kernel, chi, chunk, width // 3),
        out_shape=[jax.ShapeDtypeStruct((rows // 2, width), jnp.float32)] * 2,
        in_specs=[pl.BlockSpec(memory_space=pltpu.SMEM)] + [whole] * len(blocks),
        out_specs=[whole, whole],
        scratch_shapes=[pltpu.VMEM((chi, count * right), jnp.bfloat16), pltpu.VMEM((rows, width), jnp.float32)],
        compiler_params=pltpu.CompilerParams(vmem_limit_bytes=32 * 2**20),
        cost_estimate=pl.CostEstimate(flops=chi * chi * count * right, bytes_accessed=6 * chi * chi, transcendentals=0),
    )(places, *blocks)


def sub(x, s):
    return jnp.broadcast_to(x[s : s + 1, :], x.shape)


def lane(x, k):
    return jnp.broadcast_to(x[:, k : k + 1], x.shape)


def inverse_factor(block, tasks):
    n, wide = BLOCK // 8, 8
    rows = [block[8 * b : 8 * b + 8] for b in range(n)]
    sub_id = lax.broadcasted_iota(jnp.int32, (8, BLOCK), 0)
    lane_id = lax.broadcasted_iota(jnp.int32, (8, BLOCK), 1)
    pivots = []
    head = [lane(rows[0], c) for c in range(wide)]
    for b in range(n):
        k = wide * b
        cols = [[head[c]] + [lane(rows[i], k + c) for i in range(b + 1, n)] for c in range(wide)]
        if b + 1 < n:
            head = [lane(rows[b + 1], k + wide + c) for c in range(wide)]
        inside = (lane_id >= k) & (lane_id < k + wide)
        for i in range(b, n):
            rows[i] = jnp.where(inside, 0.0, rows[i])
        pivot = jnp.ones((8, BLOCK), jnp.float32)
        for c in range(wide):
            d = sub(cols[c][0], c)
            inverse = 1.0 / d
            pivot = jnp.where(sub_id == c, d, pivot)
            for c2 in range(c + 1, wide):
                m = sub(cols[c][0], c2) * inverse
                for i in range(n - b):
                    cols[c2][i] = cols[c2][i] - cols[c][i] * m
            factors = [cols[c][i] * inverse for i in range(n - b)]
            if b + 1 < n:
                for c2 in range(wide):
                    head[c2] = head[c2] - factors[1] * sub(cols[c][1], c2)
            factors[0] = jnp.where(sub_id > c, factors[0], 0.0)
            row = jnp.where(lane_id == k + c, 1.0, sub(rows[b], c))
            for i in range(n - b):
                rows[b + i] = rows[b + i] - factors[i] * row
        pivots.append(pivot)
        for task in tasks[len(tasks) * b // n : len(tasks) * (b + 1) // n]:
            task()
    out = []
    for b in range(n):
        diagonal = sub_id + 8 * b
        row = jnp.where(lane_id < diagonal, rows[b], jnp.where(lane_id == diagonal, 1.0, 0.0))
        out.append(row * lax.rsqrt(pivots[b]))
    return jnp.concatenate(out, 0)


def split(x, pieces):
    out = []
    for i in range(pieces):
        out.append(x.astype(jnp.bfloat16))
        if i + 1 < pieces:
            x = x - out[-1].astype(jnp.float32)
    return out


def product(a, b):
    rows = a[0].shape[0]
    both = dot(jnp.concatenate(a, 0), b[0])
    return both[:rows] + both[rows:] + dot(a[0], b[1])


def left_kernel(place_ref, *refs):
    *left_refs, left = refs
    rows, width = left_refs[0].shape
    across = left.shape[1] // width
    for i, left_ref in enumerate(left_refs):
        row_at = pl.multiple_of((place_ref[0] ^ (i // across)) * rows, 16)
        column_at = pl.multiple_of((place_ref[1] ^ (i % across)) * width, 128)
        left[pl.ds(row_at, rows), pl.ds(column_at, width)] = left_ref[...].astype(jnp.bfloat16)


def assemble_left(blocks, places, chi):
    whole = pl.BlockSpec(memory_space=pltpu.VMEM)
    return pl.pallas_call(
        left_kernel,
        out_shape=jax.ShapeDtypeStruct((chi, chi), jnp.bfloat16),
        in_specs=[pl.BlockSpec(memory_space=pltpu.SMEM)] + [whole] * len(blocks),
        out_specs=whole,
        compiler_params=pltpu.CompilerParams(vmem_limit_bytes=24 * 2**20),
        cost_estimate=pl.CostEstimate(flops=0, bytes_accessed=6 * chi * chi, transcendentals=0),
    )(places, *blocks)


def factor_kernel(scale, chunk, place_ref, mine_ref, other_ref, left, *refs):
    factor_ref, weights_ref, packed, moments, now, later, product_rows, solved, lows, low = refs
    chi = left.shape[0]
    n = chi // BLOCK
    half, third = mine_ref.shape[0], mine_ref.shape[1] // 3
    for part in range(3):
        lanes = slice(part * third, (part + 1) * third)
        for t in range(2 * half // chunk):
            at = pl.ds(pl.multiple_of((place_ref[2 + part] ^ t) * chunk, 8), chunk)
            from_ref = mine_ref if t * chunk < half else other_ref
            packed[at, lanes] = from_ref[t * chunk % half : t * chunk % half + chunk, lanes]
    for i in range(n):
        group, lo = (i, 0) if i < n // 2 else (n - 1 - i, (n - i) * BLOCK)
        for k in range(i + 1):
            block = packed[group * BLOCK : (group + 1) * BLOCK, lo + k * BLOCK : lo + (k + 1) * BLOCK]
            for piece, value in enumerate(split(block, PIECES)):
                moments[piece, i * BLOCK : (i + 1) * BLOCK, k * BLOCK : (k + 1) * BLOCK] = value
            if k < i:
                for piece, value in enumerate(split(block.T, PIECES)):
                    moments[piece, k * BLOCK : (k + 1) * BLOCK, i * BLOCK : (i + 1) * BLOCK] = value

    wide = 2 * BLOCK

    def chunks(first):
        edges = [first] + [c for c in range(0, 2 * chi + 1, wide) if c > first]
        return [slice(c, d) for c, d in zip(edges, edges[1:])]

    def left_times_moments(lo, hi, columns):
        row = sum(dot(left[lo:hi], moments[i, :, columns]) for i in range(PIECES))
        for i, piece in enumerate(split(row, PIECES)):
            product_rows[i * wide : i * wide + hi - lo, columns] = piece

    def fresh(to, lo, hi, columns):
        if columns.start >= chi:
            to[: hi - lo, columns] = left[lo:hi, columns.start - chi : columns.stop - chi].astype(jnp.float32)
        else:
            both = dot(product_rows[...], left[columns], True)
            to[: hi - lo, columns] = both[: hi - lo] + both[wide : wide + hi - lo]

    def solve(at, inverse, rows, columns):
        values = product(inverse, split(now[rows, columns], PIECES))
        for i, piece in enumerate(split(values, PIECES)):
            solved[i, at, columns] = piece
        if columns.start < chi:
            column = values.T
            low[columns, at] = column
            for i, piece in enumerate(split(column, PIECES)):
                lows[i, columns, at] = piece

    def taken(rows, before, columns):
        return product(
            [lows[i, rows, before] for i in range(PIECES)], [solved[i, before, columns] for i in range(PIECES)]
        )

    def less(to, at, source, rows, before, columns):
        to[at, columns] = source[at, columns] - taken(rows, before, columns)

    every = slice(0, wide)
    top, bottom = slice(0, BLOCK), slice(BLOCK, wide)
    bind = functools.partial
    columns_of_moments = [slice(c, c + wide) for c in range(0, chi, wide)]
    for columns in columns_of_moments:
        left_times_moments(0, wide, columns)
    fresh(now, 0, wide, every)
    tasks = [bind(fresh, now, 0, wide, columns) for columns in chunks(wide)]
    for lo in range(0, chi, wide):
        mid, hi, end = lo + BLOCK, lo + wide, lo + 2 * wide
        pair = slice(hi, end)
        if hi < chi:
            tasks += [bind(left_times_moments, hi, end, columns) for columns in columns_of_moments]
            tasks += [bind(fresh, later, hi, end, columns) for columns in chunks(hi)]
        inverse = split(inverse_factor(now[top, lo:mid], tasks), PIECES)

        at = slice(lo, mid)
        solve(at, inverse, top, slice(mid, hi))
        block = now[bottom, mid:hi] - taken(slice(mid, hi), at, slice(mid, hi))
        tasks = []
        for columns in [slice(lo, mid)] + chunks(hi):
            tasks.append(bind(solve, at, inverse, top, columns))
            if columns.start >= hi:
                tasks.append(bind(less, now, bottom, now, slice(mid, hi), at, columns))
        if hi < chi:
            tasks += [bind(less, later, every, later, pair, slice(0, mid), columns) for columns in chunks(hi)]
        now[bottom, mid:hi] = block
        inverse = split(inverse_factor(block, tasks), PIECES)

        at = slice(mid, hi)
        tasks = [bind(solve, at, inverse, bottom, slice(mid, hi))]
        if hi < chi:
            first = slice(hi, hi + BLOCK)
            solve(at, inverse, bottom, first)
            now[top, first] = later[top, first] - taken(first, at, first)
            second = slice(hi + BLOCK, end)
            tasks.append(bind(solve, at, inverse, bottom, second))
            tasks.append(bind(less, now, bottom, later, slice(hi + BLOCK, end), at, second))
            tasks.append(bind(less, now, top, later, first, at, second))
            for columns in chunks(end):
                tasks.append(bind(solve, at, inverse, bottom, columns))
                tasks.append(bind(less, now, every, later, pair, at, columns))
        else:
            tasks += [bind(solve, at, inverse, bottom, columns) for columns in chunks(hi)]
    for task in tasks:
        task()

    count = factor_ref.shape[0]
    first = place_ref[0] * count
    mine = pl.ds(pl.multiple_of(first, 16), count)
    row_id = lax.broadcasted_iota(jnp.int32, (count, chi), 0) + first
    column_id = lax.broadcasted_iota(jnp.int32, (count, chi), 1)
    factor_ref[...] = jnp.where(column_id <= row_id, low[mine, :] * (1.0 / scale), 0.0)
    weights_ref[...] = solved[0, mine, chi:]


def factorize(mine, other, left, places, rows, chunk, scale):
    chi = left.shape[0]
    whole = pl.BlockSpec(memory_space=pltpu.VMEM)
    return pl.pallas_call(
        functools.partial(factor_kernel, scale, chunk),
        out_shape=[
            jax.ShapeDtypeStruct((rows, chi), jnp.float32),
            jax.ShapeDtypeStruct((rows, chi), jnp.bfloat16),
        ],
        in_specs=[pl.BlockSpec(memory_space=pltpu.SMEM)] + [whole] * 3,
        out_specs=[whole, whole],
        scratch_shapes=[
            pltpu.VMEM((chi // 2, chi + BLOCK), jnp.float32),
            pltpu.VMEM((PIECES, chi, chi), jnp.bfloat16),
            pltpu.VMEM((2 * BLOCK, 2 * chi), jnp.float32),
            pltpu.VMEM((2 * BLOCK, 2 * chi), jnp.float32),
            pltpu.VMEM((PIECES * 2 * BLOCK, chi), jnp.bfloat16),
            pltpu.VMEM((PIECES, chi, 2 * chi), jnp.bfloat16),
            pltpu.VMEM((PIECES, chi, chi), jnp.bfloat16),
            pltpu.VMEM((chi, chi), jnp.float32),
        ],
        compiler_params=pltpu.CompilerParams(vmem_limit_bytes=52 * 2**20),
        cost_estimate=pl.CostEstimate(flops=20 * 2 * chi**3, bytes_accessed=16 * chi**2, transcendentals=0),
    )(places, mine, other, left)


def site_kernel(scale, place_ref, weights_ref, own_ref, *refs):
    *got_refs, out_ref = refs
    depth = own_ref.shape[1]
    mine = weights_ref[:, pl.ds(pl.multiple_of(place_ref[1] * depth, depth), depth)]
    other = weights_ref[:, pl.ds(pl.multiple_of((place_ref[1] ^ 1) * depth, depth), depth)]
    for slot, got_ref in enumerate(got_refs):
        count = got_ref.shape[0]
        for i in range(count):
            e = (place_ref[0] ^ slot) * count + i
            out_ref[e] = scale * (dot(mine, own_ref[e]) + dot(other, got_ref[i].astype(jnp.bfloat16)))


def make_site(weights, own, got, places, scale):
    rows, chi = weights.shape
    east, _, right = own.shape
    whole = pl.BlockSpec(memory_space=pltpu.VMEM)
    return pl.pallas_call(
        functools.partial(site_kernel, scale),
        out_shape=jax.ShapeDtypeStruct((east, rows, right), jnp.float32),
        in_specs=[pl.BlockSpec(memory_space=pltpu.SMEM)] + [whole] * (2 + len(got)),
        out_specs=whole,
        compiler_params=pltpu.CompilerParams(vmem_limit_bytes=32 * 2**20),
        cost_estimate=pl.CostEstimate(flops=2 * rows * chi * east * right, bytes_accessed=8 * east * chi * right, transcendentals=0),
    )(places, weights, own, *got)


def shards(sizes, left_factor, boundary_site, double_layer):
    lb, rb, rep = sizes["lb"], sizes["rb"], sizes["rep"]
    l, p = lax.axis_index("lb"), lax.axis_index("rep")
    depth, phys, right = boundary_site.shape
    east = phys // rep
    chi = depth * rep
    row_count = left_factor.shape[0]
    scale = math.sqrt(phys * rb * right)
    steps = {axis: steps_of(axis, size) for axis, size in sizes.items()}
    core, across = steps["lb"][:1], steps["lb"][1:]

    left_blocks = gather_slots([(0, left_factor.astype(jnp.float32))], steps["rep"])
    left_blocks = [piece for _, piece in sorted(left_blocks, key=lambda pair: pair[0])]
    left_blocks = [gather_slots([(0, piece)], across[::-1] + core) for piece in left_blocks]
    left_blocks = [sorted(pieces, key=lambda pair: pair[0]) for pieces in left_blocks]
    left_blocks = [left_blocks[q][s][1] for s in range(lb) for q in range(rep)]

    east_part, right_parts = max(1, east // lb), max(1, lb // east)
    right_part = right // right_parts
    east_at, right_at = (l // right_parts) * east_part, (l % right_parts) * right_part
    legs = [(p ^ s) * east + east_at + i for s in range(1, rep) for i in range(east_part)]
    sent = absorb(boundary_site, double_layer, legs, [east_part] * (rep - 1), jnp.float32)
    if right_parts > 1:
        sent = [lax.dynamic_slice_in_dim(piece, right_at, right_part, 2) for piece in sent]
    got = [swap(piece, ("rep", rep, s)) for s, piece in zip(range(1, rep), sent)]
    (own,) = absorb(boundary_site, double_layer, [p * east + i for i in range(east)], [east], jnp.bfloat16)
    share = lax.dynamic_slice(own, (east_at, 0, right_at), (east_part, depth, right_part))
    got, left_blocks = lax.optimization_barrier((got, left_blocks))

    near = across[:1] + steps["rep"][:1] + steps["rb"][:1]
    far = [step for step in across + steps["rep"] + steps["rb"] if step not in near]
    orders = [near[i:] + near[:i] for i in range(3)]
    cut = cut_steps(near, chi // 4)
    chunk = (chi // 4) >> cut
    bits = [position(core + order[:cut]) for order in orders]
    places = jnp.stack([p] + bits).astype(jnp.int32)
    kept, sent = moment([share] + got, places, chi, chunk)
    whole = kept + swap(sent, core[0])
    third = whole.shape[1] // 3
    parts = [whole[:, i * third : (i + 1) * third] for i in range(3)]
    parts = reduce_parts(parts, orders, cut)
    whole = jnp.concatenate(parts, 1)
    pairs = [[piece, swap(piece, core[0])] for piece in got]
    left = assemble_left(left_blocks, jnp.stack([l, p]).astype(jnp.int32), chi)
    whole, pairs, left = lax.optimization_barrier((whole, pairs, left))
    for step in far:
        whole = whole + swap(whole, step)
    parts = [whole[:, i * third : (i + 1) * third] for i in range(3)]
    parts = gather_parts(parts, orders, cut)
    whole = jnp.concatenate(parts, 1)
    other = swap(whole, core[0])

    pairs, whole = lax.optimization_barrier((pairs, whole))
    got = [gather_slots(list(zip(range(2), pair)), across[::-1]) for pair in pairs]

    places = jnp.stack([l, p] + bits).astype(jnp.int32)
    factor, weights = factorize(whole, other, left, places, row_count, chunk, scale)
    if rep == 2 and right_parts == 1:
        pieces = [piece for _, piece in sorted(got[0], key=lambda pair: pair[0])]
        site_q = make_site(weights, own, pieces, places, scale)
    else:
        nothing = double_layer[0, 0] * 0.0
        site = jnp.zeros((east, chi, right), jnp.bfloat16)
        site = lax.dynamic_update_slice(site, own, (0, p * depth, 0))
        for s, pieces in zip(range(1, rep), got):
            for slot, piece in pieces:
                owner = l ^ slot
                at = ((owner // right_parts) * east_part, (p ^ s) * depth, (owner % right_parts) * right_part)
                site = lax.dynamic_update_slice(site, (piece + nothing).astype(jnp.bfloat16), at)
        site_q = jnp.einsum("ik,ekr->eir", weights, site, preferred_element_type=jnp.float32) * scale
    return (site_q, factor)


def solution(mesh):
    return jax.shard_map(
        functools.partial(shards, dict(mesh.shape)),
        mesh=mesh,
        in_specs=(P("lb", "rep"), P("rep", None, "rb"), P()),
        out_specs=(P("rep", "lb", "rb"), P("lb", None)),
        check_vma=False,
    )
```

```python
import functools
import math

import jax
import jax.numpy as jnp
from jax import lax
from jax.experimental import pallas as pl
from jax.experimental.pallas import tpu as pltpu
from jax.sharding import PartitionSpec as P

BLOCK = 128


def swap(array, step):
    axis, size, distance = step
    return lax.ppermute(array, axis, [(i, i ^ distance) for i in range(size)])


def steps_of(axis, size):
    return [(axis, size, 1 << i) for i in range(size.bit_length() - 1)]


def gather_slots(held, steps):
    for step in steps:
        held = held + [(slot ^ step[2], swap(piece, step)) for slot, piece in held]
    return held


def cut_steps(steps, rows):
    count = 0
    while count < len(steps) and rows % 16 == 0:
        rows, count = rows // 2, count + 1
    return count


def position(steps):
    place = jnp.int32(0)
    for axis, _, distance in steps:
        place = place * 2 + lax.rem(lax.div(lax.axis_index(axis), distance), 2)
    return place


def swap_parts(parts, steps):
    parts = lax.optimization_barrier(parts)
    return lax.optimization_barrier([swap(part, step) for part, step in zip(parts, steps)])


def reduce_parts(parts, orders, cuts):
    for at in range(cuts):
        half = parts[0].shape[0] // 2
        got = swap_parts([part[half:] for part in parts], [order[at] for order in orders])
        parts = [part[:half] + other for part, other in zip(parts, got)]
    return parts


def gather_parts(parts, orders, cuts):
    for at in range(cuts - 1, -1, -1):
        got = swap_parts(parts, [order[at] for order in orders])
        parts = [jnp.concatenate([part, other], 0) for part, other in zip(parts, got)]
    return parts


HIGHEST = lax.Precision.HIGHEST
GROUP = 16
PIECES = 2


def dot(a, b, transposed=False):
    dims = (((1,), (1 if transposed else 0,)), ((), ()))
    return lax.dot_general(a, b, dims, preferred_element_type=jnp.float32)


def absorb_kernel(east_parts, legs_ref, site_ref, double_ref, *out_refs):
    phys = double_ref.shape[0]
    legs = sum(east_parts)
    row = lax.broadcasted_iota(jnp.int32, (legs * GROUP, GROUP * phys), 0)
    column = lax.broadcasted_iota(jnp.int32, (legs * GROUP, GROUP * phys), 1)
    chosen = jnp.concatenate(
        [
            jnp.where(lax.broadcasted_iota(jnp.int32, (GROUP, phys), 1) == legs_ref[i], 1.0, 0.0)
            for i in range(legs)
        ],
        0,
    )
    values = lax.dot_general(
        chosen, double_ref[...], (((1,), (1,)), ((), ())), precision=HIGHEST, preferred_element_type=jnp.float32
    )
    spread = jnp.where(
        lax.broadcasted_iota(jnp.int32, (phys, GROUP * phys), 0)
        == lax.rem(lax.broadcasted_iota(jnp.int32, (phys, GROUP * phys), 1), phys),
        1.0,
        0.0,
    )
    values = jnp.dot(values, spread, precision=HIGHEST, preferred_element_type=jnp.float32)
    both = jnp.concatenate(split(jnp.where(lax.rem(row, GROUP) == lax.div(column, phys), values, 0.0), 2), 0)
    groups = site_ref.shape[0] // (GROUP * phys)
    for g in range(groups):
        rows = site_ref[g * GROUP * phys : (g + 1) * GROUP * phys, :]
        absorbed = dot(both, rows)
        absorbed = (absorbed[: legs * GROUP] + absorbed[legs * GROUP :]).astype(jnp.bfloat16)
        leg = 0
        for out_ref, count in zip(out_refs, east_parts):
            for e in range(count):
                piece = absorbed[(leg + e) * GROUP : (leg + e + 1) * GROUP]
                out_ref[e, g * GROUP : (g + 1) * GROUP, :] = piece.astype(out_ref.dtype)
            leg += count


def absorb(boundary_site, double_layer, legs, east_parts, dtype):
    legs = jnp.stack(legs).astype(jnp.int32)
    depth, phys, right = boundary_site.shape
    tiles = max(1, depth // 128)
    tile = depth // tiles
    out_shape, out_specs = [], []
    for count in east_parts:
        out_shape.append(jax.ShapeDtypeStruct((count, depth, right), dtype))
        out_specs.append(pl.BlockSpec((count, tile, right), lambda t: (0, t, 0)))
    return pl.pallas_call(
        functools.partial(absorb_kernel, east_parts),
        grid=(tiles,),
        out_shape=out_shape,
        in_specs=[
            pl.BlockSpec(memory_space=pltpu.SMEM),
            pl.BlockSpec((tile * phys, right), lambda t: (t, 0)),
            pl.BlockSpec(memory_space=pltpu.VMEM),
        ],
        out_specs=out_specs,
        compiler_params=pltpu.CompilerParams(vmem_limit_bytes=32 * 2**20),
        cost_estimate=pl.CostEstimate(
            flops=2 * 2 * depth * right * GROUP * phys * sum(east_parts), bytes_accessed=8 * depth * right * phys, transcendentals=0
        ),
    )(legs, boundary_site.reshape(depth * phys, right), double_layer)


def gram_kernel(chi, chunk, third, blocks, place_ref, *refs):
    block_refs, left_refs = refs[:blocks], refs[blocks:-7]
    kept_ref, sent_ref, left, columns, high, low, packed = refs[-7:]
    rows, width = left_refs[0].shape
    across = chi // width
    for i, left_ref in enumerate(left_refs):
        row_at = pl.multiple_of((place_ref[0] ^ (i // across)) * rows, 16)
        column_at = pl.multiple_of((place_ref[1] ^ (i % across)) * width, 128)
        left[pl.ds(row_at, rows), pl.ds(column_at, width)] = left_ref[...].astype(jnp.bfloat16)
    count, depth, width = block_refs[0].shape
    n = chi // BLOCK
    for i, block_ref in enumerate(block_refs):
        at = pl.ds(pl.multiple_of((place_ref[1] ^ i) * depth, depth), depth)
        for e in range(count):
            columns[at, e * width : (e + 1) * width] = block_ref[e].astype(jnp.bfloat16)
    for i in range(n // 2):
        at = slice(2 * i * BLOCK, 2 * (i + 1) * BLOCK)
        high[at], low[at] = split(dot(left[at], columns[...]), 2)
    for i in range(n):
        group, lo = (i, 0) if i < n // 2 else (n - 1 - i, (n - i) * BLOCK)
        at, upto = slice(i * BLOCK, (i + 1) * BLOCK), slice(0, (i + 1) * BLOCK)
        both = dot(jnp.concatenate([high[at], low[at]], 0), high[upto], True)
        packed[group * BLOCK : (group + 1) * BLOCK, lo : lo + (i + 1) * BLOCK] = (
            both[:BLOCK] + both[BLOCK:] + dot(high[at], low[upto], True)
        )
    half = kept_ref.shape[0]
    for part in range(3):
        lanes = slice(part * third, (part + 1) * third)
        for t in range(packed.shape[0] // chunk):
            rows_at = pl.ds(pl.multiple_of((place_ref[2 + part] ^ t) * chunk, 8), chunk)
            at = t * chunk
            to_ref = kept_ref if at < half else sent_ref
            to_ref[at % half : at % half + chunk, lanes] = packed[rows_at, lanes]


def gram_of_columns(blocks, left_blocks, places, chi, chunk):
    rows, width = chi // 2, chi + BLOCK
    count, _, right = blocks[0].shape
    whole = pl.BlockSpec(memory_space=pltpu.VMEM)
    return pl.pallas_call(
        functools.partial(gram_kernel, chi, chunk, width // 3, len(blocks)),
        out_shape=[jax.ShapeDtypeStruct((rows // 2, width), jnp.float32)] * 2
        + [jax.ShapeDtypeStruct((chi, chi), jnp.bfloat16)],
        in_specs=[pl.BlockSpec(memory_space=pltpu.SMEM)] + [whole] * (len(blocks) + len(left_blocks)),
        out_specs=[whole, whole, whole],
        scratch_shapes=[pltpu.VMEM((chi, count * right), jnp.bfloat16)] * 3 + [pltpu.VMEM((rows, width), jnp.float32)],
        compiler_params=pltpu.CompilerParams(vmem_limit_bytes=40 * 2**20),
        cost_estimate=pl.CostEstimate(
            flops=5 * chi * chi * count * right, bytes_accessed=12 * chi * chi, transcendentals=0
        ),
    )(places, *blocks, *left_blocks)


def sub(x, s):
    return jnp.broadcast_to(x[s : s + 1, :], x.shape)


def lane(x, k):
    return jnp.broadcast_to(x[:, k : k + 1], x.shape)


def inverse_factor(block, tasks):
    n, wide = BLOCK // 8, 8
    rows = [block[8 * b : 8 * b + 8] for b in range(n)]
    sub_id = lax.broadcasted_iota(jnp.int32, (8, BLOCK), 0)
    lane_id = lax.broadcasted_iota(jnp.int32, (8, BLOCK), 1)
    pivots = []
    head = [lane(rows[0], c) for c in range(wide)]
    for b in range(n):
        k = wide * b
        cols = [[head[c]] + [lane(rows[i], k + c) for i in range(b + 1, n)] for c in range(wide)]
        if b + 1 < n:
            head = [lane(rows[b + 1], k + wide + c) for c in range(wide)]
        inside = (lane_id >= k) & (lane_id < k + wide)
        for i in range(b, n):
            rows[i] = jnp.where(inside, 0.0, rows[i])
        pivot = jnp.ones((8, BLOCK), jnp.float32)
        for c in range(wide):
            d = sub(cols[c][0], c)
            inverse = 1.0 / d
            pivot = jnp.where(sub_id == c, d, pivot)
            for c2 in range(c + 1, wide):
                m = sub(cols[c][0], c2) * inverse
                for i in range(n - b):
                    cols[c2][i] = cols[c2][i] - cols[c][i] * m
            factors = [cols[c][i] * inverse for i in range(n - b)]
            if b + 1 < n:
                for c2 in range(wide):
                    head[c2] = head[c2] - factors[1] * sub(cols[c][1], c2)
            factors[0] = jnp.where(sub_id > c, factors[0], 0.0)
            row = jnp.where(lane_id == k + c, 1.0, sub(rows[b], c))
            for i in range(n - b):
                rows[b + i] = rows[b + i] - factors[i] * row
        pivots.append(pivot)
        for task in tasks[len(tasks) * b // n : len(tasks) * (b + 1) // n]:
            task()
    out = []
    for b in range(n):
        diagonal = sub_id + 8 * b
        row = jnp.where(lane_id < diagonal, rows[b], jnp.where(lane_id == diagonal, 1.0, 0.0))
        out.append(row * lax.rsqrt(pivots[b]))
    return jnp.concatenate(out, 0)


def split(x, pieces):
    out = []
    for i in range(pieces):
        out.append(x.astype(jnp.bfloat16))
        if i + 1 < pieces:
            x = x - out[-1].astype(jnp.float32)
    return out


def product(a, b):
    rows = a[0].shape[0]
    both = dot(jnp.concatenate(a, 0), b[0])
    return both[:rows] + both[rows:] + dot(a[0], b[1])


def factor_kernel(scale, chunk, place_ref, mine_ref, other_ref, left, *refs):
    factor_ref, weights_ref, packed, gram, now, later, inverses, solved, lows, low = refs
    chi = left.shape[0]
    n = chi // BLOCK
    half, third = mine_ref.shape[0], mine_ref.shape[1] // 3
    for part in range(3):
        lanes = slice(part * third, (part + 1) * third)
        for t in range(2 * half // chunk):
            at = pl.ds(pl.multiple_of((place_ref[2 + part] ^ t) * chunk, 8), chunk)
            from_ref = mine_ref if t * chunk < half else other_ref
            packed[at, lanes] = from_ref[t * chunk % half : t * chunk % half + chunk, lanes]
    for i in range(n):
        group, lo = (i, 0) if i < n // 2 else (n - 1 - i, (n - i) * BLOCK)
        for k in range(i + 1):
            block = packed[group * BLOCK : (group + 1) * BLOCK, lo + k * BLOCK : lo + (k + 1) * BLOCK]
            gram[i * BLOCK : (i + 1) * BLOCK, k * BLOCK : (k + 1) * BLOCK] = block
            if k < i:
                gram[k * BLOCK : (k + 1) * BLOCK, i * BLOCK : (i + 1) * BLOCK] = block.T

    wide = 2 * BLOCK
    every, top, bottom = slice(0, wide), slice(0, BLOCK), slice(BLOCK, wide)
    chunks = [slice(c, c + wide) for c in range(0, 2 * chi, wide)]
    earlier, before_last = slice(0, chi - 2 * wide), slice(0, chi - 3 * BLOCK)
    bind = functools.partial

    def span(first, size):
        return pl.ds(pl.multiple_of(first, BLOCK), size)

    def fresh(rows, columns):
        if columns.start < chi:
            return gram[rows, columns]
        return left[rows, columns.start - chi : columns.stop - chi].astype(jnp.float32)

    def solve(at, inverse, rows, columns, of_gram):
        values = product(inverse, split(now[rows, columns], PIECES))
        for i, piece in enumerate(split(values, PIECES)):
            solved[i, at, columns] = piece
        if of_gram:
            column = values.T
            low[columns, at] = column
            for i, piece in enumerate(split(column, PIECES)):
                lows[i, columns, at] = piece

    def taken(rows, before, columns):
        return product(
            [lows[i, rows, before] for i in range(PIECES)], [solved[i, before, columns] for i in range(PIECES)]
        )

    def less(to, at, source, rows, before, columns):
        to[at, columns] = source[at, columns] - taken(rows, before, columns)

    def fresh_less(rows, before, columns):
        later[:, columns] = fresh(rows, columns) - taken(rows, before, columns)

    def solve_all(at, inverse, rows):
        return [bind(solve, at, inverse, rows, columns, columns.start < chi) for columns in chunks]

    def less_all(*args):
        return [bind(less, *args, columns) for columns in chunks]

    for i in range(PIECES):
        solved[i] = jnp.zeros_like(solved[i])
        lows[i] = jnp.zeros_like(lows[i])
        inverses[i] = jnp.zeros_like(inverses[i])
    now[...] = jnp.zeros_like(now)
    for columns in chunks:
        later[:, columns] = fresh(every, columns)
    now[top, :BLOCK] = later[top, :BLOCK]

    def body(j, _):
        lo = j * wide
        last = span(lax.rem(lo + chi - BLOCK, chi), BLOCK)
        first, second, pair = span(lo, BLOCK), span(lo + BLOCK, BLOCK), span(lo, wide)
        following = jnp.minimum(lo + wide, chi - wide)
        next_pair, next_first = span(following, wide), span(following, BLOCK)

        inverse = [inverses[i] for i in range(PIECES)]
        tasks = solve_all(last, inverse, bottom) + less_all(now, every, later, pair, last)
        of_left = [columns for columns in chunks if columns.start >= chi]
        tasks += [bind(fresh_less, next_pair, earlier, columns) for columns in of_left]
        inverse = split(inverse_factor(now[top, first], tasks), PIECES)
        solve(first, inverse, top, second, True)
        block = now[bottom, second] - taken(second, first, second)

        tasks = solve_all(first, inverse, top) + less_all(now, bottom, now, second, first)
        tasks += [bind(fresh_less, next_pair, before_last, columns) for columns in chunks if columns.start < chi]
        tasks += [bind(less, later, every, later, next_pair, first, columns) for columns in of_left]
        inverse = split(inverse_factor(block, tasks), PIECES)
        for i, piece in enumerate(inverse):
            inverses[i] = piece
        solve(second, inverse, bottom, next_pair, True)
        now[top, next_first] = later[top, next_first] - taken(next_first, second, next_first)
        return 0

    lax.fori_loop(0, chi // wide, body, 0)
    for task in solve_all(slice(chi - BLOCK, chi), [inverses[i] for i in range(PIECES)], bottom):
        task()

    count = factor_ref.shape[0]
    first = place_ref[0] * count
    mine = pl.ds(pl.multiple_of(first, 16), count)
    row_id = lax.broadcasted_iota(jnp.int32, (count, chi), 0) + first
    column_id = lax.broadcasted_iota(jnp.int32, (count, chi), 1)
    factor_ref[...] = jnp.where(column_id <= row_id, low[mine, :] * (1.0 / scale), 0.0)
    weights_ref[...] = solved[0, mine, chi:]


def factorize(mine, other, left, places, rows, chunk, scale):
    chi = left.shape[0]
    whole = pl.BlockSpec(memory_space=pltpu.VMEM)
    return pl.pallas_call(
        functools.partial(factor_kernel, scale, chunk),
        out_shape=[
            jax.ShapeDtypeStruct((rows, chi), jnp.float32),
            jax.ShapeDtypeStruct((rows, chi), jnp.bfloat16),
        ],
        in_specs=[pl.BlockSpec(memory_space=pltpu.SMEM)] + [whole] * 3,
        out_specs=[whole, whole],
        scratch_shapes=[
            pltpu.VMEM((chi // 2, chi + BLOCK), jnp.float32),
            pltpu.VMEM((chi, chi), jnp.float32),
            pltpu.VMEM((2 * BLOCK, 2 * chi), jnp.float32),
            pltpu.VMEM((2 * BLOCK, 2 * chi), jnp.float32),
            pltpu.VMEM((PIECES, BLOCK, BLOCK), jnp.bfloat16),
            pltpu.VMEM((PIECES, chi, 2 * chi), jnp.bfloat16),
            pltpu.VMEM((PIECES, chi, chi), jnp.bfloat16),
            pltpu.VMEM((chi, chi), jnp.float32),
        ],
        compiler_params=pltpu.CompilerParams(vmem_limit_bytes=52 * 2**20),
        cost_estimate=pl.CostEstimate(flops=20 * 2 * chi**3, bytes_accessed=16 * chi**2, transcendentals=0),
    )(places, mine, other, left)


def site_kernel(scale, slots, place_ref, weights_ref, own_ref, *refs):
    *got_refs, out_ref = refs
    depth = own_ref.shape[1]
    mine = weights_ref[:, pl.ds(pl.multiple_of(place_ref[1] * depth, depth), depth)]
    first = pl.multiple_of((place_ref[1] ^ 1) * depth, depth)
    count = own_ref.shape[0] // slots
    for slot in range(slots):
        for i in range(count):
            e = (place_ref[0] ^ slot) * count + i
            total, at = dot(mine, own_ref[e]), first
            for got_ref in got_refs[slot::slots]:
                part = got_ref.shape[1]
                total = total + dot(weights_ref[:, pl.ds(at, part)], got_ref[i].astype(jnp.bfloat16))
                at = pl.multiple_of(at + part, BLOCK)
            out_ref[e] = scale * total


def make_site(weights, own, got, places, scale):
    rows, chi = weights.shape
    east, _, right = own.shape
    whole = pl.BlockSpec(memory_space=pltpu.VMEM)
    pieces = sum(got, [])
    return pl.pallas_call(
        functools.partial(site_kernel, scale, len(got[0])),
        out_shape=jax.ShapeDtypeStruct((east, rows, right), jnp.float32),
        in_specs=[pl.BlockSpec(memory_space=pltpu.SMEM)] + [whole] * (2 + len(pieces)),
        out_specs=whole,
        compiler_params=pltpu.CompilerParams(vmem_limit_bytes=32 * 2**20),
        cost_estimate=pl.CostEstimate(
            flops=2 * rows * chi * east * right, bytes_accessed=8 * east * chi * right, transcendentals=0
        ),
    )(places, weights, own, *pieces)


def shards(sizes, left_factor, boundary_site, double_layer):
    lb, rb, rep = sizes["lb"], sizes["rb"], sizes["rep"]
    l, p = lax.axis_index("lb"), lax.axis_index("rep")
    depth, phys, right = boundary_site.shape
    east = phys // rep
    chi = depth * rep
    row_count = left_factor.shape[0]
    scale = math.sqrt(phys * rb * right)
    steps = {axis: steps_of(axis, size) for axis, size in sizes.items()}
    core, across = steps["lb"][:1], steps["lb"][1:]

    left_blocks = gather_slots([(0, left_factor.astype(jnp.float32))], steps["rep"])
    left_blocks = [piece for _, piece in sorted(left_blocks, key=lambda pair: pair[0])]
    left_blocks = [gather_slots([(0, piece)], across[::-1] + core) for piece in left_blocks]
    left_blocks = [sorted(pieces, key=lambda pair: pair[0]) for pieces in left_blocks]
    left_blocks = [left_blocks[q][s][1] for s in range(lb) for q in range(rep)]

    east_part, right_parts = max(1, east // lb), max(1, lb // east)
    right_part = right // right_parts
    east_at, right_at = (l // right_parts) * east_part, (l % right_parts) * right_part
    legs = [(p ^ s) * east + east_at + i for s in range(1, rep) for i in range(east_part)]
    sent = absorb(boundary_site, double_layer, legs, [east_part] * (rep - 1), jnp.float32)
    if right_parts > 1:
        sent = [lax.dynamic_slice_in_dim(piece, right_at, right_part, 2) for piece in sent]
    got = [swap(piece, ("rep", rep, s)) for s, piece in zip(range(1, rep), sent)]
    (own,) = absorb(boundary_site, double_layer, [p * east + i for i in range(east)], [east], jnp.bfloat16)
    share = lax.dynamic_slice(own, (east_at, 0, right_at), (east_part, depth, right_part))
    got, left_blocks = lax.optimization_barrier((got, left_blocks))

    near = across[:1] + steps["rep"][:1] + steps["rb"][:1]
    far = [step for step in across + steps["rep"] + steps["rb"] if step not in near]
    orders = [near[i:] + near[:i] for i in range(3)]
    cut = cut_steps(near, chi // 4)
    chunk = (chi // 4) >> cut
    bits = [position(core + order[:cut]) for order in orders]
    places = jnp.stack([l, p] + bits).astype(jnp.int32)
    kept, sent, left = gram_of_columns([share] + got, left_blocks, places, chi, chunk)
    whole = kept + swap(sent, core[0])
    third = whole.shape[1] // 3
    parts = [whole[:, i * third : (i + 1) * third] for i in range(3)]
    parts = reduce_parts(parts, orders, cut)
    whole = jnp.concatenate(parts, 1)
    cut_depth = depth // 4
    ahead = rep == 2 and right_parts == 1 and len(across) == 1 and far and cut_depth % BLOCK == 0
    after = [got[0][:, cut_depth:]] if ahead else got
    pairs = [[piece, swap(piece, core[0])] for piece in after]
    whole, pairs = lax.optimization_barrier((whole, pairs))
    for i, step in enumerate(far):
        if ahead and i == 0:
            early = got[0][:, :cut_depth]
            other, crossed = swap_parts([whole, early], [step, across[0]])
            early = gather_slots([(0, early), (across[0][2], crossed)], core)
        else:
            other = swap(whole, step)
        whole = whole + other
    parts = [whole[:, i * third : (i + 1) * third] for i in range(3)]
    parts = gather_parts(parts, orders, cut)
    whole = jnp.concatenate(parts, 1)
    other = swap(whole, core[0])
    pairs, whole = lax.optimization_barrier((pairs, whole))
    got = [gather_slots(list(zip(range(2), pair)), across[::-1]) for pair in pairs]

    factor, weights = factorize(whole, other, left, places, row_count, chunk, scale)
    if rep == 2 and right_parts == 1:
        pieces = [[piece for _, piece in sorted(held, key=lambda pair: pair[0])] for held in ([early] if ahead else []) + got]
        site_q = make_site(weights, own, pieces, places, scale)
    else:
        nothing = double_layer[0, 0] * 0.0
        site = jnp.zeros((east, chi, right), jnp.bfloat16)
        site = lax.dynamic_update_slice(site, own, (0, p * depth, 0))
        for s, pieces in zip(range(1, rep), got):
            for slot, piece in pieces:
                owner = l ^ slot
                at = ((owner // right_parts) * east_part, (p ^ s) * depth, (owner % right_parts) * right_part)
                site = lax.dynamic_update_slice(site, (piece + nothing).astype(jnp.bfloat16), at)
        site_q = jnp.einsum("ik,ekr->eir", weights, site, preferred_element_type=jnp.float32) * scale
    return (site_q, factor)


def solution(mesh):
    return jax.shard_map(
        functools.partial(shards, dict(mesh.shape)),
        mesh=mesh,
        in_specs=(P("lb", "rep"), P("rep", None, "rb"), P()),
        out_specs=(P("rep", "lb", "rb"), P("lb", None)),
        check_vma=False,
    )
```

```python
import functools
import math

import jax
import jax.numpy as jnp
from jax import lax
from jax.experimental import pallas as pl
from jax.experimental.pallas import tpu as pltpu
from jax.sharding import PartitionSpec as P

BLOCK = 128


def swap(array, step):
    axis, size, distance = step
    return lax.ppermute(array, axis, [(i, i ^ distance) for i in range(size)])


def steps_of(axis, size):
    return [(axis, size, 1 << i) for i in range(size.bit_length() - 1)]


def gather_slots(held, steps):
    for step in steps:
        held = held + [(slot ^ step[2], swap(piece, step)) for slot, piece in held]
    return held


def cut_steps(steps, rows):
    count = 0
    while count < len(steps) and rows % 16 == 0:
        rows, count = rows // 2, count + 1
    return count


def position(steps):
    place = jnp.int32(0)
    for axis, _, distance in steps:
        place = place * 2 + lax.rem(lax.div(lax.axis_index(axis), distance), 2)
    return place


def swap_parts(parts, steps):
    parts = lax.optimization_barrier(parts)
    return lax.optimization_barrier([swap(part, step) for part, step in zip(parts, steps)])


def reduce_parts(parts, orders, cuts):
    for at in range(cuts):
        half = parts[0].shape[0] // 2
        got = swap_parts([part[half:] for part in parts], [order[at] for order in orders])
        parts = [part[:half] + other for part, other in zip(parts, got)]
    return parts


def gather_parts(parts, orders, cuts):
    for at in range(cuts - 1, -1, -1):
        got = swap_parts(parts, [order[at] for order in orders])
        parts = [jnp.concatenate([part, other], 0) for part, other in zip(parts, got)]
    return parts


HIGHEST = lax.Precision.HIGHEST
GROUP = 16
PIECES = 2


def dot(a, b, transposed=False):
    dims = (((1,), (1 if transposed else 0,)), ((), ()))
    return lax.dot_general(a, b, dims, preferred_element_type=jnp.float32)


def absorb_kernel(east_parts, legs_ref, site_ref, double_ref, *out_refs):
    phys = double_ref.shape[0]
    legs = sum(east_parts)
    row = lax.broadcasted_iota(jnp.int32, (legs * GROUP, GROUP * phys), 0)
    column = lax.broadcasted_iota(jnp.int32, (legs * GROUP, GROUP * phys), 1)
    chosen = jnp.concatenate(
        [
            jnp.where(lax.broadcasted_iota(jnp.int32, (GROUP, phys), 1) == legs_ref[i], 1.0, 0.0)
            for i in range(legs)
        ],
        0,
    )
    values = lax.dot_general(
        chosen, double_ref[...], (((1,), (1,)), ((), ())), precision=HIGHEST, preferred_element_type=jnp.float32
    )
    spread = jnp.where(
        lax.broadcasted_iota(jnp.int32, (phys, GROUP * phys), 0)
        == lax.rem(lax.broadcasted_iota(jnp.int32, (phys, GROUP * phys), 1), phys),
        1.0,
        0.0,
    )
    values = jnp.dot(values, spread, precision=HIGHEST, preferred_element_type=jnp.float32)
    both = jnp.concatenate(split(jnp.where(lax.rem(row, GROUP) == lax.div(column, phys), values, 0.0), 2), 0)
    groups = site_ref.shape[0] // (GROUP * phys)
    for g in range(groups):
        rows = site_ref[g * GROUP * phys : (g + 1) * GROUP * phys, :]
        absorbed = dot(both, rows)
        absorbed = (absorbed[: legs * GROUP] + absorbed[legs * GROUP :]).astype(jnp.bfloat16)
        leg = 0
        for out_ref, count in zip(out_refs, east_parts):
            for e in range(count):
                piece = absorbed[(leg + e) * GROUP : (leg + e + 1) * GROUP]
                out_ref[e, g * GROUP : (g + 1) * GROUP, :] = piece.astype(out_ref.dtype)
            leg += count


def absorb(boundary_site, double_layer, legs, east_parts, dtype):
    legs = jnp.stack(legs).astype(jnp.int32)
    depth, phys, right = boundary_site.shape
    tiles = max(1, depth // 128)
    tile = depth // tiles
    out_shape, out_specs = [], []
    for count in east_parts:
        out_shape.append(jax.ShapeDtypeStruct((count, depth, right), dtype))
        out_specs.append(pl.BlockSpec((count, tile, right), lambda t: (0, t, 0)))
    return pl.pallas_call(
        functools.partial(absorb_kernel, east_parts),
        grid=(tiles,),
        out_shape=out_shape,
        in_specs=[
            pl.BlockSpec(memory_space=pltpu.SMEM),
            pl.BlockSpec((tile * phys, right), lambda t: (t, 0)),
            pl.BlockSpec(memory_space=pltpu.VMEM),
        ],
        out_specs=out_specs,
        compiler_params=pltpu.CompilerParams(vmem_limit_bytes=32 * 2**20),
        cost_estimate=pl.CostEstimate(
            flops=2 * 2 * depth * right * GROUP * phys * sum(east_parts), bytes_accessed=8 * depth * right * phys, transcendentals=0
        ),
    )(legs, boundary_site.reshape(depth * phys, right), double_layer)


def gram_kernel(chi, chunk, third, blocks, place_ref, *refs):
    block_refs, left_refs = refs[:blocks], refs[blocks:-7]
    kept_ref, sent_ref, left, columns, high, low, packed = refs[-7:]
    rows, width = left_refs[0].shape
    across = chi // width
    for i, left_ref in enumerate(left_refs):
        row_at = pl.multiple_of((place_ref[0] ^ (i // across)) * rows, 16)
        column_at = pl.multiple_of((place_ref[1] ^ (i % across)) * width, 128)
        left[pl.ds(row_at, rows), pl.ds(column_at, width)] = left_ref[...].astype(jnp.bfloat16)
    count, depth, width = block_refs[0].shape
    n = chi // BLOCK
    for i, block_ref in enumerate(block_refs):
        at = pl.ds(pl.multiple_of((place_ref[1] ^ i) * depth, depth), depth)
        for e in range(count):
            columns[at, e * width : (e + 1) * width] = block_ref[e].astype(jnp.bfloat16)
    for i in range(n // 2):
        at = slice(2 * i * BLOCK, 2 * (i + 1) * BLOCK)
        high[at], low[at] = split(dot(left[at], columns[...]), 2)
    for i in range(n):
        group, lo = (i, 0) if i < n // 2 else (n - 1 - i, (n - i) * BLOCK)
        at, upto = slice(i * BLOCK, (i + 1) * BLOCK), slice(0, (i + 1) * BLOCK)
        both = dot(jnp.concatenate([high[at], low[at]], 0), high[upto], True)
        packed[group * BLOCK : (group + 1) * BLOCK, lo : lo + (i + 1) * BLOCK] = (
            both[:BLOCK] + both[BLOCK:] + dot(high[at], low[upto], True)
        )
    half = kept_ref.shape[0]
    for part in range(3):
        lanes = slice(part * third, (part + 1) * third)
        for t in range(packed.shape[0] // chunk):
            rows_at = pl.ds(pl.multiple_of((place_ref[2 + part] ^ t) * chunk, 8), chunk)
            at = t * chunk
            to_ref = kept_ref if at < half else sent_ref
            to_ref[at % half : at % half + chunk, lanes] = packed[rows_at, lanes]


def gram_of_columns(blocks, left_blocks, places, chi, chunk):
    rows, width = chi // 2, chi + BLOCK
    count, _, right = blocks[0].shape
    whole = pl.BlockSpec(memory_space=pltpu.VMEM)
    return pl.pallas_call(
        functools.partial(gram_kernel, chi, chunk, width // 3, len(blocks)),
        out_shape=[jax.ShapeDtypeStruct((rows // 2, width), jnp.float32)] * 2
        + [jax.ShapeDtypeStruct((chi, chi), jnp.bfloat16)],
        in_specs=[pl.BlockSpec(memory_space=pltpu.SMEM)] + [whole] * (len(blocks) + len(left_blocks)),
        out_specs=[whole, whole, whole],
        scratch_shapes=[pltpu.VMEM((chi, count * right), jnp.bfloat16)] * 3 + [pltpu.VMEM((rows, width), jnp.float32)],
        compiler_params=pltpu.CompilerParams(vmem_limit_bytes=40 * 2**20),
        cost_estimate=pl.CostEstimate(
            flops=5 * chi * chi * count * right, bytes_accessed=12 * chi * chi, transcendentals=0
        ),
    )(places, *blocks, *left_blocks)


def sub(x, s):
    return jnp.broadcast_to(x[s : s + 1, :], x.shape)


def lane(x, k):
    return jnp.broadcast_to(x[:, k : k + 1], x.shape)


def inverse_factor(block, tasks, spread):
    n, wide = BLOCK // 8, 8
    rows = [block[8 * b : 8 * b + 8] for b in range(n)]
    sub_id = lax.broadcasted_iota(jnp.int32, (8, BLOCK), 0)
    lane_id = lax.broadcasted_iota(jnp.int32, (8, BLOCK), 1)
    pivots = []
    head = [lane(rows[0], c) for c in range(wide)]
    for b in range(n):
        k = wide * b
        cols = [[head[c]] + [lane(rows[i], k + c) for i in range(b + 1, n)] for c in range(wide)]
        if b + 1 < n:
            head = [lane(rows[b + 1], k + wide + c) for c in range(wide)]
        inside = (lane_id >= k) & (lane_id < k + wide)
        for i in range(b, n):
            rows[i] = jnp.where(inside, 0.0, rows[i])
        pivot = jnp.ones((8, BLOCK), jnp.float32)
        near = min(2, n - b)
        multiples, scaled = {}, []
        for c in range(wide):
            d = sub(cols[c][0], c)
            inverse = 1.0 / d
            pivot = jnp.where(sub_id == c, d, pivot)
            for c2 in range(c + 1, wide):
                multiples[c2, c] = sub(cols[c][0], c2) * inverse
                for i in range(near):
                    cols[c2][i] = cols[c2][i] - cols[c][i] * multiples[c2, c]
            factors = [cols[c][i] * inverse for i in range(near)]
            if b + 1 < n:
                at = (b % 2 * wide + c) * 8
                spread[at : at + 8, :] = cols[c][1]
                for c2 in range(wide):
                    head[c2] = head[c2] - factors[1] * jnp.broadcast_to(spread[at + c2 : at + c2 + 1, :], (8, BLOCK))
            factors[0] = jnp.where(sub_id > c, factors[0], 0.0)
            row = jnp.where(lane_id == k + c, 1.0, sub(rows[b], c))
            scaled.append(row * inverse)
            for i in range(near):
                rows[b + i] = rows[b + i] - factors[i] * row
        if b + 2 < n:
            for c in range(wide - 1, 0, -1):
                for c2 in range(c):
                    scaled[c2] = scaled[c2] - multiples[c, c2] * scaled[c]
            for i in range(2, n - b):
                total = cols[0][i] * scaled[0]
                for c in range(1, wide):
                    total = total + cols[c][i] * scaled[c]
                rows[b + i] = rows[b + i] - total
        pivots.append(pivot)
        for task in tasks[len(tasks) * b // n : len(tasks) * (b + 1) // n]:
            task()
    out = []
    for b in range(n):
        diagonal = sub_id + 8 * b
        row = jnp.where(lane_id < diagonal, rows[b], jnp.where(lane_id == diagonal, 1.0, 0.0))
        out.append(row * lax.rsqrt(pivots[b]))
    return jnp.concatenate(out, 0)


def split(x, pieces):
    out = []
    for i in range(pieces):
        out.append(x.astype(jnp.bfloat16))
        if i + 1 < pieces:
            x = x - out[-1].astype(jnp.float32)
    return out


def product(a, b):
    rows = a[0].shape[0]
    both = dot(jnp.concatenate(a, 0), b[0])
    return both[:rows] + both[rows:] + dot(a[0], b[1])


def factor_kernel(scale, chunk, place_ref, mine_ref, other_ref, left, *refs):
    factor_ref, weights_ref, packed, gram, now, later, inverses, spread, solved, lows, low = refs
    chi = left.shape[0]
    n = chi // BLOCK
    half, third = mine_ref.shape[0], mine_ref.shape[1] // 3
    for part in range(3):
        lanes = slice(part * third, (part + 1) * third)
        for t in range(2 * half // chunk):
            at = pl.ds(pl.multiple_of((place_ref[2 + part] ^ t) * chunk, 8), chunk)
            from_ref = mine_ref if t * chunk < half else other_ref
            packed[at, lanes] = from_ref[t * chunk % half : t * chunk % half + chunk, lanes]
    for i in range(n):
        group, lo = (i, 0) if i < n // 2 else (n - 1 - i, (n - i) * BLOCK)
        for k in range(i + 1):
            block = packed[group * BLOCK : (group + 1) * BLOCK, lo + k * BLOCK : lo + (k + 1) * BLOCK]
            gram[i * BLOCK : (i + 1) * BLOCK, k * BLOCK : (k + 1) * BLOCK] = block
            if k < i:
                gram[k * BLOCK : (k + 1) * BLOCK, i * BLOCK : (i + 1) * BLOCK] = block.T

    wide = 2 * BLOCK
    every, top, bottom = slice(0, wide), slice(0, BLOCK), slice(BLOCK, wide)
    chunks = [slice(c, c + wide) for c in range(0, 2 * chi, wide)]
    earlier, before_last = slice(0, chi - 2 * wide), slice(0, chi - 3 * BLOCK)
    bind = functools.partial

    def span(first, size):
        return pl.ds(pl.multiple_of(first, BLOCK), size)

    def fresh(rows, columns):
        if columns.start < chi:
            return gram[rows, columns]
        return left[rows, columns.start - chi : columns.stop - chi].astype(jnp.float32)

    def solve(at, inverse, rows, columns, of_gram):
        values = product(inverse, split(now[rows, columns], PIECES))
        for i, piece in enumerate(split(values, PIECES)):
            solved[i, at, columns] = piece
        if of_gram:
            column = values.T
            low[columns, at] = column
            for i, piece in enumerate(split(column, PIECES)):
                lows[i, columns, at] = piece

    def taken(rows, before, columns):
        return product(
            [lows[i, rows, before] for i in range(PIECES)], [solved[i, before, columns] for i in range(PIECES)]
        )

    def less(to, at, source, rows, before, columns):
        to[at, columns] = source[at, columns] - taken(rows, before, columns)

    def fresh_less(rows, before, columns):
        later[:, columns] = fresh(rows, columns) - taken(rows, before, columns)

    def solve_all(at, inverse, rows):
        return [bind(solve, at, inverse, rows, columns, columns.start < chi) for columns in chunks]

    def less_all(*args):
        return [bind(less, *args, columns) for columns in chunks]

    for i in range(PIECES):
        solved[i, before_last] = jnp.zeros((chi - 3 * BLOCK, 2 * chi), jnp.bfloat16)
        lows[i, :, before_last] = jnp.zeros((chi, chi - 3 * BLOCK), jnp.bfloat16)
        inverses[i] = jnp.zeros_like(inverses[i])
    now[...] = jnp.zeros_like(now)
    for columns in chunks:
        later[:, columns] = fresh(every, columns)
    now[top, :BLOCK] = later[top, :BLOCK]

    def body(j, _):
        lo = j * wide
        last = span(lax.rem(lo + chi - BLOCK, chi), BLOCK)
        first, second, pair = span(lo, BLOCK), span(lo + BLOCK, BLOCK), span(lo, wide)
        following = jnp.minimum(lo + wide, chi - wide)
        next_pair, next_first = span(following, wide), span(following, BLOCK)

        inverse = [inverses[i] for i in range(PIECES)]
        tasks = solve_all(last, inverse, bottom) + less_all(now, every, later, pair, last)
        of_left = [columns for columns in chunks if columns.start >= chi]
        tasks += [bind(fresh_less, next_pair, earlier, columns) for columns in of_left]
        inverse = split(inverse_factor(now[top, first], tasks, spread), PIECES)
        solve(first, inverse, top, second, True)
        block = now[bottom, second] - taken(second, first, second)

        tasks = solve_all(first, inverse, top) + less_all(now, bottom, now, second, first)
        tasks += [bind(fresh_less, next_pair, before_last, columns) for columns in chunks if columns.start < chi]
        tasks += [bind(less, later, every, later, next_pair, first, columns) for columns in of_left]
        inverse = split(inverse_factor(block, tasks, spread), PIECES)
        for i, piece in enumerate(inverse):
            inverses[i] = piece
        solve(second, inverse, bottom, next_pair, True)
        now[top, next_first] = later[top, next_first] - taken(next_first, second, next_first)
        return 0

    lax.fori_loop(0, chi // wide, body, 0)
    for task in solve_all(slice(chi - BLOCK, chi), [inverses[i] for i in range(PIECES)], bottom)[chi // wide - 1 :]:
        task()

    count = factor_ref.shape[0]
    first = place_ref[0] * count
    mine = pl.ds(pl.multiple_of(first, 16), count)
    row_id = lax.broadcasted_iota(jnp.int32, (count, chi), 0) + first
    column_id = lax.broadcasted_iota(jnp.int32, (count, chi), 1)
    factor_ref[...] = jnp.where(column_id <= row_id, low[mine, :] * (1.0 / scale), 0.0)
    weights_ref[...] = solved[0, mine, chi:]


def factorize(mine, other, left, places, rows, chunk, scale):
    chi = left.shape[0]
    whole = pl.BlockSpec(memory_space=pltpu.VMEM)
    return pl.pallas_call(
        functools.partial(factor_kernel, scale, chunk),
        out_shape=[
            jax.ShapeDtypeStruct((rows, chi), jnp.float32),
            jax.ShapeDtypeStruct((rows, chi), jnp.bfloat16),
        ],
        in_specs=[pl.BlockSpec(memory_space=pltpu.SMEM)] + [whole] * 3,
        out_specs=[whole, whole],
        scratch_shapes=[
            pltpu.VMEM((chi // 2, chi + BLOCK), jnp.float32),
            pltpu.VMEM((chi, chi), jnp.float32),
            pltpu.VMEM((2 * BLOCK, 2 * chi), jnp.float32),
            pltpu.VMEM((2 * BLOCK, 2 * chi), jnp.float32),
            pltpu.VMEM((PIECES, BLOCK, BLOCK), jnp.bfloat16),
            pltpu.VMEM((BLOCK, BLOCK), jnp.float32),
            pltpu.VMEM((PIECES, chi, 2 * chi), jnp.bfloat16),
            pltpu.VMEM((PIECES, chi, chi), jnp.bfloat16),
            pltpu.VMEM((chi, chi), jnp.float32),
        ],
        compiler_params=pltpu.CompilerParams(vmem_limit_bytes=52 * 2**20),
        cost_estimate=pl.CostEstimate(flops=20 * 2 * chi**3, bytes_accessed=16 * chi**2, transcendentals=0),
    )(places, mine, other, left)


def site_kernel(scale, slots, place_ref, weights_ref, own_ref, *refs):
    *got_refs, out_ref = refs
    depth = own_ref.shape[1]
    mine = weights_ref[:, pl.ds(pl.multiple_of(place_ref[1] * depth, depth), depth)]
    first = pl.multiple_of((place_ref[1] ^ 1) * depth, depth)
    count = own_ref.shape[0] // slots
    for slot in range(slots):
        for i in range(count):
            e = (place_ref[0] ^ slot) * count + i
            total, at = dot(mine, own_ref[e]), first
            for got_ref in got_refs[slot::slots]:
                part = got_ref.shape[1]
                total = total + dot(weights_ref[:, pl.ds(at, part)], got_ref[i].astype(jnp.bfloat16))
                at = pl.multiple_of(at + part, BLOCK)
            out_ref[e] = scale * total


def make_site(weights, own, got, places, scale):
    rows, chi = weights.shape
    east, _, right = own.shape
    whole = pl.BlockSpec(memory_space=pltpu.VMEM)
    pieces = sum(got, [])
    return pl.pallas_call(
        functools.partial(site_kernel, scale, len(got[0])),
        out_shape=jax.ShapeDtypeStruct((east, rows, right), jnp.float32),
        in_specs=[pl.BlockSpec(memory_space=pltpu.SMEM)] + [whole] * (2 + len(pieces)),
        out_specs=whole,
        compiler_params=pltpu.CompilerParams(vmem_limit_bytes=32 * 2**20),
        cost_estimate=pl.CostEstimate(
            flops=2 * rows * chi * east * right, bytes_accessed=8 * east * chi * right, transcendentals=0
        ),
    )(places, weights, own, *pieces)


def shards(sizes, left_factor, boundary_site, double_layer):
    lb, rb, rep = sizes["lb"], sizes["rb"], sizes["rep"]
    l, p = lax.axis_index("lb"), lax.axis_index("rep")
    depth, phys, right = boundary_site.shape
    east = phys // rep
    chi = depth * rep
    row_count = left_factor.shape[0]
    scale = math.sqrt(phys * rb * right)
    steps = {axis: steps_of(axis, size) for axis, size in sizes.items()}
    core, across = steps["lb"][:1], steps["lb"][1:]

    left_blocks = gather_slots([(0, left_factor.astype(jnp.float32))], steps["rep"])
    left_blocks = [piece for _, piece in sorted(left_blocks, key=lambda pair: pair[0])]
    left_blocks = [gather_slots([(0, piece)], across[::-1] + core) for piece in left_blocks]
    left_blocks = [sorted(pieces, key=lambda pair: pair[0]) for pieces in left_blocks]
    left_blocks = [left_blocks[q][s][1] for s in range(lb) for q in range(rep)]

    east_part, right_parts = max(1, east // lb), max(1, lb // east)
    right_part = right // right_parts
    east_at, right_at = (l // right_parts) * east_part, (l % right_parts) * right_part
    legs = [(p ^ s) * east + east_at + i for s in range(1, rep) for i in range(east_part)]
    sent = absorb(boundary_site, double_layer, legs, [east_part] * (rep - 1), jnp.float32)
    if right_parts > 1:
        sent = [lax.dynamic_slice_in_dim(piece, right_at, right_part, 2) for piece in sent]
    got = [swap(piece, ("rep", rep, s)) for s, piece in zip(range(1, rep), sent)]
    (own,) = absorb(boundary_site, double_layer, [p * east + i for i in range(east)], [east], jnp.bfloat16)
    share = lax.dynamic_slice(own, (east_at, 0, right_at), (east_part, depth, right_part))
    got, left_blocks = lax.optimization_barrier((got, left_blocks))

    near = across[:1] + steps["rep"][:1] + steps["rb"][:1]
    far = [step for step in across + steps["rep"] + steps["rb"] if step not in near]
    orders = [near[i:] + near[:i] for i in range(3)]
    cut = cut_steps(near, chi // 4)
    chunk = (chi // 4) >> cut
    bits = [position(core + order[:cut]) for order in orders]
    places = jnp.stack([l, p] + bits).astype(jnp.int32)
    kept, sent, left = gram_of_columns([share] + got, left_blocks, places, chi, chunk)
    whole = kept + swap(sent, core[0])
    third = whole.shape[1] // 3
    parts = [whole[:, i * third : (i + 1) * third] for i in range(3)]
    parts = reduce_parts(parts, orders, cut)
    whole = jnp.concatenate(parts, 1)
    cut_depth = depth // 4
    ahead = rep == 2 and right_parts == 1 and len(across) == 1 and far and cut_depth % BLOCK == 0
    after = [got[0][:, cut_depth:]] if ahead else got
    pairs = [[piece, swap(piece, core[0])] for piece in after]
    whole, pairs = lax.optimization_barrier((whole, pairs))
    for i, step in enumerate(far):
        if ahead and i == 0:
            early = got[0][:, :cut_depth]
            other, crossed = swap_parts([whole, early], [step, across[0]])
            early = gather_slots([(0, early), (across[0][2], crossed)], core)
        else:
            other = swap(whole, step)
        whole = whole + other
    parts = [whole[:, i * third : (i + 1) * third] for i in range(3)]
    parts = gather_parts(parts, orders, cut)
    whole = jnp.concatenate(parts, 1)
    other = swap(whole, core[0])
    pairs, whole = lax.optimization_barrier((pairs, whole))
    got = [gather_slots(list(zip(range(2), pair)), across[::-1]) for pair in pairs]

    factor, weights = factorize(whole, other, left, places, row_count, chunk, scale)
    if rep == 2 and right_parts == 1:
        pieces = [[piece for _, piece in sorted(held, key=lambda pair: pair[0])] for held in ([early] if ahead else []) + got]
        site_q = make_site(weights, own, pieces, places, scale)
    else:
        nothing = double_layer[0, 0] * 0.0
        site = jnp.zeros((east, chi, right), jnp.bfloat16)
        site = lax.dynamic_update_slice(site, own, (0, p * depth, 0))
        for s, pieces in zip(range(1, rep), got):
            for slot, piece in pieces:
                owner = l ^ slot
                at = ((owner // right_parts) * east_part, (p ^ s) * depth, (owner % right_parts) * right_part)
                site = lax.dynamic_update_slice(site, (piece + nothing).astype(jnp.bfloat16), at)
        site_q = jnp.einsum("ik,ekr->eir", weights, site, preferred_element_type=jnp.float32) * scale
    return (site_q, factor)


def solution(mesh):
    return jax.shard_map(
        functools.partial(shards, dict(mesh.shape)),
        mesh=mesh,
        in_specs=(P("lb", "rep"), P("rep", None, "rb"), P()),
        out_specs=(P("rep", "lb", "rb"), P("lb", None)),
        check_vma=False,
    )
```

```python
import functools
import math

import jax
import jax.numpy as jnp
from jax import lax
from jax.experimental import pallas as pl
from jax.experimental.pallas import tpu as pltpu
from jax.sharding import PartitionSpec as P

BLOCK = 128


def swap(array, step):
    axis, size, distance = step
    return lax.ppermute(array, axis, [(i, i ^ distance) for i in range(size)])


def steps_of(axis, size):
    return [(axis, size, 1 << i) for i in range(size.bit_length() - 1)]


def gather_slots(held, steps):
    for step in steps:
        held = held + [(slot ^ step[2], swap(piece, step)) for slot, piece in held]
    return held


def cut_steps(steps, rows):
    count = 0
    while count < len(steps) and rows % 16 == 0:
        rows, count = rows // 2, count + 1
    return count


def position(steps):
    place = jnp.int32(0)
    for axis, _, distance in steps:
        place = place * 2 + lax.rem(lax.div(lax.axis_index(axis), distance), 2)
    return place


def swap_parts(parts, steps):
    parts = lax.optimization_barrier(parts)
    return lax.optimization_barrier([swap(part, step) for part, step in zip(parts, steps)])


def reduce_parts(parts, orders, cuts):
    for at in range(cuts):
        half = parts[0].shape[0] // 2
        got = swap_parts([part[half:] for part in parts], [order[at] for order in orders])
        parts = [part[:half] + other for part, other in zip(parts, got)]
    return parts


def gather_parts(parts, orders, cuts):
    for at in range(cuts - 1, -1, -1):
        got = swap_parts(parts, [order[at] for order in orders])
        parts = [jnp.concatenate([part, other], 0) for part, other in zip(parts, got)]
    return parts


HIGHEST = lax.Precision.HIGHEST
GROUP = 16
PIECES = 2


def dot(a, b, transposed=False):
    dims = (((1,), (1 if transposed else 0,)), ((), ()))
    return lax.dot_general(a, b, dims, preferred_element_type=jnp.float32)


def absorb_kernel(east_parts, legs_ref, site_ref, double_ref, *out_refs):
    phys = double_ref.shape[0]
    legs = sum(east_parts)
    row = lax.broadcasted_iota(jnp.int32, (legs * GROUP, GROUP * phys), 0)
    column = lax.broadcasted_iota(jnp.int32, (legs * GROUP, GROUP * phys), 1)
    chosen = jnp.concatenate(
        [
            jnp.where(lax.broadcasted_iota(jnp.int32, (GROUP, phys), 1) == legs_ref[i], 1.0, 0.0)
            for i in range(legs)
        ],
        0,
    )
    values = lax.dot_general(
        chosen, double_ref[...], (((1,), (1,)), ((), ())), precision=HIGHEST, preferred_element_type=jnp.float32
    )
    spread = jnp.where(
        lax.broadcasted_iota(jnp.int32, (phys, GROUP * phys), 0)
        == lax.rem(lax.broadcasted_iota(jnp.int32, (phys, GROUP * phys), 1), phys),
        1.0,
        0.0,
    )
    values = jnp.dot(values, spread, precision=HIGHEST, preferred_element_type=jnp.float32)
    both = jnp.concatenate(split(jnp.where(lax.rem(row, GROUP) == lax.div(column, phys), values, 0.0), 2), 0)
    groups = site_ref.shape[0] // (GROUP * phys)
    for g in range(groups):
        rows = site_ref[g * GROUP * phys : (g + 1) * GROUP * phys, :]
        absorbed = dot(both, rows)
        absorbed = (absorbed[: legs * GROUP] + absorbed[legs * GROUP :]).astype(jnp.bfloat16)
        leg = 0
        for out_ref, count in zip(out_refs, east_parts):
            for e in range(count):
                piece = absorbed[(leg + e) * GROUP : (leg + e + 1) * GROUP]
                out_ref[e, g * GROUP : (g + 1) * GROUP, :] = piece.astype(out_ref.dtype)
            leg += count


def absorb(boundary_site, double_layer, legs, east_parts, dtype):
    legs = jnp.stack(legs).astype(jnp.int32)
    depth, phys, right = boundary_site.shape
    tiles = max(1, depth // 128)
    tile = depth // tiles
    out_shape, out_specs = [], []
    for count in east_parts:
        out_shape.append(jax.ShapeDtypeStruct((count, depth, right), dtype))
        out_specs.append(pl.BlockSpec((count, tile, right), lambda t: (0, t, 0)))
    return pl.pallas_call(
        functools.partial(absorb_kernel, east_parts),
        grid=(tiles,),
        out_shape=out_shape,
        in_specs=[
            pl.BlockSpec(memory_space=pltpu.SMEM),
            pl.BlockSpec((tile * phys, right), lambda t: (t, 0)),
            pl.BlockSpec(memory_space=pltpu.VMEM),
        ],
        out_specs=out_specs,
        compiler_params=pltpu.CompilerParams(vmem_limit_bytes=32 * 2**20),
        cost_estimate=pl.CostEstimate(
            flops=2 * 2 * depth * right * GROUP * phys * sum(east_parts), bytes_accessed=8 * depth * right * phys, transcendentals=0
        ),
    )(legs, boundary_site.reshape(depth * phys, right), double_layer)


def gram_kernel(chi, chunk, third, blocks, place_ref, *refs):
    block_refs, left_refs = refs[:blocks], refs[blocks:-7]
    kept_ref, sent_ref, left, columns, high, low, packed = refs[-7:]
    rows, width = left_refs[0].shape
    across = chi // width
    for i, left_ref in enumerate(left_refs):
        row_at = pl.multiple_of((place_ref[0] ^ (i // across)) * rows, 16)
        column_at = pl.multiple_of((place_ref[1] ^ (i % across)) * width, 128)
        left[pl.ds(row_at, rows), pl.ds(column_at, width)] = left_ref[...].astype(jnp.bfloat16)
    count, depth, width = block_refs[0].shape
    n = chi // BLOCK
    for i, block_ref in enumerate(block_refs):
        at = pl.ds(pl.multiple_of((place_ref[1] ^ i) * depth, depth), depth)
        for e in range(count):
            columns[at, e * width : (e + 1) * width] = block_ref[e].astype(jnp.bfloat16)
    for i in range(n // 2):
        at = slice(2 * i * BLOCK, 2 * (i + 1) * BLOCK)
        high[at], low[at] = split(dot(left[at], columns[...]), 2)
    for i in range(n):
        group, lo = (i, 0) if i < n // 2 else (n - 1 - i, (n - i) * BLOCK)
        at, upto = slice(i * BLOCK, (i + 1) * BLOCK), slice(0, (i + 1) * BLOCK)
        both = dot(jnp.concatenate([high[at], low[at]], 0), high[upto], True)
        packed[group * BLOCK : (group + 1) * BLOCK, lo : lo + (i + 1) * BLOCK] = (
            both[:BLOCK] + both[BLOCK:] + dot(high[at], low[upto], True)
        )
    half = kept_ref.shape[0]
    for part in range(3):
        lanes = slice(part * third, (part + 1) * third)
        for t in range(packed.shape[0] // chunk):
            rows_at = pl.ds(pl.multiple_of((place_ref[2 + part] ^ t) * chunk, 8), chunk)
            at = t * chunk
            to_ref = kept_ref if at < half else sent_ref
            to_ref[at % half : at % half + chunk, lanes] = packed[rows_at, lanes]


def gram_of_columns(blocks, left_blocks, places, chi, chunk):
    rows, width = chi // 2, chi + BLOCK
    count, _, right = blocks[0].shape
    whole = pl.BlockSpec(memory_space=pltpu.VMEM)
    return pl.pallas_call(
        functools.partial(gram_kernel, chi, chunk, width // 3, len(blocks)),
        out_shape=[jax.ShapeDtypeStruct((rows // 2, width), jnp.float32)] * 2
        + [jax.ShapeDtypeStruct((chi, chi), jnp.bfloat16)],
        in_specs=[pl.BlockSpec(memory_space=pltpu.SMEM)] + [whole] * (len(blocks) + len(left_blocks)),
        out_specs=[whole, whole, whole],
        scratch_shapes=[pltpu.VMEM((chi, count * right), jnp.bfloat16)] * 3 + [pltpu.VMEM((rows, width), jnp.float32)],
        compiler_params=pltpu.CompilerParams(vmem_limit_bytes=40 * 2**20),
        cost_estimate=pl.CostEstimate(
            flops=5 * chi * chi * count * right, bytes_accessed=12 * chi * chi, transcendentals=0
        ),
    )(places, *blocks, *left_blocks)


def sub(x, s):
    return jnp.broadcast_to(x[s : s + 1, :], x.shape)


def lane(x, k):
    return jnp.broadcast_to(x[:, k : k + 1], x.shape)


def inverse_factor(block, tasks, spread):
    n, wide = BLOCK // 8, 8
    rows = [block[8 * b : 8 * b + 8] for b in range(n)]
    sub_id = lax.broadcasted_iota(jnp.int32, (8, BLOCK), 0)
    lane_id = lax.broadcasted_iota(jnp.int32, (8, BLOCK), 1)
    pivots = []
    head = [lane(rows[0], c) for c in range(wide)]
    for b in range(n):
        k = wide * b
        cols = [[head[c]] + [lane(rows[i], k + c) for i in range(b + 1, n)] for c in range(wide)]
        if b + 1 < n:
            head = [lane(rows[b + 1], k + wide + c) for c in range(wide)]
        inside = (lane_id >= k) & (lane_id < k + wide)
        for i in range(b, n):
            rows[i] = jnp.where(inside, 0.0, rows[i])
        pivot = jnp.ones((8, BLOCK), jnp.float32)
        near = min(2, n - b)
        multiples, scaled = {}, []
        for c in range(wide):
            d = sub(cols[c][0], c)
            inverse = 1.0 / d
            pivot = jnp.where(sub_id == c, d, pivot)
            for c2 in range(c + 1, wide):
                multiples[c2, c] = sub(cols[c][0], c2) * inverse
                for i in range(near):
                    cols[c2][i] = cols[c2][i] - cols[c][i] * multiples[c2, c]
            factors = [cols[c][i] * inverse for i in range(near)]
            if b + 1 < n:
                at = (b % 2 * wide + c) * 8
                spread[at : at + 8, :] = cols[c][1]
                for c2 in range(wide):
                    head[c2] = head[c2] - factors[1] * jnp.broadcast_to(spread[at + c2 : at + c2 + 1, :], (8, BLOCK))
            factors[0] = jnp.where(sub_id > c, factors[0], 0.0)
            row = jnp.where(lane_id == k + c, 1.0, sub(rows[b], c))
            scaled.append(row * inverse)
            for i in range(near):
                rows[b + i] = rows[b + i] - factors[i] * row
        if b + 2 < n:
            for c in range(wide - 1, 0, -1):
                for c2 in range(c):
                    scaled[c2] = scaled[c2] - multiples[c, c2] * scaled[c]
            for i in range(2, n - b):
                total = cols[0][i] * scaled[0]
                for c in range(1, wide):
                    total = total + cols[c][i] * scaled[c]
                rows[b + i] = rows[b + i] - total
        pivots.append(pivot)
        for task in tasks[len(tasks) * b // n : len(tasks) * (b + 1) // n]:
            task()
    out = []
    for b in range(n):
        diagonal = sub_id + 8 * b
        row = jnp.where(lane_id < diagonal, rows[b], jnp.where(lane_id == diagonal, 1.0, 0.0))
        out.append(row * lax.rsqrt(pivots[b]))
    return jnp.concatenate(out, 0)


def split(x, pieces):
    out = []
    for i in range(pieces):
        out.append(x.astype(jnp.bfloat16))
        if i + 1 < pieces:
            x = x - out[-1].astype(jnp.float32)
    return out


def product(a, b):
    rows = a[0].shape[0]
    both = dot(jnp.concatenate(a, 0), b[0])
    return both[:rows] + both[rows:] + dot(a[0], b[1])


def factor_kernel(scale, chunk, place_ref, mine_ref, other_ref, left, *refs):
    factor_ref, weights_ref, packed, gram, now, later, inverses, spread, solved, lows, low = refs
    chi = left.shape[0]
    n = chi // BLOCK
    half, third = mine_ref.shape[0], mine_ref.shape[1] // 3
    for part in range(3):
        lanes = slice(part * third, (part + 1) * third)
        for t in range(2 * half // chunk):
            at = pl.ds(pl.multiple_of((place_ref[2 + part] ^ t) * chunk, 8), chunk)
            from_ref = mine_ref if t * chunk < half else other_ref
            packed[at, lanes] = from_ref[t * chunk % half : t * chunk % half + chunk, lanes]
    for i in range(n):
        group, lo = (i, 0) if i < n // 2 else (n - 1 - i, (n - i) * BLOCK)
        for k in range(i + 1):
            block = packed[group * BLOCK : (group + 1) * BLOCK, lo + k * BLOCK : lo + (k + 1) * BLOCK]
            gram[i * BLOCK : (i + 1) * BLOCK, k * BLOCK : (k + 1) * BLOCK] = block
            if k < i:
                gram[k * BLOCK : (k + 1) * BLOCK, i * BLOCK : (i + 1) * BLOCK] = block.T

    wide = 2 * BLOCK
    every, top, bottom = slice(0, wide), slice(0, BLOCK), slice(BLOCK, wide)
    chunks = [slice(c, c + wide) for c in range(0, 2 * chi, wide)]
    earlier = slice(0, chi - 2 * wide)
    bind = functools.partial

    def span(first, size):
        return pl.ds(pl.multiple_of(first, BLOCK), size)

    def fresh(rows, columns):
        if columns.start < chi:
            return gram[rows, columns]
        return left[rows, columns.start - chi : columns.stop - chi].astype(jnp.float32)

    def solve(at, inverse, rows, columns, of_gram):
        values = product(inverse, split(now[rows, columns], PIECES))
        for i, piece in enumerate(split(values, PIECES)):
            solved[i, at, columns] = piece
        if of_gram:
            column = values.T
            low[columns, at] = column
            for i, piece in enumerate(split(column, PIECES)):
                lows[i, columns, at] = piece

    def taken(rows, before, columns):
        return product(
            [lows[i, rows, before] for i in range(PIECES)], [solved[i, before, columns] for i in range(PIECES)]
        )

    def less(to, at, source, rows, before, columns):
        to[at, columns] = source[at, columns] - taken(rows, before, columns)

    def fresh_less(rows, before, columns):
        later[:, columns] = fresh(rows, columns) - taken(rows, before, columns)

    def solve_all(at, inverse, rows):
        return [bind(solve, at, inverse, rows, columns, columns.start < chi) for columns in chunks]

    def less_all(*args):
        return [bind(less, *args, columns) for columns in chunks]

    for i in range(PIECES):
        solved[i, earlier] = jnp.zeros((chi - 2 * wide, 2 * chi), jnp.bfloat16)
        lows[i, :, earlier] = jnp.zeros((chi, chi - 2 * wide), jnp.bfloat16)
        inverses[i] = jnp.zeros_like(inverses[i])
    now[...] = jnp.zeros_like(now)
    for columns in chunks:
        later[:, columns] = fresh(every, columns)

    def next_block(inverse, row, block):
        values = product(inverse, split(row, PIECES))
        return block - product(split(values.T, PIECES), split(values, PIECES))

    def body(j, block):
        lo = j * wide
        last = span(lax.rem(lo + chi - BLOCK, chi), BLOCK)
        first, second, pair = span(lo, BLOCK), span(lo + BLOCK, BLOCK), span(lo, wide)
        following = jnp.minimum(lo + wide, chi - wide)
        next_pair, next_first = span(following, wide), span(following, BLOCK)

        inverse = [inverses[i] for i in range(PIECES)]
        tasks = solve_all(last, inverse, bottom) + less_all(now, every, later, pair, last)
        tasks += [bind(fresh_less, next_pair, earlier, columns) for columns in chunks]
        inverse = split(inverse_factor(block, tasks, spread), PIECES)
        block = next_block(inverse, now[top, second], now[bottom, second])

        tasks = solve_all(first, inverse, top) + less_all(now, bottom, now, second, first)
        tasks += less_all(later, every, later, next_pair, first)
        inverse = split(inverse_factor(block, tasks, spread), PIECES)
        for i, piece in enumerate(inverse):
            inverses[i] = piece
        return next_block(inverse, now[bottom, next_first], later[top, next_first])

    lax.fori_loop(0, chi // wide, body, gram[:BLOCK, :BLOCK])
    for task in solve_all(slice(chi - BLOCK, chi), [inverses[i] for i in range(PIECES)], bottom)[chi // wide - 1 :]:
        task()

    count = factor_ref.shape[0]
    first = place_ref[0] * count
    mine = pl.ds(pl.multiple_of(first, 16), count)
    row_id = lax.broadcasted_iota(jnp.int32, (count, chi), 0) + first
    column_id = lax.broadcasted_iota(jnp.int32, (count, chi), 1)
    factor_ref[...] = jnp.where(column_id <= row_id, low[mine, :] * (1.0 / scale), 0.0)
    weights_ref[...] = solved[0, mine, chi:]


def factorize(mine, other, left, places, rows, chunk, scale):
    chi = left.shape[0]
    whole = pl.BlockSpec(memory_space=pltpu.VMEM)
    return pl.pallas_call(
        functools.partial(factor_kernel, scale, chunk),
        out_shape=[
            jax.ShapeDtypeStruct((rows, chi), jnp.float32),
            jax.ShapeDtypeStruct((rows, chi), jnp.bfloat16),
        ],
        in_specs=[pl.BlockSpec(memory_space=pltpu.SMEM)] + [whole] * 3,
        out_specs=[whole, whole],
        scratch_shapes=[
            pltpu.VMEM((chi // 2, chi + BLOCK), jnp.float32),
            pltpu.VMEM((chi, chi), jnp.float32),
            pltpu.VMEM((2 * BLOCK, 2 * chi), jnp.float32),
            pltpu.VMEM((2 * BLOCK, 2 * chi), jnp.float32),
            pltpu.VMEM((PIECES, BLOCK, BLOCK), jnp.bfloat16),
            pltpu.VMEM((BLOCK, BLOCK), jnp.float32),
            pltpu.VMEM((PIECES, chi, 2 * chi), jnp.bfloat16),
            pltpu.VMEM((PIECES, chi, chi), jnp.bfloat16),
            pltpu.VMEM((chi, chi), jnp.float32),
        ],
        compiler_params=pltpu.CompilerParams(vmem_limit_bytes=52 * 2**20),
        cost_estimate=pl.CostEstimate(flops=20 * 2 * chi**3, bytes_accessed=16 * chi**2, transcendentals=0),
    )(places, mine, other, left)


def site_kernel(scale, slots, place_ref, weights_ref, own_ref, *refs):
    *got_refs, out_ref = refs
    depth = own_ref.shape[1]
    mine = weights_ref[:, pl.ds(pl.multiple_of(place_ref[1] * depth, depth), depth)]
    first = pl.multiple_of((place_ref[1] ^ 1) * depth, depth)
    count = own_ref.shape[0] // slots
    for slot in range(slots):
        for i in range(count):
            e = (place_ref[0] ^ slot) * count + i
            total, at = dot(mine, own_ref[e]), first
            for got_ref in got_refs[slot::slots]:
                part = got_ref.shape[1]
                total = total + dot(weights_ref[:, pl.ds(at, part)], got_ref[i].astype(jnp.bfloat16))
                at = pl.multiple_of(at + part, BLOCK)
            out_ref[e] = scale * total


def make_site(weights, own, got, places, scale):
    rows, chi = weights.shape
    east, _, right = own.shape
    whole = pl.BlockSpec(memory_space=pltpu.VMEM)
    pieces = sum(got, [])
    return pl.pallas_call(
        functools.partial(site_kernel, scale, len(got[0])),
        out_shape=jax.ShapeDtypeStruct((east, rows, right), jnp.float32),
        in_specs=[pl.BlockSpec(memory_space=pltpu.SMEM)] + [whole] * (2 + len(pieces)),
        out_specs=whole,
        compiler_params=pltpu.CompilerParams(vmem_limit_bytes=32 * 2**20),
        cost_estimate=pl.CostEstimate(
            flops=2 * rows * chi * east * right, bytes_accessed=8 * east * chi * right, transcendentals=0
        ),
    )(places, weights, own, *pieces)


def shards(sizes, left_factor, boundary_site, double_layer):
    lb, rb, rep = sizes["lb"], sizes["rb"], sizes["rep"]
    l, p = lax.axis_index("lb"), lax.axis_index("rep")
    depth, phys, right = boundary_site.shape
    east = phys // rep
    chi = depth * rep
    row_count = left_factor.shape[0]
    scale = math.sqrt(phys * rb * right)
    steps = {axis: steps_of(axis, size) for axis, size in sizes.items()}
    core, across = steps["lb"][:1], steps["lb"][1:]

    left_blocks = gather_slots([(0, left_factor.astype(jnp.float32))], steps["rep"])
    left_blocks = [piece for _, piece in sorted(left_blocks, key=lambda pair: pair[0])]
    left_blocks = [gather_slots([(0, piece)], across[::-1] + core) for piece in left_blocks]
    left_blocks = [sorted(pieces, key=lambda pair: pair[0]) for pieces in left_blocks]
    left_blocks = [left_blocks[q][s][1] for s in range(lb) for q in range(rep)]

    east_part, right_parts = max(1, east // lb), max(1, lb // east)
    right_part = right // right_parts
    east_at, right_at = (l // right_parts) * east_part, (l % right_parts) * right_part
    legs = [(p ^ s) * east + east_at + i for s in range(1, rep) for i in range(east_part)]
    sent = absorb(boundary_site, double_layer, legs, [east_part] * (rep - 1), jnp.float32)
    if right_parts > 1:
        sent = [lax.dynamic_slice_in_dim(piece, right_at, right_part, 2) for piece in sent]
    got = [swap(piece, ("rep", rep, s)) for s, piece in zip(range(1, rep), sent)]
    (own,) = absorb(boundary_site, double_layer, [p * east + i for i in range(east)], [east], jnp.bfloat16)
    share = lax.dynamic_slice(own, (east_at, 0, right_at), (east_part, depth, right_part))
    got, left_blocks = lax.optimization_barrier((got, left_blocks))

    near = across[:1] + steps["rep"][:1] + steps["rb"][:1]
    far = [step for step in across + steps["rep"] + steps["rb"] if step not in near]
    orders = [near[i:] + near[:i] for i in range(3)]
    cut = cut_steps(near, chi // 4)
    chunk = (chi // 4) >> cut
    bits = [position(core + order[:cut]) for order in orders]
    places = jnp.stack([l, p] + bits).astype(jnp.int32)
    kept, sent, left = gram_of_columns([share] + got, left_blocks, places, chi, chunk)
    whole = kept + swap(sent, core[0])
    third = whole.shape[1] // 3
    parts = [whole[:, i * third : (i + 1) * third] for i in range(3)]
    parts = reduce_parts(parts, orders, cut)
    whole = jnp.concatenate(parts, 1)
    cut_depth = depth // 4
    ahead = rep == 2 and right_parts == 1 and len(across) == 1 and far and cut_depth % BLOCK == 0
    after = [got[0][:, cut_depth:]] if ahead else got
    pairs = [[piece, swap(piece, core[0])] for piece in after]
    whole, pairs = lax.optimization_barrier((whole, pairs))
    for i, step in enumerate(far):
        if ahead and i == 0:
            early = got[0][:, :cut_depth]
            other, crossed = swap_parts([whole, early], [step, across[0]])
            early = gather_slots([(0, early), (across[0][2], crossed)], core)
        else:
            other = swap(whole, step)
        whole = whole + other
    parts = [whole[:, i * third : (i + 1) * third] for i in range(3)]
    parts = gather_parts(parts, orders, cut)
    whole = jnp.concatenate(parts, 1)
    other = swap(whole, core[0])
    pairs, whole = lax.optimization_barrier((pairs, whole))
    got = [gather_slots(list(zip(range(2), pair)), across[::-1]) for pair in pairs]

    factor, weights = factorize(whole, other, left, places, row_count, chunk, scale)
    if rep == 2 and right_parts == 1:
        pieces = [[piece for _, piece in sorted(held, key=lambda pair: pair[0])] for held in ([early] if ahead else []) + got]
        site_q = make_site(weights, own, pieces, places, scale)
    else:
        nothing = double_layer[0, 0] * 0.0
        site = jnp.zeros((east, chi, right), jnp.bfloat16)
        site = lax.dynamic_update_slice(site, own, (0, p * depth, 0))
        for s, pieces in zip(range(1, rep), got):
            for slot, piece in pieces:
                owner = l ^ slot
                at = ((owner // right_parts) * east_part, (p ^ s) * depth, (owner % right_parts) * right_part)
                site = lax.dynamic_update_slice(site, (piece + nothing).astype(jnp.bfloat16), at)
        site_q = jnp.einsum("ik,ekr->eir", weights, site, preferred_element_type=jnp.float32) * scale
    return (site_q, factor)


def solution(mesh):
    return jax.shard_map(
        functools.partial(shards, dict(mesh.shape)),
        mesh=mesh,
        in_specs=(P("lb", "rep"), P("rep", None, "rb"), P()),
        out_specs=(P("rep", "lb", "rb"), P("lb", None)),
        check_vma=False,
    )
```

```python
import functools
import math

import jax
import jax.numpy as jnp
from jax import lax
from jax.experimental import pallas as pl
from jax.experimental.pallas import tpu as pltpu
from jax.sharding import PartitionSpec as P

BLOCK = 128


def swap(array, step):
    axis, size, distance = step
    return lax.ppermute(array, axis, [(i, i ^ distance) for i in range(size)])


def steps_of(axis, size):
    return [(axis, size, 1 << i) for i in range(size.bit_length() - 1)]


def gather_slots(held, steps):
    for step in steps:
        held = held + [(slot ^ step[2], swap(piece, step)) for slot, piece in held]
    return held


def cut_steps(steps, rows):
    count = 0
    while count < len(steps) and rows % 16 == 0:
        rows, count = rows // 2, count + 1
    return count


def position(steps):
    place = jnp.int32(0)
    for axis, _, distance in steps:
        place = place * 2 + lax.rem(lax.div(lax.axis_index(axis), distance), 2)
    return place


def swap_parts(parts, steps):
    parts = lax.optimization_barrier(parts)
    return lax.optimization_barrier([swap(part, step) for part, step in zip(parts, steps)])


def reduce_parts(parts, orders, cuts):
    for at in range(cuts):
        half = parts[0].shape[0] // 2
        got = swap_parts([part[half:] for part in parts], [order[at] for order in orders])
        parts = [part[:half] + other for part, other in zip(parts, got)]
    return parts


def gather_parts(parts, orders, cuts):
    for at in range(cuts - 1, -1, -1):
        got = swap_parts(parts, [order[at] for order in orders])
        parts = [jnp.concatenate([part, other], 0) for part, other in zip(parts, got)]
    return parts


HIGHEST = lax.Precision.HIGHEST
GROUP = 16
PIECES = 2


def dot(a, b, transposed=False):
    dims = (((1,), (1 if transposed else 0,)), ((), ()))
    return lax.dot_general(a, b, dims, preferred_element_type=jnp.float32)


def absorb_kernel(east_parts, legs_ref, site_ref, double_ref, *out_refs):
    phys = double_ref.shape[0]
    legs = sum(east_parts)
    row = lax.broadcasted_iota(jnp.int32, (legs * GROUP, GROUP * phys), 0)
    column = lax.broadcasted_iota(jnp.int32, (legs * GROUP, GROUP * phys), 1)
    chosen = jnp.concatenate(
        [
            jnp.where(lax.broadcasted_iota(jnp.int32, (GROUP, phys), 1) == legs_ref[i], 1.0, 0.0)
            for i in range(legs)
        ],
        0,
    )
    values = lax.dot_general(
        chosen, double_ref[...], (((1,), (1,)), ((), ())), precision=HIGHEST, preferred_element_type=jnp.float32
    )
    spread = jnp.where(
        lax.broadcasted_iota(jnp.int32, (phys, GROUP * phys), 0)
        == lax.rem(lax.broadcasted_iota(jnp.int32, (phys, GROUP * phys), 1), phys),
        1.0,
        0.0,
    )
    values = jnp.dot(values, spread, precision=HIGHEST, preferred_element_type=jnp.float32)
    both = jnp.concatenate(split(jnp.where(lax.rem(row, GROUP) == lax.div(column, phys), values, 0.0), 2), 0)
    groups = site_ref.shape[0] // (GROUP * phys)
    for g in range(groups):
        rows = site_ref[g * GROUP * phys : (g + 1) * GROUP * phys, :]
        absorbed = dot(both, rows)
        absorbed = (absorbed[: legs * GROUP] + absorbed[legs * GROUP :]).astype(jnp.bfloat16)
        leg = 0
        for out_ref, count in zip(out_refs, east_parts):
            for e in range(count):
                piece = absorbed[(leg + e) * GROUP : (leg + e + 1) * GROUP]
                out_ref[e, g * GROUP : (g + 1) * GROUP, :] = piece.astype(out_ref.dtype)
            leg += count


def absorb(boundary_site, double_layer, legs, east_parts, dtype):
    legs = jnp.stack(legs).astype(jnp.int32)
    depth, phys, right = boundary_site.shape
    tiles = max(1, depth // 128)
    tile = depth // tiles
    out_shape, out_specs = [], []
    for count in east_parts:
        out_shape.append(jax.ShapeDtypeStruct((count, depth, right), dtype))
        out_specs.append(pl.BlockSpec((count, tile, right), lambda t: (0, t, 0)))
    return pl.pallas_call(
        functools.partial(absorb_kernel, east_parts),
        grid=(tiles,),
        out_shape=out_shape,
        in_specs=[
            pl.BlockSpec(memory_space=pltpu.SMEM),
            pl.BlockSpec((tile * phys, right), lambda t: (t, 0)),
            pl.BlockSpec(memory_space=pltpu.VMEM),
        ],
        out_specs=out_specs,
        compiler_params=pltpu.CompilerParams(vmem_limit_bytes=32 * 2**20),
        cost_estimate=pl.CostEstimate(
            flops=2 * 2 * depth * right * GROUP * phys * sum(east_parts), bytes_accessed=8 * depth * right * phys, transcendentals=0
        ),
    )(legs, boundary_site.reshape(depth * phys, right), double_layer)


def gram_kernel(chi, chunk, third, blocks, place_ref, *refs):
    block_refs, left_refs = refs[:blocks], refs[blocks:-7]
    kept_ref, sent_ref, left, columns, high, low, packed = refs[-7:]
    rows, width = left_refs[0].shape
    across = chi // width
    for i, left_ref in enumerate(left_refs):
        row_at = pl.multiple_of((place_ref[0] ^ (i // across)) * rows, 16)
        column_at = pl.multiple_of((place_ref[1] ^ (i % across)) * width, 128)
        left[pl.ds(row_at, rows), pl.ds(column_at, width)] = left_ref[...].astype(jnp.bfloat16)
    count, depth, width = block_refs[0].shape
    n = chi // BLOCK
    for i, block_ref in enumerate(block_refs):
        at = pl.ds(pl.multiple_of((place_ref[1] ^ i) * depth, depth), depth)
        for e in range(count):
            columns[at, e * width : (e + 1) * width] = block_ref[e].astype(jnp.bfloat16)
    for i in range(n // 2):
        at = slice(2 * i * BLOCK, 2 * (i + 1) * BLOCK)
        high[at], low[at] = split(dot(left[at], columns[...]), 2)
    for i in range(n):
        group, lo = (i, 0) if i < n // 2 else (n - 1 - i, (n - i) * BLOCK)
        at, upto = slice(i * BLOCK, (i + 1) * BLOCK), slice(0, (i + 1) * BLOCK)
        both = dot(jnp.concatenate([high[at], low[at]], 0), high[upto], True)
        packed[group * BLOCK : (group + 1) * BLOCK, lo : lo + (i + 1) * BLOCK] = (
            both[:BLOCK] + both[BLOCK:] + dot(high[at], low[upto], True)
        )
    half = kept_ref.shape[0]
    for part in range(3):
        lanes = slice(part * third, (part + 1) * third)
        for t in range(packed.shape[0] // chunk):
            rows_at = pl.ds(pl.multiple_of((place_ref[2 + part] ^ t) * chunk, 8), chunk)
            at = t * chunk
            to_ref = kept_ref if at < half else sent_ref
            to_ref[at % half : at % half + chunk, lanes] = packed[rows_at, lanes]


def gram_of_columns(blocks, left_blocks, places, chi, chunk):
    rows, width = chi // 2, chi + BLOCK
    count, _, right = blocks[0].shape
    whole = pl.BlockSpec(memory_space=pltpu.VMEM)
    return pl.pallas_call(
        functools.partial(gram_kernel, chi, chunk, width // 3, len(blocks)),
        out_shape=[jax.ShapeDtypeStruct((rows // 2, width), jnp.float32)] * 2
        + [jax.ShapeDtypeStruct((chi, chi), jnp.bfloat16)],
        in_specs=[pl.BlockSpec(memory_space=pltpu.SMEM)] + [whole] * (len(blocks) + len(left_blocks)),
        out_specs=[whole, whole, whole],
        scratch_shapes=[pltpu.VMEM((chi, count * right), jnp.bfloat16)] * 3 + [pltpu.VMEM((rows, width), jnp.float32)],
        compiler_params=pltpu.CompilerParams(vmem_limit_bytes=40 * 2**20),
        cost_estimate=pl.CostEstimate(
            flops=5 * chi * chi * count * right, bytes_accessed=12 * chi * chi, transcendentals=0
        ),
    )(places, *blocks, *left_blocks)


def sub(x, s):
    return jnp.broadcast_to(x[s : s + 1, :], x.shape)


def lane(x, k):
    return jnp.broadcast_to(x[:, k : k + 1], x.shape)


def inverse_factor(block, tasks, spread):
    n, wide = BLOCK // 8, 8
    rows = [block[8 * b : 8 * b + 8] for b in range(n)]
    sub_id = lax.broadcasted_iota(jnp.int32, (8, BLOCK), 0)
    lane_id = lax.broadcasted_iota(jnp.int32, (8, BLOCK), 1)
    pivots = []
    head = [lane(rows[0], c) for c in range(wide)]
    for b in range(n):
        k = wide * b
        cols = [[head[c]] + [lane(rows[i], k + c) for i in range(b + 1, n)] for c in range(wide)]
        if b + 1 < n:
            head = [lane(rows[b + 1], k + wide + c) for c in range(wide)]
        inside = (lane_id >= k) & (lane_id < k + wide)
        for i in range(b, n):
            rows[i] = jnp.where(inside, 0.0, rows[i])
        pivot = jnp.ones((8, BLOCK), jnp.float32)
        near = min(2, n - b)
        multiples, scaled = {}, []
        for c in range(wide):
            d = sub(cols[c][0], c)
            inverse = 1.0 / d
            pivot = jnp.where(sub_id == c, d, pivot)
            for c2 in range(c + 1, wide):
                multiples[c2, c] = sub(cols[c][0], c2) * inverse
                for i in range(near):
                    cols[c2][i] = cols[c2][i] - cols[c][i] * multiples[c2, c]
            factors = [cols[c][i] * inverse for i in range(near)]
            if b + 1 < n:
                at = (b % 2 * wide + c) * 8
                spread[at : at + 8, :] = cols[c][1]
                for c2 in range(wide):
                    head[c2] = head[c2] - factors[1] * jnp.broadcast_to(spread[at + c2 : at + c2 + 1, :], (8, BLOCK))
            factors[0] = jnp.where(sub_id > c, factors[0], 0.0)
            row = jnp.where(lane_id == k + c, 1.0, sub(rows[b], c))
            scaled.append(row * inverse)
            for i in range(near):
                rows[b + i] = rows[b + i] - factors[i] * row
        if b + 2 < n:
            for c in range(wide - 1, 0, -1):
                for c2 in range(c):
                    scaled[c2] = scaled[c2] - multiples[c, c2] * scaled[c]
            for i in range(2, n - b):
                total = cols[0][i] * scaled[0]
                for c in range(1, wide):
                    total = total + cols[c][i] * scaled[c]
                rows[b + i] = rows[b + i] - total
        pivots.append(pivot)
        for task in tasks[len(tasks) * b // n : len(tasks) * (b + 1) // n]:
            task()
    out = []
    for b in range(n):
        diagonal = sub_id + 8 * b
        row = jnp.where(lane_id < diagonal, rows[b], jnp.where(lane_id == diagonal, 1.0, 0.0))
        out.append(row * lax.rsqrt(pivots[b]))
    return jnp.concatenate(out, 0)


def split(x, pieces):
    out = []
    for i in range(pieces):
        out.append(x.astype(jnp.bfloat16))
        if i + 1 < pieces:
            x = x - out[-1].astype(jnp.float32)
    return out


def product(a, b):
    rows = a[0].shape[0]
    both = dot(jnp.concatenate(a, 0), b[0])
    return both[:rows] + both[rows:] + dot(a[0], b[1])


def factor_kernel(scale, chunk, place_ref, mine_ref, other_ref, left, *refs):
    factor_ref, weights_ref, packed, gram, now, later, inverses, spread, solved, lows, low = refs
    chi = left.shape[0]
    n = chi // BLOCK
    half, third = mine_ref.shape[0], mine_ref.shape[1] // 3
    for part in range(3):
        lanes = slice(part * third, (part + 1) * third)
        for t in range(2 * half // chunk):
            at = pl.ds(pl.multiple_of((place_ref[2 + part] ^ t) * chunk, 8), chunk)
            from_ref = mine_ref if t * chunk < half else other_ref
            packed[at, lanes] = from_ref[t * chunk % half : t * chunk % half + chunk, lanes]
    for i in range(n):
        group, lo = (i, 0) if i < n // 2 else (n - 1 - i, (n - i) * BLOCK)
        for k in range(i + 1):
            block = packed[group * BLOCK : (group + 1) * BLOCK, lo + k * BLOCK : lo + (k + 1) * BLOCK]
            gram[i * BLOCK : (i + 1) * BLOCK, k * BLOCK : (k + 1) * BLOCK] = block
            if k < i:
                gram[k * BLOCK : (k + 1) * BLOCK, i * BLOCK : (i + 1) * BLOCK] = block.T

    wide = 2 * BLOCK
    every, top, bottom = slice(0, wide), slice(0, BLOCK), slice(BLOCK, wide)
    chunks = [slice(c, c + wide) for c in range(0, 2 * chi, wide)]
    earlier = slice(0, chi - 2 * wide)
    bind = functools.partial

    def span(first, size):
        return pl.ds(pl.multiple_of(first, BLOCK), size)

    def fresh(rows, columns):
        if columns.start < chi:
            return gram[rows, columns]
        return left[rows, columns.start - chi : columns.stop - chi].astype(jnp.float32)

    def solve(at, inverse, rows, columns, of_gram):
        values = product(inverse, split(now[rows, columns], PIECES))
        for i, piece in enumerate(split(values, PIECES)):
            solved[i, at, columns] = piece
        if of_gram:
            column = values.T
            low[columns, at] = column
            for i, piece in enumerate(split(column, PIECES)):
                lows[i, columns, at] = piece

    def taken(rows, before, columns):
        return product(
            [lows[i, rows, before] for i in range(PIECES)], [solved[i, before, columns] for i in range(PIECES)]
        )

    def less(to, at, source, rows, before, columns):
        to[at, columns] = source[at, columns] - taken(rows, before, columns)

    def fresh_less(rows, before, columns):
        later[:, columns] = fresh(rows, columns) - taken(rows, before, columns)

    def solve_all(at, inverse, rows):
        return [bind(solve, at, inverse, rows, columns, columns.start < chi) for columns in chunks]

    def less_all(*args):
        return [bind(less, *args, columns) for columns in chunks]

    for i in range(PIECES):
        solved[i, earlier] = jnp.zeros((chi - 2 * wide, 2 * chi), jnp.bfloat16)
        lows[i, :, earlier] = jnp.zeros((chi, chi - 2 * wide), jnp.bfloat16)
        inverses[i] = jnp.zeros_like(inverses[i])
    now[...] = jnp.zeros_like(now)
    for columns in chunks:
        later[:, columns] = fresh(every, columns)

    def next_block(inverse, row, block):
        values = product(inverse, split(row, PIECES))
        return block - product(split(values.T, PIECES), split(values, PIECES))

    def body(j, block):
        lo = j * wide
        last = span(lax.rem(lo + chi - BLOCK, chi), BLOCK)
        first, second, pair = span(lo, BLOCK), span(lo + BLOCK, BLOCK), span(lo, wide)
        following = jnp.minimum(lo + wide, chi - wide)
        next_pair, next_first = span(following, wide), span(following, BLOCK)

        inverse = [inverses[i] for i in range(PIECES)]
        tasks = solve_all(last, inverse, bottom) + less_all(now, every, later, pair, last)
        tasks += [bind(fresh_less, next_pair, earlier, columns) for columns in chunks]
        inverse = split(inverse_factor(block, tasks, spread), PIECES)
        block = next_block(inverse, now[top, second], now[bottom, second])

        tasks = solve_all(first, inverse, top) + less_all(now, bottom, now, second, first)
        tasks += less_all(later, every, later, next_pair, first)
        inverse = split(inverse_factor(block, tasks, spread), PIECES)
        for i, piece in enumerate(inverse):
            inverses[i] = piece
        return next_block(inverse, now[bottom, next_first], later[top, next_first])

    lax.fori_loop(0, chi // wide, body, gram[:BLOCK, :BLOCK])
    for task in solve_all(slice(chi - BLOCK, chi), [inverses[i] for i in range(PIECES)], bottom)[chi // wide - 1 :]:
        task()

    count = factor_ref.shape[0]
    first = place_ref[0] * count
    mine = pl.ds(pl.multiple_of(first, 16), count)
    row_id = lax.broadcasted_iota(jnp.int32, (count, chi), 0) + first
    column_id = lax.broadcasted_iota(jnp.int32, (count, chi), 1)
    factor_ref[...] = jnp.where(column_id <= row_id, low[mine, :] * (1.0 / scale), 0.0)
    weights_ref[...] = solved[0, mine, chi:]


def factorize(mine, other, left, places, rows, chunk, scale):
    chi = left.shape[0]
    whole = pl.BlockSpec(memory_space=pltpu.VMEM)
    return pl.pallas_call(
        functools.partial(factor_kernel, scale, chunk),
        out_shape=[
            jax.ShapeDtypeStruct((rows, chi), jnp.float32),
            jax.ShapeDtypeStruct((rows, chi), jnp.bfloat16),
        ],
        in_specs=[pl.BlockSpec(memory_space=pltpu.SMEM)] + [whole] * 3,
        out_specs=[whole, whole],
        scratch_shapes=[
            pltpu.VMEM((chi // 2, chi + BLOCK), jnp.float32),
            pltpu.VMEM((chi, chi), jnp.float32),
            pltpu.VMEM((2 * BLOCK, 2 * chi), jnp.float32),
            pltpu.VMEM((2 * BLOCK, 2 * chi), jnp.float32),
            pltpu.VMEM((PIECES, BLOCK, BLOCK), jnp.bfloat16),
            pltpu.VMEM((BLOCK, BLOCK), jnp.float32),
            pltpu.VMEM((PIECES, chi, 2 * chi), jnp.bfloat16),
            pltpu.VMEM((PIECES, chi, chi), jnp.bfloat16),
            pltpu.VMEM((chi, chi), jnp.float32),
        ],
        compiler_params=pltpu.CompilerParams(vmem_limit_bytes=40 * 2**20),
        cost_estimate=pl.CostEstimate(flops=20 * 2 * chi**3, bytes_accessed=16 * chi**2, transcendentals=0),
    )(places, mine, other, left)


def site_kernel(scale, place_ref, weights_ref, own_ref, first_ref, second_ref, *refs):
    out_ref = refs[-1]
    depth = own_ref.shape[1]
    mine = weights_ref[:, pl.ds(pl.multiple_of(place_ref[1] * depth, depth), depth)]
    other = weights_ref[:, pl.ds(pl.multiple_of((place_ref[1] ^ 1) * depth, depth), depth)]
    got = jnp.where(pl.program_id(0) == 0, first_ref[0], second_ref[0]).astype(jnp.bfloat16)
    out_ref[0] = scale * (dot(mine, own_ref[0]) + dot(other, got))


def make_site(weights, own, slots, got, places, scale, before):
    rows, chi = weights.shape
    east, depth, right = own.shape
    count = got[0].shape[0]
    first, second = slots

    def leg(s, i, place_ref):
        return ((place_ref[0] ^ (first + s * (second - first))) * count + i, 0, 0)

    piece = pl.BlockSpec((1, depth, right), lambda s, i, place_ref: (i, 0, 0))
    return pl.pallas_call(
        functools.partial(site_kernel, scale),
        out_shape=jax.ShapeDtypeStruct((east, rows, right), jnp.float32),
        grid_spec=pltpu.PrefetchScalarGridSpec(
            num_scalar_prefetch=1,
            grid=(2, count),
            in_specs=[
                pl.BlockSpec((rows, chi), lambda s, i, place_ref: (0, 0)),
                pl.BlockSpec((1, depth, right), leg),
                piece,
                piece,
            ]
            + [pl.BlockSpec(memory_space=pl.ANY)] * len(before),
            out_specs=pl.BlockSpec((1, rows, right), leg),
        ),
        input_output_aliases={5: 0} if before else {},
        compiler_params=pltpu.CompilerParams(vmem_limit_bytes=24 * 2**20),
        cost_estimate=pl.CostEstimate(
            flops=rows * chi * east * right, bytes_accessed=4 * east * chi * right, transcendentals=0
        ),
    )(places, weights, own, *got, *before)


def shards(sizes, left_factor, boundary_site, double_layer):
    lb, rb, rep = sizes["lb"], sizes["rb"], sizes["rep"]
    l, p = lax.axis_index("lb"), lax.axis_index("rep")
    depth, phys, right = boundary_site.shape
    east = phys // rep
    chi = depth * rep
    row_count = left_factor.shape[0]
    scale = math.sqrt(phys * rb * right)
    steps = {axis: steps_of(axis, size) for axis, size in sizes.items()}
    core, across = steps["lb"][:1], steps["lb"][1:]

    left_blocks = gather_slots([(0, left_factor.astype(jnp.float32))], steps["rep"])
    left_blocks = [piece for _, piece in sorted(left_blocks, key=lambda pair: pair[0])]
    left_blocks = [gather_slots([(0, piece)], across[::-1] + core) for piece in left_blocks]
    left_blocks = [sorted(pieces, key=lambda pair: pair[0]) for pieces in left_blocks]
    left_blocks = [left_blocks[q][s][1] for s in range(lb) for q in range(rep)]

    east_part, right_parts = max(1, east // lb), max(1, lb // east)
    right_part = right // right_parts
    east_at, right_at = (l // right_parts) * east_part, (l % right_parts) * right_part
    legs = [(p ^ s) * east + east_at + i for s in range(1, rep) for i in range(east_part)]
    sent = absorb(boundary_site, double_layer, legs, [east_part] * (rep - 1), jnp.float32)
    if right_parts > 1:
        sent = [lax.dynamic_slice_in_dim(piece, right_at, right_part, 2) for piece in sent]
    got = [swap(piece, ("rep", rep, s)) for s, piece in zip(range(1, rep), sent)]
    (own,) = absorb(boundary_site, double_layer, [p * east + i for i in range(east)], [east], jnp.bfloat16)
    share = lax.dynamic_slice(own, (east_at, 0, right_at), (east_part, depth, right_part))
    got, left_blocks = lax.optimization_barrier((got, left_blocks))

    near = across[:1] + steps["rep"][:1] + steps["rb"][:1]
    far = [step for step in across + steps["rep"] + steps["rb"] if step not in near]
    orders = [near[i:] + near[:i] for i in range(3)]
    cut = cut_steps(near, chi // 4)
    chunk = (chi // 4) >> cut
    bits = [position(core + order[:cut]) for order in orders]
    places = jnp.stack([l, p] + bits).astype(jnp.int32)
    kept, sent, left = gram_of_columns([share] + got, left_blocks, places, chi, chunk)
    whole = kept + swap(sent, core[0])
    third = whole.shape[1] // 3
    parts = [whole[:, i * third : (i + 1) * third] for i in range(3)]
    parts = reduce_parts(parts, orders, cut)
    whole = jnp.concatenate(parts, 1)
    pairs = [[piece, swap(piece, core[0])] for piece in got]
    whole, pairs = lax.optimization_barrier((whole, pairs))
    for step in far:
        whole = whole + swap(whole, step)
    parts = [whole[:, i * third : (i + 1) * third] for i in range(3)]
    parts = gather_parts(parts, orders, cut)
    whole = jnp.concatenate(parts, 1)
    other = swap(whole, core[0])
    pairs, whole = lax.optimization_barrier((pairs, whole))
    halved = rep == 2 and right_parts == 1 and len(across) == 1
    if halved:
        crossed = swap(pairs[0][0], across[0])

    factor, weights = factorize(whole, other, left, places, row_count, chunk, scale)
    if halved:
        crossed, weights = lax.optimization_barrier((crossed, weights))
        pair = [crossed, swap(crossed, core[0])]
        site_q = make_site(weights, own, (0, 1), pairs[0], places, scale, [])
        site_q = make_site(weights, own, (2, 3), pair, places, scale, [site_q])
    else:
        got = [gather_slots(list(zip(range(2), pair)), across[::-1]) for pair in pairs]
        nothing = double_layer[0, 0] * 0.0
        site = jnp.zeros((east, chi, right), jnp.bfloat16)
        site = lax.dynamic_update_slice(site, own, (0, p * depth, 0))
        for s, pieces in zip(range(1, rep), got):
            for slot, piece in pieces:
                owner = l ^ slot
                at = ((owner // right_parts) * east_part, (p ^ s) * depth, (owner % right_parts) * right_part)
                site = lax.dynamic_update_slice(site, (piece + nothing).astype(jnp.bfloat16), at)
        site_q = jnp.einsum("ik,ekr->eir", weights, site, preferred_element_type=jnp.float32) * scale
    return (site_q, factor)


def solution(mesh):
    return jax.shard_map(
        functools.partial(shards, dict(mesh.shape)),
        mesh=mesh,
        in_specs=(P("lb", "rep"), P("rep", None, "rb"), P()),
        out_specs=(P("rep", "lb", "rb"), P("lb", None)),
        check_vma=False,
    )
```

```python
import functools
import math

import jax
import jax.numpy as jnp
from jax import lax
from jax.experimental import pallas as pl
from jax.experimental.pallas import tpu as pltpu
from jax.sharding import PartitionSpec as P

BLOCK = 128


def swap(array, step):
    axis, size, distance = step
    return lax.ppermute(array, axis, [(i, i ^ distance) for i in range(size)])


def steps_of(axis, size):
    return [(axis, size, 1 << i) for i in range(size.bit_length() - 1)]


def gather_slots(held, steps):
    for step in steps:
        held = held + [(slot ^ step[2], swap(piece, step)) for slot, piece in held]
    return held


def cut_steps(steps, rows):
    count = 0
    while count < len(steps) and rows % 16 == 0:
        rows, count = rows // 2, count + 1
    return count


def position(steps):
    place = jnp.int32(0)
    for axis, _, distance in steps:
        place = place * 2 + lax.rem(lax.div(lax.axis_index(axis), distance), 2)
    return place


def swap_parts(parts, steps):
    parts = lax.optimization_barrier(parts)
    return lax.optimization_barrier([swap(part, step) for part, step in zip(parts, steps)])


def reduce_parts(parts, orders, cuts):
    for at in range(cuts):
        half = parts[0].shape[0] // 2
        got = swap_parts([part[half:] for part in parts], [order[at] for order in orders])
        parts = [part[:half] + other for part, other in zip(parts, got)]
    return parts


def gather_parts(parts, orders, cuts):
    for at in range(cuts - 1, -1, -1):
        got = swap_parts(parts, [order[at] for order in orders])
        parts = [jnp.concatenate([part, other], 0) for part, other in zip(parts, got)]
    return parts


HIGHEST = lax.Precision.HIGHEST
GROUP = 16
PIECES = 2


def dot(a, b, transposed=False):
    dims = (((1,), (1 if transposed else 0,)), ((), ()))
    return lax.dot_general(a, b, dims, preferred_element_type=jnp.float32)


def absorb_kernel(east_parts, legs_ref, site_ref, double_ref, *out_refs):
    phys = double_ref.shape[0]
    legs = sum(east_parts)
    row = lax.broadcasted_iota(jnp.int32, (legs * GROUP, GROUP * phys), 0)
    column = lax.broadcasted_iota(jnp.int32, (legs * GROUP, GROUP * phys), 1)
    chosen = jnp.concatenate(
        [
            jnp.where(lax.broadcasted_iota(jnp.int32, (GROUP, phys), 1) == legs_ref[i], 1.0, 0.0)
            for i in range(legs)
        ],
        0,
    )
    values = lax.dot_general(
        chosen, double_ref[...], (((1,), (1,)), ((), ())), precision=HIGHEST, preferred_element_type=jnp.float32
    )
    spread = jnp.where(
        lax.broadcasted_iota(jnp.int32, (phys, GROUP * phys), 0)
        == lax.rem(lax.broadcasted_iota(jnp.int32, (phys, GROUP * phys), 1), phys),
        1.0,
        0.0,
    )
    values = jnp.dot(values, spread, precision=HIGHEST, preferred_element_type=jnp.float32)
    both = jnp.concatenate(split(jnp.where(lax.rem(row, GROUP) == lax.div(column, phys), values, 0.0), 2), 0)
    groups = site_ref.shape[0] // (GROUP * phys)
    for g in range(groups):
        rows = site_ref[g * GROUP * phys : (g + 1) * GROUP * phys, :]
        absorbed = dot(both, rows)
        absorbed = (absorbed[: legs * GROUP] + absorbed[legs * GROUP :]).astype(jnp.bfloat16)
        leg = 0
        for out_ref, count in zip(out_refs, east_parts):
            for e in range(count):
                piece = absorbed[(leg + e) * GROUP : (leg + e + 1) * GROUP]
                out_ref[e, g * GROUP : (g + 1) * GROUP, :] = piece.astype(out_ref.dtype)
            leg += count


def absorb(boundary_site, double_layer, legs, east_parts, dtype):
    legs = jnp.stack(legs).astype(jnp.int32)
    depth, phys, right = boundary_site.shape
    tiles = max(1, depth // 128)
    tile = depth // tiles
    out_shape, out_specs = [], []
    for count in east_parts:
        out_shape.append(jax.ShapeDtypeStruct((count, depth, right), dtype))
        out_specs.append(pl.BlockSpec((count, tile, right), lambda t: (0, t, 0)))
    return pl.pallas_call(
        functools.partial(absorb_kernel, east_parts),
        grid=(tiles,),
        out_shape=out_shape,
        in_specs=[
            pl.BlockSpec(memory_space=pltpu.SMEM),
            pl.BlockSpec((tile * phys, right), lambda t: (t, 0)),
            pl.BlockSpec(memory_space=pltpu.VMEM),
        ],
        out_specs=out_specs,
        compiler_params=pltpu.CompilerParams(vmem_limit_bytes=32 * 2**20),
        cost_estimate=pl.CostEstimate(
            flops=2 * 2 * depth * right * GROUP * phys * sum(east_parts), bytes_accessed=8 * depth * right * phys, transcendentals=0
        ),
    )(legs, boundary_site.reshape(depth * phys, right), double_layer)


def gram_kernel(chi, chunk, third, blocks, place_ref, *refs):
    block_refs, left_refs = refs[:blocks], refs[blocks:-7]
    kept_ref, sent_ref, left, columns, high, low, packed = refs[-7:]
    rows, width = left_refs[0].shape
    across = chi // width
    for i, left_ref in enumerate(left_refs):
        row_at = pl.multiple_of((place_ref[0] ^ (i // across)) * rows, 16)
        column_at = pl.multiple_of((place_ref[1] ^ (i % across)) * width, 128)
        left[pl.ds(row_at, rows), pl.ds(column_at, width)] = left_ref[...].astype(jnp.bfloat16)
    count, depth, width = block_refs[0].shape
    n = chi // BLOCK
    for i, block_ref in enumerate(block_refs):
        at = pl.ds(pl.multiple_of((place_ref[1] ^ i) * depth, depth), depth)
        for e in range(count):
            columns[at, e * width : (e + 1) * width] = block_ref[e].astype(jnp.bfloat16)
    for i in range(n // 2):
        at = slice(2 * i * BLOCK, 2 * (i + 1) * BLOCK)
        high[at], low[at] = split(dot(left[at], columns[...]), 2)
    for i in range(n):
        group, lo = (i, 0) if i < n // 2 else (n - 1 - i, (n - i) * BLOCK)
        at, upto = slice(i * BLOCK, (i + 1) * BLOCK), slice(0, (i + 1) * BLOCK)
        both = dot(jnp.concatenate([high[at], low[at]], 0), high[upto], True)
        packed[group * BLOCK : (group + 1) * BLOCK, lo : lo + (i + 1) * BLOCK] = (
            both[:BLOCK] + both[BLOCK:] + dot(high[at], low[upto], True)
        )
    half = kept_ref.shape[0]
    for part in range(3):
        lanes = slice(part * third, (part + 1) * third)
        for t in range(packed.shape[0] // chunk):
            rows_at = pl.ds(pl.multiple_of((place_ref[2 + part] ^ t) * chunk, 8), chunk)
            at = t * chunk
            to_ref = kept_ref if at < half else sent_ref
            to_ref[at % half : at % half + chunk, lanes] = packed[rows_at, lanes]


def gram_of_columns(blocks, left_blocks, places, chi, chunk):
    rows, width = chi // 2, chi + BLOCK
    count, _, right = blocks[0].shape
    whole = pl.BlockSpec(memory_space=pltpu.VMEM)
    return pl.pallas_call(
        functools.partial(gram_kernel, chi, chunk, width // 3, len(blocks)),
        out_shape=[jax.ShapeDtypeStruct((rows // 2, width), jnp.float32)] * 2
        + [jax.ShapeDtypeStruct((chi, chi), jnp.bfloat16)],
        in_specs=[pl.BlockSpec(memory_space=pltpu.SMEM)] + [whole] * (len(blocks) + len(left_blocks)),
        out_specs=[whole, whole, whole],
        scratch_shapes=[pltpu.VMEM((chi, count * right), jnp.bfloat16)] * 3 + [pltpu.VMEM((rows, width), jnp.float32)],
        compiler_params=pltpu.CompilerParams(vmem_limit_bytes=26 * 2**20),
        cost_estimate=pl.CostEstimate(
            flops=5 * chi * chi * count * right, bytes_accessed=12 * chi * chi, transcendentals=0
        ),
    )(places, *blocks, *left_blocks)


def sub(x, s):
    return jnp.broadcast_to(x[s : s + 1, :], x.shape)


def lane(x, k):
    return jnp.broadcast_to(x[:, k : k + 1], x.shape)


def inverse_factor(block, tasks, spread):
    n, wide = BLOCK // 8, 8
    rows = [block[8 * b : 8 * b + 8] for b in range(n)]
    sub_id = lax.broadcasted_iota(jnp.int32, (8, BLOCK), 0)
    lane_id = lax.broadcasted_iota(jnp.int32, (8, BLOCK), 1)
    pivots = []
    head = [lane(rows[0], c) for c in range(wide)]
    for b in range(n):
        k = wide * b
        cols = [[head[c]] + [lane(rows[i], k + c) for i in range(b + 1, n)] for c in range(wide)]
        if b + 1 < n:
            head = [lane(rows[b + 1], k + wide + c) for c in range(wide)]
        inside = (lane_id >= k) & (lane_id < k + wide)
        for i in range(b, n):
            rows[i] = jnp.where(inside, 0.0, rows[i])
        pivot = jnp.ones((8, BLOCK), jnp.float32)
        near = min(2, n - b)
        multiples, scaled = {}, []
        for c in range(wide):
            d = sub(cols[c][0], c)
            inverse = 1.0 / d
            pivot = jnp.where(sub_id == c, d, pivot)
            for c2 in range(c + 1, wide):
                multiples[c2, c] = sub(cols[c][0], c2) * inverse
                for i in range(near):
                    cols[c2][i] = cols[c2][i] - cols[c][i] * multiples[c2, c]
            factors = [cols[c][i] * inverse for i in range(near)]
            if b + 1 < n:
                at = (b % 2 * wide + c) * 8
                spread[at : at + 8, :] = cols[c][1]
                for c2 in range(wide):
                    head[c2] = head[c2] - factors[1] * jnp.broadcast_to(spread[at + c2 : at + c2 + 1, :], (8, BLOCK))
            factors[0] = jnp.where(sub_id > c, factors[0], 0.0)
            row = jnp.where(lane_id == k + c, 1.0, sub(rows[b], c))
            scaled.append(row * inverse)
            for i in range(near):
                rows[b + i] = rows[b + i] - factors[i] * row
        if b + 2 < n:
            for c in range(wide - 1, 0, -1):
                for c2 in range(c):
                    scaled[c2] = scaled[c2] - multiples[c, c2] * scaled[c]
            for i in range(2, n - b):
                total = cols[0][i] * scaled[0]
                for c in range(1, wide):
                    total = total + cols[c][i] * scaled[c]
                rows[b + i] = rows[b + i] - total
        pivots.append(pivot)
        for task in tasks[len(tasks) * b // n : len(tasks) * (b + 1) // n]:
            task()
    out = []
    for b in range(n):
        diagonal = sub_id + 8 * b
        row = jnp.where(lane_id < diagonal, rows[b], jnp.where(lane_id == diagonal, 1.0, 0.0))
        out.append(row * lax.rsqrt(pivots[b]))
    return jnp.concatenate(out, 0)


def split(x, pieces):
    out = []
    for i in range(pieces):
        out.append(x.astype(jnp.bfloat16))
        if i + 1 < pieces:
            x = x - out[-1].astype(jnp.float32)
    return out


def product(a, b):
    rows = a[0].shape[0]
    both = dot(jnp.concatenate(a, 0), b[0])
    return both[:rows] + both[rows:] + dot(a[0], b[1])


def factor_kernel(scale, chunk, place_ref, mine_ref, other_ref, left, *refs):
    factor_ref, weights_ref, packed, gram, now, later, inverses, spread, solved, lows, low = refs
    chi = left.shape[0]
    n = chi // BLOCK
    half, third = mine_ref.shape[0], mine_ref.shape[1] // 3
    for part in range(3):
        lanes = slice(part * third, (part + 1) * third)
        for t in range(2 * half // chunk):
            at = pl.ds(pl.multiple_of((place_ref[2 + part] ^ t) * chunk, 8), chunk)
            from_ref = mine_ref if t * chunk < half else other_ref
            packed[at, lanes] = from_ref[t * chunk % half : t * chunk % half + chunk, lanes]
    for i in range(n):
        group, lo = (i, 0) if i < n // 2 else (n - 1 - i, (n - i) * BLOCK)
        for k in range(i + 1):
            block = packed[group * BLOCK : (group + 1) * BLOCK, lo + k * BLOCK : lo + (k + 1) * BLOCK]
            gram[i * BLOCK : (i + 1) * BLOCK, k * BLOCK : (k + 1) * BLOCK] = block
            if k < i:
                gram[k * BLOCK : (k + 1) * BLOCK, i * BLOCK : (i + 1) * BLOCK] = block.T

    wide = 2 * BLOCK
    every, top, bottom = slice(0, wide), slice(0, BLOCK), slice(BLOCK, wide)
    chunks = [slice(c, c + wide) for c in range(0, 2 * chi, wide)]
    earlier = slice(0, chi - 2 * wide)
    bind = functools.partial

    def span(first, size):
        return pl.ds(pl.multiple_of(first, BLOCK), size)

    def fresh(rows, columns):
        if columns.start < chi:
            return gram[rows, columns]
        return left[rows, columns.start - chi : columns.stop - chi].astype(jnp.float32)

    def solve(at, inverse, rows, columns, of_gram):
        values = product(inverse, split(now[rows, columns], PIECES))
        for i, piece in enumerate(split(values, PIECES)):
            solved[i, at, columns] = piece
        if of_gram:
            column = values.T
            low[columns, at] = column
            for i, piece in enumerate(split(column, PIECES)):
                lows[i, columns, at] = piece

    def taken(rows, before, columns):
        return product(
            [lows[i, rows, before] for i in range(PIECES)], [solved[i, before, columns] for i in range(PIECES)]
        )

    def less(to, at, source, rows, before, columns):
        to[at, columns] = source[at, columns] - taken(rows, before, columns)

    def fresh_less(rows, before, columns):
        later[:, columns] = fresh(rows, columns) - taken(rows, before, columns)

    def solve_all(at, inverse, rows):
        return [bind(solve, at, inverse, rows, columns, columns.start < chi) for columns in chunks]

    def less_all(*args):
        return [bind(less, *args, columns) for columns in chunks]

    for i in range(PIECES):
        solved[i, earlier] = jnp.zeros((chi - 2 * wide, 2 * chi), jnp.bfloat16)
        lows[i, :, earlier] = jnp.zeros((chi, chi - 2 * wide), jnp.bfloat16)
        inverses[i] = jnp.zeros_like(inverses[i])
    now[...] = jnp.zeros_like(now)
    for columns in chunks:
        later[:, columns] = fresh(every, columns)

    def next_block(inverse, row, block):
        values = product(inverse, split(row, PIECES))
        return block - product(split(values.T, PIECES), split(values, PIECES))

    def body(j, block):
        lo = j * wide
        last = span(lax.rem(lo + chi - BLOCK, chi), BLOCK)
        first, second, pair = span(lo, BLOCK), span(lo + BLOCK, BLOCK), span(lo, wide)
        following = jnp.minimum(lo + wide, chi - wide)
        next_pair, next_first = span(following, wide), span(following, BLOCK)

        inverse = [inverses[i] for i in range(PIECES)]
        tasks = solve_all(last, inverse, bottom) + less_all(now, every, later, pair, last)
        tasks += [bind(fresh_less, next_pair, earlier, columns) for columns in chunks]
        inverse = split(inverse_factor(block, tasks, spread), PIECES)
        block = next_block(inverse, now[top, second], now[bottom, second])

        tasks = solve_all(first, inverse, top) + less_all(now, bottom, now, second, first)
        tasks += less_all(later, every, later, next_pair, first)
        inverse = split(inverse_factor(block, tasks, spread), PIECES)
        for i, piece in enumerate(inverse):
            inverses[i] = piece
        return next_block(inverse, now[bottom, next_first], later[top, next_first])

    lax.fori_loop(0, chi // wide, body, gram[:BLOCK, :BLOCK])
    for task in solve_all(slice(chi - BLOCK, chi), [inverses[i] for i in range(PIECES)], bottom)[chi // wide - 1 :]:
        task()

    count = factor_ref.shape[0]
    first = place_ref[0] * count
    mine = pl.ds(pl.multiple_of(first, 16), count)
    row_id = lax.broadcasted_iota(jnp.int32, (count, chi), 0) + first
    column_id = lax.broadcasted_iota(jnp.int32, (count, chi), 1)
    factor_ref[...] = jnp.where(column_id <= row_id, low[mine, :] * (1.0 / scale), 0.0)
    weights_ref[...] = solved[0, mine, chi:]


def factorize(mine, other, left, places, rows, chunk, scale):
    chi = left.shape[0]
    whole = pl.BlockSpec(memory_space=pltpu.VMEM)
    return pl.pallas_call(
        functools.partial(factor_kernel, scale, chunk),
        out_shape=[
            jax.ShapeDtypeStruct((rows, chi), jnp.float32),
            jax.ShapeDtypeStruct((rows, chi), jnp.bfloat16),
        ],
        in_specs=[pl.BlockSpec(memory_space=pltpu.SMEM)] + [whole] * 3,
        out_specs=[whole, whole],
        scratch_shapes=[
            pltpu.VMEM((chi // 2, chi + BLOCK), jnp.float32),
            pltpu.VMEM((chi, chi), jnp.float32),
            pltpu.VMEM((2 * BLOCK, 2 * chi), jnp.float32),
            pltpu.VMEM((2 * BLOCK, 2 * chi), jnp.float32),
            pltpu.VMEM((PIECES, BLOCK, BLOCK), jnp.bfloat16),
            pltpu.VMEM((BLOCK, BLOCK), jnp.float32),
            pltpu.VMEM((PIECES, chi, 2 * chi), jnp.bfloat16),
            pltpu.VMEM((PIECES, chi, chi), jnp.bfloat16),
            pltpu.VMEM((chi, chi), jnp.float32),
        ],
        compiler_params=pltpu.CompilerParams(vmem_limit_bytes=40 * 2**20),
        cost_estimate=pl.CostEstimate(flops=20 * 2 * chi**3, bytes_accessed=16 * chi**2, transcendentals=0),
    )(places, mine, other, left)


def site_kernel(scale, place_ref, weights_ref, own_ref, first_ref, second_ref, *refs):
    out_ref = refs[-1]
    depth = own_ref.shape[1]
    mine = weights_ref[:, pl.ds(pl.multiple_of(place_ref[1] * depth, depth), depth)]
    other = weights_ref[:, pl.ds(pl.multiple_of((place_ref[1] ^ 1) * depth, depth), depth)]
    got = jnp.where(pl.program_id(0) == 0, first_ref[0], second_ref[0]).astype(jnp.bfloat16)
    out_ref[0] = scale * (dot(mine, own_ref[0]) + dot(other, got))


def make_site(weights, own, slots, got, places, scale, before):
    rows, chi = weights.shape
    east, depth, right = own.shape
    count = got[0].shape[0]
    first, second = slots

    def leg(s, i, place_ref):
        return ((place_ref[0] ^ (first + s * (second - first))) * count + i, 0, 0)

    piece = pl.BlockSpec((1, depth, right), lambda s, i, place_ref: (i, 0, 0))
    return pl.pallas_call(
        functools.partial(site_kernel, scale),
        out_shape=jax.ShapeDtypeStruct((east, rows, right), jnp.float32),
        grid_spec=pltpu.PrefetchScalarGridSpec(
            num_scalar_prefetch=1,
            grid=(2, count),
            in_specs=[
                pl.BlockSpec((rows, chi), lambda s, i, place_ref: (0, 0)),
                pl.BlockSpec((1, depth, right), leg),
                piece,
                piece,
            ]
            + [pl.BlockSpec(memory_space=pl.ANY)] * len(before),
            out_specs=pl.BlockSpec((1, rows, right), leg),
        ),
        input_output_aliases={5: 0} if before else {},
        compiler_params=pltpu.CompilerParams(vmem_limit_bytes=24 * 2**20),
        cost_estimate=pl.CostEstimate(
            flops=rows * chi * east * right, bytes_accessed=4 * east * chi * right, transcendentals=0
        ),
    )(places, weights, own, *got, *before)


def shards(sizes, left_factor, boundary_site, double_layer):
    lb, rb, rep = sizes["lb"], sizes["rb"], sizes["rep"]
    l, p = lax.axis_index("lb"), lax.axis_index("rep")
    depth, phys, right = boundary_site.shape
    east = phys // rep
    chi = depth * rep
    row_count = left_factor.shape[0]
    scale = math.sqrt(phys * rb * right)
    steps = {axis: steps_of(axis, size) for axis, size in sizes.items()}
    core, across = steps["lb"][:1], steps["lb"][1:]

    left_blocks = gather_slots([(0, left_factor.astype(jnp.float32))], steps["rep"])
    left_blocks = [piece for _, piece in sorted(left_blocks, key=lambda pair: pair[0])]
    left_blocks = [gather_slots([(0, piece)], across[::-1] + core) for piece in left_blocks]
    left_blocks = [sorted(pieces, key=lambda pair: pair[0]) for pieces in left_blocks]
    left_blocks = [left_blocks[q][s][1] for s in range(lb) for q in range(rep)]

    east_part, right_parts = max(1, east // lb), max(1, lb // east)
    right_part = right // right_parts
    east_at, right_at = (l // right_parts) * east_part, (l % right_parts) * right_part
    legs = [(p ^ s) * east + east_at + i for s in range(1, rep) for i in range(east_part)]
    sent = absorb(boundary_site, double_layer, legs, [east_part] * (rep - 1), jnp.float32)
    if right_parts > 1:
        sent = [lax.dynamic_slice_in_dim(piece, right_at, right_part, 2) for piece in sent]
    got = [swap(piece, ("rep", rep, s)) for s, piece in zip(range(1, rep), sent)]
    (own,) = absorb(boundary_site, double_layer, [p * east + i for i in range(east)], [east], jnp.bfloat16)
    share = lax.dynamic_slice(own, (east_at, 0, right_at), (east_part, depth, right_part))
    got, left_blocks = lax.optimization_barrier((got, left_blocks))

    near = across[:1] + steps["rep"][:1] + steps["rb"][:1]
    far = [step for step in across + steps["rep"] + steps["rb"] if step not in near]
    orders = [near[i:] + near[:i] for i in range(3)]
    cut = cut_steps(near, chi // 4)
    chunk = (chi // 4) >> cut
    bits = [position(core + order[:cut]) for order in orders]
    places = jnp.stack([l, p] + bits).astype(jnp.int32)
    kept, sent, left = gram_of_columns([share] + got, left_blocks, places, chi, chunk)
    whole = kept + swap(sent, core[0])
    third = whole.shape[1] // 3
    parts = [whole[:, i * third : (i + 1) * third] for i in range(3)]
    parts = reduce_parts(parts, orders, cut)
    whole = jnp.concatenate(parts, 1)
    pairs = [[piece, swap(piece, core[0])] for piece in got]
    whole, pairs = lax.optimization_barrier((whole, pairs))
    for step in far:
        whole = whole + swap(whole, step)
    parts = [whole[:, i * third : (i + 1) * third] for i in range(3)]
    parts = gather_parts(parts, orders, cut)
    whole = jnp.concatenate(parts, 1)
    other = swap(whole, core[0])
    pairs, whole = lax.optimization_barrier((pairs, whole))
    halved = rep == 2 and right_parts == 1 and len(across) == 1
    if halved:
        crossed = swap(pairs[0][0], across[0])

    factor, weights = factorize(whole, other, left, places, row_count, chunk, scale)
    if halved:
        crossed, weights = lax.optimization_barrier((crossed, weights))
        pair = [crossed, swap(crossed, core[0])]
        site_q = make_site(weights, own, (0, 1), pairs[0], places, scale, [])
        site_q = make_site(weights, own, (2, 3), pair, places, scale, [site_q])
    else:
        got = [gather_slots(list(zip(range(2), pair)), across[::-1]) for pair in pairs]
        nothing = double_layer[0, 0] * 0.0
        site = jnp.zeros((east, chi, right), jnp.bfloat16)
        site = lax.dynamic_update_slice(site, own, (0, p * depth, 0))
        for s, pieces in zip(range(1, rep), got):
            for slot, piece in pieces:
                owner = l ^ slot
                at = ((owner // right_parts) * east_part, (p ^ s) * depth, (owner % right_parts) * right_part)
                site = lax.dynamic_update_slice(site, (piece + nothing).astype(jnp.bfloat16), at)
        site_q = jnp.einsum("ik,ekr->eir", weights, site, preferred_element_type=jnp.float32) * scale
    return (site_q, factor)


def solution(mesh):
    return jax.shard_map(
        functools.partial(shards, dict(mesh.shape)),
        mesh=mesh,
        in_specs=(P("lb", "rep"), P("rep", None, "rb"), P()),
        out_specs=(P("rep", "lb", "rb"), P("lb", None)),
        check_vma=False,
    )
```
